32 devices in a mesh: groups: 2 (over x), pairs: 8 (over z, y), aux: 2 (over core).
Axes of the slice: x: 2, y: 2, z: 4, core: 2. Of those that a mesh axis runs over, the one named last changes fastest.
Arguments:
- blocks: bfloat16 [256, 32, 10240], P(('groups', 'pairs'), None, 'aux'), parts along dimension 0, may hold values from -0.75 to 0.75
- wanted: int32 [256], P(('groups', 'pairs')), parts along dimension 0, may hold values from 0 to 127, as said below
- pair_slots: int32 [256, 16], P(('groups', 'pairs')), parts along dimension 0, may hold values from 0 to 15
- fock: bfloat16 [256, 256, 256], P(('groups', 'pairs', 'aux')), parts along dimension 0, may hold values from -0.375 to 0.375
- correlation: bfloat16 [256, 256, 256], P(('groups', 'pairs', 'aux')), parts along dimension 0, may hold values from -0.375 to 0.375
- amplitudes: bfloat16 [256, 256, 256], P(('groups', 'pairs', 'aux')), parts along dimension 0, may hold values from -6 to 6
Outputs:
- pair_residual: bfloat16 [256, 256, 256], P(('groups', 'pairs', 'aux')), parts along dimension 0
The draws below stay inside these ranges and needn't reach their ends.
There are 2 independent parts, one for each index of `groups`. The reference program is written for one: setup_inputs(seed, part) draws one part's arguments, and reference() takes and returns one part's arrays. A program takes and returns all parts, laid end to end along the dimension named above; each array names one. Nothing has to cross between parts.
Inputs may be any that keep to these rules, and one draw needn't show every extreme that they name: `wanted`: block b is held by orbital owner b // 16 along pairs. Among the 16 entries of one pair owner at most 4 name blocks of the same orbital owner, and on every pair owner some orbital owner is named exactly 4 times.
All inputs are finite; a program needn't handle non-finite values.
Results may differ from the reference program's by a relative error of at most 0.012.
Values may be sent and summed in bfloat16 or wider, within the bound.
No kernel may reach another device: no remote copies, remote signals or barrier semaphores. Data moves between devices by JAX's collectives and lax.ppermute only.
A program may use at most 128 MiB of HBM per device.

```python
import jax
import jax.numpy as jnp
from jax import lax

BLKW = 32
DOM = 8
UNIQ = 16
BLK_DEV = 16
PAIR_DEV = 16
CAP = 4
NAUX = 10240
DOMW = 256
NBLOCKS = 128
PAIRS = 128
WANTED = 128


def draw_wanted(key, part):
    key = jax.random.fold_in(key, 7)
    devices = WANTED // UNIQ
    device_keys = jax.random.split(key, devices)

    def one_device(subkey):
        first, second, third, fourth = jax.random.split(subkey, 4)
        order = jax.random.permutation(first, devices)
        counts = jax.random.randint(second, (devices,), CAP // 2, CAP + 1)
        counts = counts.at[0].set(CAP)
        ends = jnp.cumsum(counts)
        position = jnp.arange(UNIQ)
        which = jnp.sum((position[:, None] >= ends[None, :]).astype(jnp.int32), axis=1)
        holder = order[which]
        holder = holder[jax.random.permutation(fourth, UNIQ)]
        local_ids = jax.random.randint(third, (UNIQ,), 0, BLK_DEV)
        return (holder * BLK_DEV + local_ids).astype(jnp.int32)
    return jax.vmap(one_device)(device_keys).reshape(-1)


def with_ends(entries, stream_key, low, top_value):
    extent = entries.shape
    place = [jax.random.randint(jax.random.fold_in(stream_key, axis), (), 0, extent[axis]) for axis in range(len(extent))]
    entries = entries.at[tuple(place)].set(low)
    longest = extent.index(max(extent))
    place[longest] = (place[longest] + 1) % extent[longest]
    return entries.at[tuple(place)].set(top_value)


def block_levels(stream_key, extent, pieces, low, high):
    level = 1.0
    for dim, shards_of in pieces:
        steps = jax.random.uniform(jax.random.fold_in(jax.random.fold_in(stream_key, 6), dim), (shards_of,), jnp.float32, low / len(pieces), high / len(pieces))
        level = level * jnp.repeat(jnp.exp(steps), extent[dim] // shards_of).reshape((-1,) + (1,) * (len(extent) - 1 - dim))
    return level


def scatter_about(stream_key, shape, deviation, reach, cuts=(), held_as=jnp.bfloat16):
    values = jax.random.normal(stream_key, shape, jnp.float32) * deviation
    if len(cuts) > 0:
        values = block_levels(stream_key, shape, cuts, -0.22, 0.18) * values
    return jnp.clip(values, min=-reach, max=reach).astype(held_as)


def setup_inputs(seed: int = 0, part: int = 0) -> dict:
    arg_keys = jax.random.split(jax.random.key(seed), 7)
    own_keys = jax.random.split(jax.random.fold_in(arg_keys[6], part), 7)
    return {
        "blocks": scatter_about(own_keys[0], (NBLOCKS, BLKW, NAUX), 64 ** -0.5, 0.75, ((0, 8), (2, 2))),
        "wanted": draw_wanted(jax.random.fold_in(jax.random.fold_in(arg_keys[6], part), 71), part),
        "pair_slots": with_ends(jax.random.randint(own_keys[2], (PAIRS, 2 * DOM), 0, UNIQ), jax.random.fold_in(own_keys[2], 1), 0, UNIQ - 1).astype(jnp.int32),
        "fock": scatter_about(own_keys[3], (PAIRS, DOMW, DOMW), DOMW ** -0.5, 0.375, ((0, 16),)),
        "correlation": scatter_about(own_keys[4], (PAIRS, DOMW, DOMW), DOMW ** -0.5, 0.375, ((0, 16),)),
        "amplitudes": scatter_about(own_keys[5], (PAIRS, DOMW, DOMW), 1.0, 6.0, ((0, 16),)),
    }


def reference(blocks, wanted, pair_slots, fock, correlation, amplitudes):
    owner_of_pair = (jnp.arange(PAIRS) // PAIR_DEV).astype(jnp.int32)
    positions = (owner_of_pair[:, None] * UNIQ + pair_slots).astype(jnp.int32)
    chosen = jnp.take(wanted, positions, axis=0)

    def one_pair(items):
        block_ids, fock_pair, correlation_pair, amp_pair = items
        left_rows = jnp.take(blocks, block_ids[:DOM], axis=0).reshape(DOM * BLKW, NAUX)
        right_rows = jnp.take(blocks, block_ids[DOM:], axis=0).reshape(DOM * BLKW, NAUX)
        integrals = jnp.dot(left_rows, right_rows.T, preferred_element_type=jnp.float32)
        fock_amp = jnp.dot(fock_pair, amp_pair, preferred_element_type=jnp.float32).astype(jnp.bfloat16)
        over_amp = jnp.dot(correlation_pair, amp_pair, preferred_element_type=jnp.float32).astype(jnp.bfloat16)
        first_term = jnp.dot(fock_amp, correlation_pair, preferred_element_type=jnp.float32)
        second_term = jnp.dot(over_amp, fock_pair, preferred_element_type=jnp.float32)
        return (integrals + first_term + second_term).astype(jnp.bfloat16)

    return lax.map(one_pair, (chosen, fock, correlation, amplitudes))
```

```python
import functools

import jax
import jax.numpy as jnp
from jax import lax
from jax.experimental import pallas as pl
from jax.experimental.pallas import tpu as pltpu
from jax.sharding import PartitionSpec as P

DOM = 8
UNIQ = 16
TILE = 128
VMEM_BYTES = 48 * 1024 * 1024
SMEM_SPEC = pl.BlockSpec(memory_space=pltpu.SMEM)
VMEM_SPEC = pl.BlockSpec(memory_space=pltpu.VMEM)
ANY_SPEC = pl.BlockSpec(memory_space=pl.ANY)


def upper_tiles(side):
    return [(i, j) for i in range(side) for j in range(i, side)]


def terms_kernel(fock_ref, corr_ref, amp_ref, out_ref):
    fock, corr, amp = fock_ref[0], corr_ref[0], amp_ref[0]
    fock_amp = jnp.dot(fock, amp, preferred_element_type=jnp.float32).astype(jnp.bfloat16)
    over_amp = jnp.dot(corr, amp, preferred_element_type=jnp.float32).astype(jnp.bfloat16)
    first = jnp.dot(fock_amp, corr, preferred_element_type=jnp.float32)
    out_ref[0] = first + jnp.dot(over_amp, fock, preferred_element_type=jnp.float32)


def pair_terms(fock, correlation, amplitudes):
    pairs, rows, cols = fock.shape
    spec = pl.BlockSpec((1, rows, cols), lambda p: (p, 0, 0))
    return pl.pallas_call(
        terms_kernel,
        grid=(pairs,),
        in_specs=[spec] * 3,
        out_specs=spec,
        out_shape=jax.ShapeDtypeStruct(fock.shape, jnp.float32),
        compiler_params=pltpu.CompilerParams(vmem_limit_bytes=VMEM_BYTES),
        cost_estimate=pl.CostEstimate(
            flops=8 * pairs * rows * rows * cols,
            bytes_accessed=10 * pairs * rows * cols,
            transcendentals=0,
        ),
    )(fock, correlation, amplitudes)


def gram_kernel(holders, addr_ref, core_ref, place_ref, blocks_ref, *rest):
    arrived_refs = rest[: holders - 1]
    keep_ref, send_ref, pool, rows_ref, sems = rest[holders - 1 :]
    owned, width, depth = blocks_ref.shape
    columns = depth // holders
    start = pl.multiple_of(place_ref[0] * columns, TILE)
    copies = [
        pltpu.make_async_copy(
            blocks_ref.at[:, :, pl.ds(start, columns)], pool.at[pl.ds(0, owned)], sems.at[0]
        )
    ]
    for k, ref in enumerate(arrived_refs, 1):
        copies.append(
            pltpu.make_async_copy(ref, pool.at[pl.ds(k * owned, owned)], sems.at[k])
        )
    for copy in copies:
        copy.start()
    for copy in copies:
        copy.wait()
    side = UNIQ * width // TILE
    half = len(upper_tiles(side)) // 2
    core = core_ref[0]

    @pl.loop(0, holders)
    def _(k):
        for m in range(UNIQ):
            rows_ref[m * width : (m + 1) * width, :] = pool[addr_ref[k, m]]
        tiles = []
        for i in range(side):
            strip = lax.dot_general(
                rows_ref[i * TILE : (i + 1) * TILE, :],
                rows_ref[i * TILE :, :],
                (((1,), (1,)), ((), ())),
                preferred_element_type=jnp.float32,
            ).astype(jnp.bfloat16)
            for j in range(i, side):
                tiles.append(strip[:, (j - i) * TILE : (j - i + 1) * TILE])

        @pl.when(core == 0)
        def _():
            for t in range(half):
                keep_ref[k, t * TILE : (t + 1) * TILE, :] = tiles[t]
                send_ref[k, t * TILE : (t + 1) * TILE, :] = tiles[half + t]

        @pl.when(core != 0)
        def _():
            for t in range(half):
                send_ref[k, t * TILE : (t + 1) * TILE, :] = tiles[t]
                keep_ref[k, t * TILE : (t + 1) * TILE, :] = tiles[half + t]


def partial_grams(addr, core, place, blocks, arrived):
    holders = len(arrived) + 1
    owned, width, depth = blocks.shape
    columns = depth // holders
    side = UNIQ * width // TILE
    half = len(upper_tiles(side)) // 2
    out = jax.ShapeDtypeStruct((holders, half * TILE, TILE), jnp.bfloat16)
    return pl.pallas_call(
        functools.partial(gram_kernel, holders),
        in_specs=[SMEM_SPEC] * 3 + [ANY_SPEC] * holders,
        out_specs=[VMEM_SPEC] * 2,
        out_shape=[out, out],
        scratch_shapes=[
            pltpu.VMEM((holders * owned, width, columns), jnp.bfloat16),
            pltpu.VMEM((UNIQ * width, columns), jnp.bfloat16),
            pltpu.SemaphoreType.DMA((holders,)),
        ],
        compiler_params=pltpu.CompilerParams(vmem_limit_bytes=VMEM_BYTES),
        cost_estimate=pl.CostEstimate(
            flops=2 * holders * (UNIQ * width) ** 2 * columns,
            bytes_accessed=2 * holders * owned * width * columns,
            transcendentals=0,
        ),
    )(addr, core, place, blocks, *arrived)


def finish_kernel(slots_ref, core_ref, mine_ref, other_ref, right_ref, terms_ref, out_ref, gram):
    core = core_ref[0]
    side = gram.shape[0] // TILE
    order = upper_tiles(side)
    half = len(order) // 2
    width = gram.shape[0] // UNIQ
    pair = pl.program_id(0)

    def place(t, value):
        i, j = order[t]
        gram[i * TILE : (i + 1) * TILE, j * TILE : (j + 1) * TILE] = value
        if i != j:
            flipped = value.astype(jnp.float32).T.astype(jnp.bfloat16)
            gram[j * TILE : (j + 1) * TILE, i * TILE : (i + 1) * TILE] = flipped

    @pl.when(pair == 0)
    def _():
        for t in range(half):
            mine = mine_ref[t * TILE : (t + 1) * TILE, :]
            other = other_ref[t * TILE : (t + 1) * TILE, :]
            place(t, jnp.where(core == 0, mine, other))
            place(half + t, jnp.where(core == 0, other, mine))

    left = jnp.concatenate(
        [gram[pl.ds(slots_ref[pair, m] * width, width), :] for m in range(DOM)], axis=0
    )
    rows = lax.broadcasted_iota(jnp.int32, (gram.shape[0], DOM * width), 0)
    choose = (rows == right_ref[0]).astype(jnp.float32).astype(jnp.bfloat16)
    integrals = jnp.dot(left, choose, preferred_element_type=jnp.float32)
    out_ref[0] = (integrals + terms_ref[0]).astype(jnp.bfloat16)


def finish(slots, core, mine, other, right_rows, terms):
    pairs, rows, cols = terms.shape
    tile = pl.BlockSpec((1, rows, cols), lambda p: (p, 0, 0))
    whole = pl.BlockSpec(mine.shape, lambda p: (0, 0))
    gram_side = UNIQ * rows // DOM
    return pl.pallas_call(
        finish_kernel,
        grid=(pairs,),
        in_specs=[
            SMEM_SPEC,
            SMEM_SPEC,
            whole,
            whole,
            pl.BlockSpec((1, 1, cols), lambda p: (p, 0, 0)),
            tile,
        ],
        out_specs=tile,
        out_shape=jax.ShapeDtypeStruct(terms.shape, jnp.bfloat16),
        scratch_shapes=[pltpu.VMEM((gram_side, gram_side), jnp.bfloat16)],
        compiler_params=pltpu.CompilerParams(vmem_limit_bytes=VMEM_BYTES),
        cost_estimate=pl.CostEstimate(
            flops=2 * pairs * rows * cols * gram_side,
            bytes_accessed=6 * pairs * rows * cols,
            transcendentals=0,
        ),
    )(slots, core, mine, other, right_rows, terms)


def swap(value, axis, bit):
    size = lax.axis_size(axis)
    return lax.ppermute(value, axis, [(i, i ^ bit) for i in range(size)])


def split_by_columns(blocks, wanted, pair_slots, fock, correlation, amplitudes):
    holders = lax.axis_size("pairs")
    me = lax.axis_index("pairs")
    core = lax.axis_index("aux")
    owned, width, depth = blocks.shape
    columns = depth // holders
    everyone = lax.all_gather(wanted, "pairs", tiled=False)
    arrived = []
    for k in range(1, holders):
        part = lax.dynamic_slice_in_dim(blocks, (me ^ k) * columns, columns, axis=2)
        arrived.append(swap(part, "pairs", k))
    owners = me ^ jnp.arange(holders, dtype=jnp.int32)
    asked = jnp.take(everyone, owners, axis=0)
    addr = ((asked // owned) ^ me) * owned + asked % owned
    pairs_here = fock.shape[0]
    slots = lax.dynamic_slice_in_dim(pair_slots, core * pairs_here, pairs_here, axis=0)
    offsets = jnp.arange(width, dtype=jnp.int32)
    right_rows = (slots[:, DOM:, None] * width + offsets).reshape(pairs_here, 1, DOM * width)
    terms = pair_terms(fock, correlation, amplitudes)
    core_id = core.reshape(1).astype(jnp.int32)
    keep, send = partial_grams(addr, core_id, me.reshape(1).astype(jnp.int32), blocks, arrived)
    both = keep.astype(jnp.float32) + swap(send, "aux", 1).astype(jnp.float32)
    both = both.astype(jnp.bfloat16)
    total = both[0].astype(jnp.float32)
    for k in range(1, holders):
        total = total + swap(both[k], "pairs", k).astype(jnp.float32)
    mine = total.astype(jnp.bfloat16)
    other = swap(mine, "aux", 1)
    return finish(slots, core_id, mine, other, right_rows, terms)


def pick_tiles(gram, left_ids, right_ids):
    count = left_ids.shape[0]
    sides = left_ids.shape[1]
    width = gram.shape[2]
    tiles = gram[left_ids[:, :, None], right_ids[:, None, :]]
    return tiles.transpose(0, 1, 3, 2, 4).reshape(count, sides * width, sides * width)


def pair_integrals(held, left_ids, right_ids):
    units, width, depth = held.shape
    stacked = held.reshape(units * width, depth)
    gram = lax.dot_general(
        stacked, stacked, (((1,), (1,)), ((), ())), preferred_element_type=jnp.float32
    )
    gram = gram.reshape(units, width, units, width).transpose(0, 2, 1, 3)
    return pick_tiles(gram, left_ids, right_ids)


def by_request(blocks, wanted, pair_slots, fock, correlation, amplitudes):
    holders = lax.axis_size("pairs")
    owned, width, depth = blocks.shape
    capacity = max(2, (2 * UNIQ + holders - 1) // holders)
    holder = wanted // owned
    local_ids = wanted - holder * owned
    order_ids = jnp.arange(wanted.shape[0])
    earlier = (holder[None, :] == holder[:, None]) & (order_ids[None, :] < order_ids[:, None])
    rank = jnp.sum(earlier.astype(jnp.int32), axis=1)
    slot = holder * capacity + rank
    places = jnp.arange(holders * capacity)
    table = jnp.sum(jnp.where(places[:, None] == slot[None, :], local_ids[None, :], 0), axis=1)
    table = table.reshape(holders, capacity)
    asked = lax.all_to_all(table, "pairs", split_axis=0, concat_axis=0, tiled=True)
    outgoing = jnp.take(blocks, asked.reshape(-1), axis=0).reshape(holders, capacity, width, depth)
    arrived = lax.all_to_all(outgoing, "pairs", split_axis=0, concat_axis=0, tiled=True)
    held = jnp.take(arrived.reshape(holders * capacity, width, depth), slot, axis=0)
    partial_value = pair_integrals(held, pair_slots[:, :DOM], pair_slots[:, DOM:])
    integrals = lax.psum_scatter(
        partial_value.astype(jnp.bfloat16), "aux", scatter_dimension=0, tiled=True
    ).astype(jnp.float32)
    terms = pair_terms(fock, correlation, amplitudes)
    return (integrals + terms).astype(jnp.bfloat16)


def on_device(blocks, *others):
    holders = lax.axis_size("pairs")
    even = holders & (holders - 1) == 0 and blocks.shape[2] % (TILE * holders) == 0
    body = split_by_columns if even and holders <= UNIQ else by_request
    return body(blocks, *others)


def solution(mesh):
    return jax.shard_map(
        on_device,
        mesh=mesh,
        in_specs=(
            P(("groups", "pairs"), None, "aux"),
            P(("groups", "pairs")),
            P(("groups", "pairs"), None),
            P(("groups", "pairs", "aux"), None, None),
            P(("groups", "pairs", "aux"), None, None),
            P(("groups", "pairs", "aux"), None, None),
        ),
        out_specs=P(("groups", "pairs", "aux"), None, None),
        check_vma=False,
    )
```

```python
import functools

import jax
import jax.numpy as jnp
from jax import lax
from jax.experimental import pallas as pl
from jax.experimental.pallas import tpu as pltpu
from jax.sharding import PartitionSpec as P

DOM = 8
UNIQ = 16
TILE = 128
STRIP = 256
LIST_ROWS = 16
VMEM_BYTES = 60 * 1024 * 1024
LAST_VMEM = 24 * 1024 * 1024
FIRST = 448
SMEM_SPEC = pl.BlockSpec(memory_space=pltpu.SMEM)
VMEM_SPEC = pl.BlockSpec(memory_space=pltpu.VMEM)
HBM_SPEC = pl.BlockSpec(memory_space=pltpu.HBM)


def upper_tiles(side):
    return [(i, j) for i in range(side) for j in range(i, side)]


def terms_kernel(fock_ref, corr_ref, amp_ref, out_ref):
    fock, corr, amp = fock_ref[0], corr_ref[0], amp_ref[0]
    fock_amp = jnp.dot(fock, amp, preferred_element_type=jnp.float32).astype(jnp.bfloat16)
    over_amp = jnp.dot(corr, amp, preferred_element_type=jnp.float32).astype(jnp.bfloat16)
    first = jnp.dot(fock_amp, corr, preferred_element_type=jnp.float32)
    out_ref[0] = first + jnp.dot(over_amp, fock, preferred_element_type=jnp.float32)


def pair_terms(fock, correlation, amplitudes):
    pairs, rows, cols = fock.shape
    spec = pl.BlockSpec((1, rows, cols), lambda p: (p, 0, 0))
    return pl.pallas_call(
        terms_kernel,
        grid=(pairs,),
        in_specs=[spec] * 3,
        out_specs=spec,
        out_shape=jax.ShapeDtypeStruct(fock.shape, jnp.float32),
        compiler_params=pltpu.CompilerParams(vmem_limit_bytes=VMEM_BYTES),
        cost_estimate=pl.CostEstimate(
            flops=8 * pairs * rows * rows * cols,
            bytes_accessed=10 * pairs * rows * cols,
            transcendentals=0,
        ),
    )(fock, correlation, amplitudes)


def split_kernel(offsets, wanted_ref, place_ref, core_ref, blocks_ref, *rest):
    count = (len(rest) - 3) // 2
    outs, bufs, (tail, in_sems, out_sems) = rest[:count], rest[count : 2 * count], rest[-3:]
    rows, depth = blocks_ref.shape
    chunks = (outs[0].shape[0] - LIST_ROWS) // rows
    lane = lax.broadcasted_iota(jnp.int32, tail.shape, 1)

    def fetch(n, c):
        offset = jnp.where(core_ref[0] % 2 == 0, offsets[0][n], offsets[1][n])
        start = pl.multiple_of(((place_ref[0] ^ offset) * chunks + c) * TILE, TILE)
        return pltpu.make_async_copy(
            blocks_ref.at[:, pl.ds(start, TILE)],
            bufs[n].at[pl.ds(c * rows, rows)],
            in_sems.at[n, c],
        )

    fetches = [[fetch(n, c) for c in range(chunks)] for n in range(count)]
    for some in fetches:
        for copy in some:
            copy.start()
    ids = jnp.zeros(tail.shape, jnp.int32)
    for m in range(UNIQ):
        ids = jnp.where(lane == m, wanted_ref[m], ids)
    tail[...] = ids.astype(jnp.float32).astype(jnp.bfloat16)
    for buf in bufs:
        buf[chunks * rows :, :] = tail[...]
    stores = []
    for n, (buf, out) in enumerate(zip(bufs, outs)):
        for copy in fetches[n]:
            copy.wait()
        stores.append(pltpu.make_async_copy(buf, out, out_sems.at[n]))
        stores[-1].start()
    for copy in stores:
        copy.wait()


def column_parts(offsets, holders, wanted, place, core, blocks):
    rows, depth = blocks.shape
    chunks = depth // holders // TILE
    shape = (chunks * rows + LIST_ROWS, TILE)
    count = len(offsets[0])
    return pl.pallas_call(
        functools.partial(split_kernel, offsets),
        in_specs=[SMEM_SPEC] * 3 + [HBM_SPEC],
        out_specs=[HBM_SPEC] * count,
        out_shape=[jax.ShapeDtypeStruct(shape, blocks.dtype)] * count,
        scratch_shapes=[
            *([pltpu.VMEM(shape, blocks.dtype)] * count),
            pltpu.VMEM((LIST_ROWS, TILE), blocks.dtype),
            pltpu.SemaphoreType.DMA((count, chunks)),
            pltpu.SemaphoreType.DMA((count,)),
        ],
        compiler_params=pltpu.CompilerParams(vmem_limit_bytes=VMEM_BYTES),
    )(wanted, place, core, blocks)


def gram_kernel(ks, owned, wanted_ref, core_ref, place_ref, slot_ref, blocks_ref, *rest):
    holders = 1 + len(rest) - 8
    arrived_refs = rest[: holders - 1]
    keep_ref, send_ref, pool, lists, ids_vmem, ids, sems, list_sems = rest[holders - 1 :]
    rows, depth = blocks_ref.shape
    width = rows // owned
    chunks = depth // holders // TILE
    part = chunks * rows
    me = place_ref[0]
    tails = [
        pltpu.make_async_copy(ref.at[pl.ds(part, LIST_ROWS)], lists.at[k], list_sems.at[k])
        for k, ref in enumerate(arrived_refs, 1)
    ]
    for copy in tails:
        copy.start()
    copies = []
    for c in range(chunks):
        start = pl.multiple_of((me * chunks + c) * TILE, TILE)
        copies.append(
            pltpu.make_async_copy(
                blocks_ref.at[:, pl.ds(start, TILE)], pool.at[pl.ds(c * rows, rows)], sems.at[0, c]
            )
        )
    for k, ref in enumerate(arrived_refs, 1):
        copies.append(
            pltpu.make_async_copy(
                ref.at[pl.ds(0, part)], pool.at[pl.ds(k * part, part)], sems.at[k, 0]
            )
        )
    for copy in copies:
        copy.start()
    for copy in tails:
        copy.wait()
    for n, k in enumerate(ks):
        if k > 0:
            ids_vmem[n, :] = lists[slot_ref[k]].astype(jnp.float32).astype(jnp.int32)[0]
    to_scalars = pltpu.make_async_copy(ids_vmem, ids, list_sems.at[0])
    to_scalars.start()
    to_scalars.wait()
    for n, k in enumerate(ks):
        if k == 0:
            for m in range(UNIQ):
                ids[n, m] = wanted_ref[m]
    for copy in copies:
        copy.wait()
    side = UNIQ * width // TILE
    half = len(upper_tiles(side)) // 2
    core = core_ref[0]

    @pl.loop(0, len(ks))
    def _(n):
        places = []
        for m in range(UNIQ):
            holder = lax.div(ids[n, m], owned)
            local = ids[n, m] - holder * owned
            places.append(slot_ref[holder ^ me] * part + local * width)
        held = jnp.concatenate(
            [
                jnp.concatenate(
                    [
                        pool[pl.ds(pl.multiple_of(place + c * rows, width), width), :]
                        for place in places
                    ],
                    axis=0,
                )
                for c in range(chunks)
            ],
            axis=1,
        )
        found = {}
        for top in range(0, side * TILE, STRIP):
            strip = lax.dot_general(
                held[top : top + STRIP],
                held[top:],
                (((1,), (1,)), ((), ())),
                preferred_element_type=jnp.float32,
            ).astype(jnp.bfloat16)
            for i in range(top // TILE, min(top + STRIP, side * TILE) // TILE):
                for j in range(i, side):
                    r, c = i * TILE - top, j * TILE - top
                    found[i, j] = strip[r : r + TILE, c : c + TILE]
        tiles = [found[t] for t in upper_tiles(side)]

        @pl.when(core == 0)
        def _():
            for t in range(half):
                keep_ref[n, t * TILE : (t + 1) * TILE, :] = tiles[t]
                send_ref[n, t * TILE : (t + 1) * TILE, :] = tiles[half + t]

        @pl.when(core != 0)
        def _():
            for t in range(half):
                send_ref[n, t * TILE : (t + 1) * TILE, :] = tiles[t]
                keep_ref[n, t * TILE : (t + 1) * TILE, :] = tiles[half + t]


def partial_grams(ks, owned, wanted, core, place, slot, blocks, arrived):
    holders = len(arrived) + 1
    rows, depth = blocks.shape
    columns = depth // holders
    side = UNIQ * rows // owned // TILE
    half = len(upper_tiles(side)) // 2
    out = jax.ShapeDtypeStruct((len(ks), half * TILE, TILE), jnp.bfloat16)
    return pl.pallas_call(
        functools.partial(gram_kernel, ks, owned),
        in_specs=[SMEM_SPEC] * 4 + [HBM_SPEC] * holders,
        out_specs=[VMEM_SPEC] * 2,
        out_shape=[out, out],
        scratch_shapes=[
            pltpu.VMEM((holders * rows * columns // TILE, TILE), jnp.bfloat16),
            pltpu.VMEM((holders, LIST_ROWS, TILE), jnp.bfloat16),
            pltpu.VMEM((len(ks), TILE), jnp.int32),
            pltpu.SMEM((len(ks), TILE), jnp.int32),
            pltpu.SemaphoreType.DMA((holders, max(2, columns // TILE))),
            pltpu.SemaphoreType.DMA((holders,)),
        ],
        compiler_params=pltpu.CompilerParams(vmem_limit_bytes=VMEM_BYTES),
        cost_estimate=pl.CostEstimate(
            flops=2 * len(ks) * (side * TILE) ** 2 * columns,
            bytes_accessed=2 * holders * rows * columns,
            transcendentals=0,
        ),
    )(wanted, core, place, slot, blocks, *arrived)


def finish_kernel(slots_ref, core_ref, mine_ref, other_ref, right_ref, terms_ref, out_ref, gram):
    core = core_ref[0]
    side = gram.shape[0] // TILE
    order = upper_tiles(side)
    half = len(order) // 2
    width = gram.shape[0] // UNIQ
    pair = pl.program_id(0)

    def place(t, value):
        i, j = order[t]
        gram[i * TILE : (i + 1) * TILE, j * TILE : (j + 1) * TILE] = value
        if i != j:
            flipped = value.astype(jnp.float32).T.astype(jnp.bfloat16)
            gram[j * TILE : (j + 1) * TILE, i * TILE : (i + 1) * TILE] = flipped

    @pl.when(pair == 0)
    def _():
        for t in range(half):
            mine = mine_ref[t * TILE : (t + 1) * TILE, :]
            other = other_ref[t * TILE : (t + 1) * TILE, :]
            place(t, jnp.where(core == 0, mine, other))
            place(half + t, jnp.where(core == 0, other, mine))

    left = jnp.concatenate(
        [gram[pl.ds(slots_ref[pair, m] * width, width), :] for m in range(DOM)], axis=0
    )
    rows = lax.broadcasted_iota(jnp.int32, (gram.shape[0], DOM * width), 0)
    choose = (rows == right_ref[0]).astype(jnp.float32).astype(jnp.bfloat16)
    integrals = jnp.dot(left, choose, preferred_element_type=jnp.float32)
    out_ref[0] = (integrals + terms_ref[0]).astype(jnp.bfloat16)


def finish(slots, core, mine, other, right_rows, terms):
    pairs, rows, cols = terms.shape
    tile = pl.BlockSpec((1, rows, cols), lambda p: (p, 0, 0))
    whole = pl.BlockSpec(mine.shape, lambda p: (0, 0))
    gram_side = UNIQ * rows // DOM
    return pl.pallas_call(
        finish_kernel,
        grid=(pairs,),
        in_specs=[
            SMEM_SPEC,
            SMEM_SPEC,
            whole,
            whole,
            pl.BlockSpec((1, 1, cols), lambda p: (p, 0, 0)),
            tile,
        ],
        out_specs=tile,
        out_shape=jax.ShapeDtypeStruct(terms.shape, jnp.bfloat16),
        scratch_shapes=[pltpu.VMEM((gram_side, gram_side), jnp.bfloat16)],
        compiler_params=pltpu.CompilerParams(vmem_limit_bytes=LAST_VMEM),
        cost_estimate=pl.CostEstimate(
            flops=2 * pairs * rows * cols * gram_side,
            bytes_accessed=6 * pairs * rows * cols,
            transcendentals=0,
        ),
    )(slots, core, mine, other, right_rows, terms)


def swap(value, axis, bit):
    size = lax.axis_size(axis)
    return lax.ppermute(value, axis, [(i, i ^ bit) for i in range(size)])


def add(*values):
    return sum(value.astype(jnp.float32) for value in values)


def to_owner(keep, came):
    half = keep.shape[0] // 2
    keep, came = (v.reshape(2, half, *v.shape[1:]) for v in (keep, came))

    def both(bits, offsets, rows):
        return add(keep[bits, offsets, rows], came[bits, offsets, rows]).astype(jnp.bfloat16)

    every, top, rest = slice(None), slice(0, FIRST), slice(FIRST, None)
    top_near = swap(both(1, every, top), "pairs", 1)
    rest_far = [swap(both(every, j, rest), "pairs", 2 * j) for j in range(1, half)]
    top_sums = [
        add(keep[0, j, top], came[0, j, top], top_near[j]).astype(jnp.bfloat16)
        for j in range(half)
    ]
    top_far = [swap(top_sums[j], "pairs", 2 * j) for j in range(1, half)]
    rest_sums = [
        add(keep[b, 0, rest], came[b, 0, rest], *(v[b] for v in rest_far)).astype(jnp.bfloat16)
        for b in range(2)
    ]
    rest_near = swap(rest_sums[1], "pairs", 1)
    top_total = add(top_sums[0], *top_far).astype(jnp.bfloat16)
    rest_total = add(rest_sums[0], rest_near).astype(jnp.bfloat16)
    return jnp.concatenate([top_total, rest_total], axis=0)


def exchange_orders(holders):
    light, heavy = [*range(1, holders // 2)], [*range(holders // 2, holders)]
    first = heavy[:1]
    for pair in zip(heavy[1:], light):
        first += pair
    second = [k for pair in zip(light, heavy) for k in pair] + heavy[-1:]
    return [first, second]


def split_by_columns(blocks, wanted, pair_slots, fock, correlation, amplitudes):
    holders = lax.axis_size("pairs")
    core = lax.axis_index("aux")
    owned, width, depth = blocks.shape
    stacked = blocks.reshape(owned * width, depth)
    place = lax.axis_index("pairs").reshape(1).astype(jnp.int32)
    core_id = core.reshape(1).astype(jnp.int32)
    orders = exchange_orders(holders)
    slot_tables = [[0] * holders for _ in orders]
    for table, ks in zip(slot_tables, orders):
        for n, k in enumerate(ks, 1):
            table[k] = n
    slot = jnp.asarray(slot_tables, jnp.int32)[core % 2]
    early = 2
    begun = column_parts([o[:early] for o in orders], holders, wanted, place, core_id, stacked)
    begun, later = lax.optimization_barrier((begun, stacked))
    parts = begun + column_parts([o[early:] for o in orders], holders, wanted, place, core_id, later)
    arrived = []
    cores = lax.axis_size("aux")
    for n, part in enumerate(parts):
        moves = [
            (p * cores + c, (p ^ orders[c % 2][n]) * cores + c)
            for p in range(holders)
            for c in range(cores)
        ]
        arrived.append(lax.ppermute(part, ("pairs", "aux"), moves))
    pairs_here = fock.shape[0]
    slots = lax.dynamic_slice_in_dim(pair_slots, core * pairs_here, pairs_here, axis=0)
    offsets = jnp.arange(width, dtype=jnp.int32)
    right_rows = (slots[:, DOM:, None] * width + offsets).reshape(pairs_here, 1, DOM * width)
    terms = pair_terms(fock, correlation, amplitudes)
    arrived, terms = lax.optimization_barrier((arrived, terms))
    shared = (owned, wanted, core_id, place, slot, stacked, arrived)
    order = (*range(0, holders, 2), *range(1, holders, 2))
    keep, send = partial_grams(order, *shared)
    mine = to_owner(keep, swap(send, "aux", 1))
    other = swap(mine, "aux", 1)
    return finish(slots, core_id, mine, other, right_rows, terms)


def pick_tiles(gram, left_ids, right_ids):
    count = left_ids.shape[0]
    sides = left_ids.shape[1]
    width = gram.shape[2]
    tiles = gram[left_ids[:, :, None], right_ids[:, None, :]]
    return tiles.transpose(0, 1, 3, 2, 4).reshape(count, sides * width, sides * width)


def pair_integrals(held, left_ids, right_ids):
    units, width, depth = held.shape
    stacked = held.reshape(units * width, depth)
    gram = lax.dot_general(
        stacked, stacked, (((1,), (1,)), ((), ())), preferred_element_type=jnp.float32
    )
    gram = gram.reshape(units, width, units, width).transpose(0, 2, 1, 3)
    return pick_tiles(gram, left_ids, right_ids)


def by_request(blocks, wanted, pair_slots, fock, correlation, amplitudes):
    holders = lax.axis_size("pairs")
    owned, width, depth = blocks.shape
    capacity = max(2, (2 * UNIQ + holders - 1) // holders)
    holder = wanted // owned
    local_ids = wanted - holder * owned
    order_ids = jnp.arange(wanted.shape[0])
    earlier = (holder[None, :] == holder[:, None]) & (order_ids[None, :] < order_ids[:, None])
    rank = jnp.sum(earlier.astype(jnp.int32), axis=1)
    slot = holder * capacity + rank
    places = jnp.arange(holders * capacity)
    table = jnp.sum(jnp.where(places[:, None] == slot[None, :], local_ids[None, :], 0), axis=1)
    table = table.reshape(holders, capacity)
    asked = lax.all_to_all(table, "pairs", split_axis=0, concat_axis=0, tiled=True)
    outgoing = jnp.take(blocks, asked.reshape(-1), axis=0).reshape(holders, capacity, width, depth)
    arrived = lax.all_to_all(outgoing, "pairs", split_axis=0, concat_axis=0, tiled=True)
    held = jnp.take(arrived.reshape(holders * capacity, width, depth), slot, axis=0)
    partial_value = pair_integrals(held, pair_slots[:, :DOM], pair_slots[:, DOM:])
    integrals = lax.psum_scatter(
        partial_value.astype(jnp.bfloat16), "aux", scatter_dimension=0, tiled=True
    ).astype(jnp.float32)
    terms = pair_terms(fock, correlation, amplitudes)
    return (integrals + terms).astype(jnp.bfloat16)


def on_device(blocks, *others):
    holders = lax.axis_size("pairs")
    even = holders > 1 and holders & (holders - 1) == 0
    even = even and blocks.shape[2] % (TILE * holders) == 0 and holders * blocks.shape[0] <= 256
    return (split_by_columns if even else by_request)(blocks, *others)


def solution(mesh):
    return jax.shard_map(
        on_device,
        mesh=mesh,
        in_specs=(
            P(("groups", "pairs"), None, "aux"),
            P(("groups", "pairs")),
            P(("groups", "pairs"), None),
            P(("groups", "pairs", "aux"), None, None),
            P(("groups", "pairs", "aux"), None, None),
            P(("groups", "pairs", "aux"), None, None),
        ),
        out_specs=P(("groups", "pairs", "aux"), None, None),
        check_vma=False,
    )
```

```python
import functools

import jax
import jax.numpy as jnp
from jax import lax
from jax.experimental import pallas as pl
from jax.experimental.pallas import tpu as pltpu
from jax.sharding import PartitionSpec as P

DOM = 8
UNIQ = 16
TILE = 128
SIDE = 4
LATE = 1
STRIP = 256
LIST_ROWS = 16
VMEM_BYTES = 60 * 1024 * 1024
LAST_VMEM = 24 * 1024 * 1024
FIRST = 416
SMEM_SPEC = pl.BlockSpec(memory_space=pltpu.SMEM)
VMEM_SPEC = pl.BlockSpec(memory_space=pltpu.VMEM)
HBM_SPEC = pl.BlockSpec(memory_space=pltpu.HBM)


def terms_kernel(right_ref, fock_ref, corr_ref, amp_ref, out_ref, choose_ref):
    fock, corr, amp = fock_ref[0], corr_ref[0], amp_ref[0]
    fock_amp = jnp.dot(fock, amp, preferred_element_type=jnp.float32).astype(jnp.bfloat16)
    over_amp = jnp.dot(corr, amp, preferred_element_type=jnp.float32).astype(jnp.bfloat16)
    first = jnp.dot(fock_amp, corr, preferred_element_type=jnp.float32)
    out_ref[0] = first + jnp.dot(over_amp, fock, preferred_element_type=jnp.float32)
    rows = lax.broadcasted_iota(jnp.int32, choose_ref.shape[1:], 0)
    choose_ref[0] = (rows == right_ref[0]).astype(jnp.float32).astype(jnp.bfloat16)


def pair_terms(right_rows, fock, correlation, amplitudes):
    pairs, rows, cols = fock.shape
    spec = pl.BlockSpec((1, rows, cols), lambda p: (p, 0, 0))
    side = UNIQ * rows // DOM
    return pl.pallas_call(
        terms_kernel,
        grid=(pairs,),
        in_specs=[pl.BlockSpec((1, 1, cols), lambda p: (p, 0, 0))] + [spec] * 3,
        out_specs=[spec, pl.BlockSpec((1, side, cols), lambda p: (p, 0, 0))],
        out_shape=[
            jax.ShapeDtypeStruct(fock.shape, jnp.float32),
            jax.ShapeDtypeStruct((pairs, side, cols), jnp.bfloat16),
        ],
        compiler_params=pltpu.CompilerParams(vmem_limit_bytes=VMEM_BYTES),
        cost_estimate=pl.CostEstimate(
            flops=8 * pairs * rows * rows * cols,
            bytes_accessed=14 * pairs * rows * cols,
            transcendentals=0,
        ),
    )(right_rows, fock, correlation, amplitudes)


def split_kernel(orders, span, wanted_ref, place_ref, core_ref, blocks_ref, *rest):
    outs, (bufs, tail, in_sems, out_sems) = rest[:-4], rest[-4:]
    rows, depth = blocks_ref.shape
    columns = depth // (len(outs) + 1)
    chunks = bufs.shape[2] // TILE
    with_list = outs[0].shape[0] > chunks * rows
    fetches = []
    for n, ks in enumerate(zip(*orders)):
        offset = jnp.where(core_ref[0] % 2 == 0, *ks)
        start = pl.multiple_of((place_ref[0] ^ offset) * columns + span[0] * TILE, TILE)
        source = blocks_ref.at[:, pl.ds(start, chunks * TILE)]
        fetches.append(pltpu.make_async_copy(source, bufs.at[n], in_sems.at[n]))
        fetches[-1].start()
    stores = []
    if with_list:
        lane = lax.broadcasted_iota(jnp.int32, tail.shape, 1)
        ids = jnp.zeros(tail.shape, jnp.int32)
        for m in range(UNIQ):
            ids = jnp.where(lane == m, wanted_ref[m], ids)
        tail[...] = ids.astype(jnp.float32).astype(jnp.bfloat16)
        for n, out in enumerate(outs):
            target = out.at[pl.ds(chunks * rows, LIST_ROWS)]
            stores.append(pltpu.make_async_copy(tail, target, out_sems.at[n, chunks]))
            stores[-1].start()
    for n, out in enumerate(outs):
        fetches[n].wait()
        for c in range(chunks):
            source = bufs.at[n, :, pl.ds(c * TILE, TILE)]
            target = out.at[pl.ds(c * rows, rows)]
            stores.append(pltpu.make_async_copy(source, target, out_sems.at[n, c]))
            stores[-1].start()
    for copy in stores:
        copy.wait()


def column_parts(orders, span, with_list, wanted, place, core, blocks):
    rows, _ = blocks.shape
    count = len(orders[0])
    chunks = span[1] - span[0]
    height = chunks * rows + LIST_ROWS * with_list
    out = jax.ShapeDtypeStruct((height, TILE), blocks.dtype)
    return pl.pallas_call(
        functools.partial(split_kernel, orders, span),
        in_specs=[SMEM_SPEC] * 3 + [HBM_SPEC],
        out_specs=[HBM_SPEC] * count,
        out_shape=[out] * count,
        scratch_shapes=[
            pltpu.VMEM((count, rows, chunks * TILE), blocks.dtype),
            pltpu.VMEM((LIST_ROWS, TILE), blocks.dtype),
            pltpu.SemaphoreType.DMA((count,)),
            pltpu.SemaphoreType.DMA((count, chunks + 1)),
        ],
        compiler_params=pltpu.CompilerParams(vmem_limit_bytes=VMEM_BYTES),
    )(wanted, place, core, blocks)


def block_order(width):
    bits = width.bit_length() - 1
    row = lax.broadcasted_iota(jnp.int32, (TILE, TILE), 0) >> bits
    col = lax.broadcasted_iota(jnp.int32, (TILE, TILE), 1) >> bits
    return row, col


def packed_gram(held, width):
    tile = {}
    for top in range(0, SIDE * TILE, STRIP):
        strip = lax.dot_general(
            held[top : top + STRIP],
            held[top:],
            (((1,), (1,)), ((), ())),
            preferred_element_type=jnp.float32,
        )
        for i in range(top // TILE, (top + STRIP) // TILE):
            for j in range(i, SIDE):
                r, c = i * TILE - top, j * TILE - top
                tile[i, j] = strip[r : r + TILE, c : c + TILE]
    row, col = block_order(width)

    def diagonal(value):
        found = value[:width]
        for r in range(1, TILE // width):
            here = col[:width] == r
            found = jnp.where(here, value[r * width : (r + 1) * width], found)
        return found

    both = [jnp.where(row <= col, tile[i, i], tile[i + 1, i + 1]) for i in (0, 2)]
    first = [tile[0, 1], tile[0, 2], tile[0, 3], tile[1, 2], diagonal(tile[1, 1])]
    second = [tile[1, 3], tile[2, 3], *both, diagonal(tile[3, 3])]
    return first, second


def gather_rows(pool, places, rows, width, chunks):
    return jnp.concatenate(
        [
            jnp.concatenate(
                [
                    pool[pl.ds(pl.multiple_of(place + c * rows, width), width), :]
                    for place in places
                ],
                axis=0,
            )
            for c in range(chunks)
        ],
        axis=1,
    )


def pool_copies(span, me, blocks_ref, arrived_refs, pool, sems):
    rows, depth = blocks_ref.shape
    holders = len(arrived_refs) + 1
    part = (span[1] - span[0]) * rows
    copies = []
    for n, c in enumerate(range(*span)):
        start = pl.multiple_of(me * (depth // holders) + c * TILE, TILE)
        source = blocks_ref.at[:, pl.ds(start, TILE)]
        copies.append(pltpu.make_async_copy(source, pool.at[pl.ds(n * rows, rows)], sems.at[0, n]))
    for k, ref in enumerate(arrived_refs, 1):
        target = pool.at[pl.ds(k * part, part)]
        copies.append(pltpu.make_async_copy(ref.at[pl.ds(0, part)], target, sems.at[k, 0]))
    return copies


def early_kernel(ks, span, owned, wanted_ref, place_ref, slot_ref, blocks_ref, *rest):
    arrived_refs, rest = rest[:-8], rest[-8:]
    acc_ref, spots_ref, pool, lists, ids_vmem, ids, sems, list_sems = rest
    rows = blocks_ref.shape[0]
    width = rows // owned
    chunks = span[1] - span[0]
    part = chunks * rows
    me = place_ref[0]
    tails = [
        pltpu.make_async_copy(ref.at[pl.ds(part, LIST_ROWS)], lists.at[k], list_sems.at[k])
        for k, ref in enumerate(arrived_refs, 1)
    ]
    copies = pool_copies(span, me, blocks_ref, arrived_refs, pool, sems)
    for copy in tails + copies:
        copy.start()
    for copy in tails:
        copy.wait()
    ids_vmem[...] = jnp.zeros_like(ids_vmem)
    for n, k in enumerate(ks):
        if k > 0:
            ids_vmem[n, :] = lists[slot_ref[k]].astype(jnp.float32).astype(jnp.int32)[0]
    to_scalars = pltpu.make_async_copy(ids_vmem, ids, list_sems.at[0])
    to_scalars.start()
    to_scalars.wait()
    for n, k in enumerate(ks):
        for m in range(UNIQ):
            entry = wanted_ref[m] if k == 0 else ids[n, m]
            holder = lax.div(entry, owned)
            spots_ref[n, m] = slot_ref[holder ^ me] * owned + (entry - holder * owned)
    for copy in copies:
        copy.wait()

    @pl.loop(0, len(ks))
    def _(n):
        places = []
        for m in range(UNIQ):
            where = lax.div(spots_ref[n, m], owned)
            places.append(where * part + (spots_ref[n, m] - where * owned) * width)
        held = gather_rows(pool, places, rows, width, chunks)
        at = 0
        for value in sum(packed_gram(held, width), []):
            acc_ref[n, at : at + value.shape[0], :] = value
            at += value.shape[0]


def late_kernel(span, owned, spots_ref, core_ref, place_ref, blocks_ref, acc_ref, *rest):
    arrived_refs, rest = rest[:-4], rest[-4:]
    keep_ref, send_ref, pool, sems = rest
    rows = blocks_ref.shape[0]
    width = rows // owned
    chunks = span[1] - span[0]
    part = chunks * rows
    owners = acc_ref.shape[0]
    half = acc_ref.shape[1] // 2
    core = core_ref[0]
    copies = pool_copies(span, place_ref[0], blocks_ref, arrived_refs, pool, sems)
    for copy in copies:
        copy.start()
    for copy in copies:
        copy.wait()
    for n in range(owners):
        places = []
        for m in range(UNIQ):
            where = lax.div(spots_ref[n, m], owned)
            places.append(where * part + (spots_ref[n, m] - where * owned) * width)
        halves = packed_gram(gather_rows(pool, places, rows, width, chunks), width)
        at = 0
        for first, second in zip(*halves):
            height = first.shape[0]
            first += acc_ref[n, at : at + height, :]
            second += acc_ref[n, half + at : half + at + height, :]
            keep = jnp.where(core == 0, first, second)
            send = jnp.where(core == 0, second, first)
            keep_ref[n, at : at + height, :] = keep.astype(jnp.bfloat16)
            send_ref[n, at : at + height, :] = send.astype(jnp.bfloat16)
            at += height


def half_rows(width):
    return SIDE * TILE + width


def early_grams(ks, span, owned, wanted, place, slot, blocks, arrived):
    holders = len(arrived) + 1
    rows, depth = blocks.shape
    width = rows // owned
    chunks = span[1] - span[0]
    return pl.pallas_call(
        functools.partial(early_kernel, ks, span, owned),
        in_specs=[SMEM_SPEC] * 3 + [HBM_SPEC] * holders,
        out_specs=[VMEM_SPEC, SMEM_SPEC],
        out_shape=[
            jax.ShapeDtypeStruct((len(ks), 2 * half_rows(width), TILE), jnp.float32),
            jax.ShapeDtypeStruct((len(ks), UNIQ), jnp.int32),
        ],
        scratch_shapes=[
            pltpu.VMEM((holders * rows * chunks, TILE), jnp.bfloat16),
            pltpu.VMEM((holders, LIST_ROWS, TILE), jnp.bfloat16),
            pltpu.VMEM((len(ks), TILE), jnp.int32),
            pltpu.SMEM((len(ks), TILE), jnp.int32),
            pltpu.SemaphoreType.DMA((holders, chunks)),
            pltpu.SemaphoreType.DMA((holders,)),
        ],
        compiler_params=pltpu.CompilerParams(vmem_limit_bytes=24 * 1024 * 1024),
        cost_estimate=pl.CostEstimate(
            flops=2 * len(ks) * (SIDE * TILE) ** 2 * chunks * TILE,
            bytes_accessed=2 * holders * rows * chunks * TILE,
            transcendentals=0,
        ),
    )(wanted, place, slot, blocks, *arrived)


def late_grams(span, owned, spots, core, place, blocks, acc, arrived):
    holders = len(arrived) + 1
    rows, depth = blocks.shape
    width = rows // owned
    chunks = span[1] - span[0]
    half = half_rows(width)
    out = jax.ShapeDtypeStruct((acc.shape[0], half, TILE), jnp.bfloat16)
    owners = acc.shape[0]
    return pl.pallas_call(
        functools.partial(late_kernel, span, owned),
        in_specs=[SMEM_SPEC] * 3 + [HBM_SPEC, VMEM_SPEC] + [HBM_SPEC] * len(arrived),
        out_specs=[VMEM_SPEC] * 2,
        out_shape=[out, out],
        scratch_shapes=[
            pltpu.VMEM((holders * rows * chunks, TILE), jnp.bfloat16),
            pltpu.SemaphoreType.DMA((holders, chunks)),
        ],
        compiler_params=pltpu.CompilerParams(vmem_limit_bytes=16 * 1024 * 1024),
        cost_estimate=pl.CostEstimate(
            flops=2 * owners * (SIDE * TILE) ** 2 * chunks * TILE,
            bytes_accessed=2 * holders * rows * chunks * TILE,
            transcendentals=0,
        ),
    )(spots, core, place, blocks, acc, *arrived)


def finish_kernel(slots_ref, core_ref, mine_ref, other_ref, choose_ref, terms_ref, out_ref, gram, stage, sems):
    core = core_ref[0]
    width = gram.shape[0] // UNIQ
    pairs = out_ref.shape[0]

    def put(i, j, value):
        gram[i * TILE : (i + 1) * TILE, j * TILE : (j + 1) * TILE] = value.astype(jnp.bfloat16)

    mine, other = mine_ref[...], other_ref[...]
    first = jnp.where(core == 0, mine, other).astype(jnp.float32)
    second = jnp.where(core == 0, other, mine).astype(jnp.float32)
    pieces = [v[t * TILE : (t + 1) * TILE] for v in (first, second) for t in range(SIDE)]
    places = [(0, 1), (0, 2), (0, 3), (1, 2), (1, 3), (2, 3)]
    for (i, j), value in zip(places, pieces):
        put(i, j, value)
        put(j, i, value.T)
    row, col = block_order(width)
    for i, value, diagonal in zip((0, 2), pieces[6:], (first, second)):
        flipped = value.T
        squares = jnp.concatenate([diagonal[SIDE * TILE :]] * (TILE // width), axis=0)
        put(i, i, jnp.where(row <= col, value, flipped))
        lower = jnp.where(row > col, value, flipped)
        put(i + 1, i + 1, jnp.where(row == col, squares, lower))

    def result(pair):
        return pltpu.make_async_copy(stage.at[pair], out_ref.at[pair], sems.at[pair])

    for pair in range(pairs):
        left = jnp.concatenate(
            [gram[pl.ds(slots_ref[pair, m] * width, width), :] for m in range(DOM)], axis=0
        )
        integrals = jnp.dot(left, choose_ref[pair], preferred_element_type=jnp.float32)
        stage[pair] = (integrals + terms_ref[pair]).astype(jnp.bfloat16)
        result(pair).start()
    for pair in range(pairs):
        result(pair).wait()


def finish(slots, core, mine, other, choose, terms):
    pairs, rows, cols = terms.shape
    gram_side = UNIQ * rows // DOM
    return pl.pallas_call(
        finish_kernel,
        in_specs=[SMEM_SPEC] * 2 + [VMEM_SPEC] * 4,
        out_specs=HBM_SPEC,
        out_shape=jax.ShapeDtypeStruct(terms.shape, jnp.bfloat16),
        scratch_shapes=[
            pltpu.VMEM((gram_side, gram_side), jnp.bfloat16),
            pltpu.VMEM(terms.shape, jnp.bfloat16),
            pltpu.SemaphoreType.DMA((pairs,)),
        ],
        compiler_params=pltpu.CompilerParams(vmem_limit_bytes=LAST_VMEM),
        cost_estimate=pl.CostEstimate(
            flops=2 * pairs * rows * cols * gram_side,
            bytes_accessed=10 * pairs * rows * cols,
            transcendentals=0,
        ),
    )(slots, core, mine, other, choose, terms)


def swap(value, axis, bit):
    size = lax.axis_size(axis)
    return lax.ppermute(value, axis, [(i, i ^ bit) for i in range(size)])


def add(*values):
    return sum(value.astype(jnp.float32) for value in values)


def to_owner(keep, came):
    half = keep.shape[0] // 2
    keep, came = (v.reshape(2, half, *v.shape[1:]) for v in (keep, came))

    def both(bits, offsets, rows):
        return add(keep[bits, offsets, rows], came[bits, offsets, rows]).astype(jnp.bfloat16)

    every, top, rest = slice(None), slice(0, FIRST), slice(FIRST, None)
    top_near = swap(both(1, every, top), "pairs", 1)
    rest_far = [swap(both(every, j, rest), "pairs", 2 * j) for j in range(1, half)]
    top_sums = [
        add(keep[0, j, top], came[0, j, top], top_near[j]).astype(jnp.bfloat16)
        for j in range(half)
    ]
    top_far = [swap(top_sums[j], "pairs", 2 * j) for j in range(1, half)]
    rest_sums = [
        add(keep[b, 0, rest], came[b, 0, rest], *(v[b] for v in rest_far)).astype(jnp.bfloat16)
        for b in range(2)
    ]
    rest_near = swap(rest_sums[1], "pairs", 1)
    top_total = add(top_sums[0], *top_far).astype(jnp.bfloat16)
    rest_total = add(rest_sums[0], rest_near).astype(jnp.bfloat16)
    return jnp.concatenate([top_total, rest_total], axis=0)


def exchange_orders(holders):
    light, heavy = [*range(1, holders // 2)], [*range(holders // 2, holders)]
    first = heavy[:1]
    for pair in zip(heavy[1:], light):
        first += pair
    second = [k for pair in zip(light, heavy) for k in pair] + heavy[-1:]
    return [first, second]


def split_by_columns(blocks, wanted, pair_slots, fock, correlation, amplitudes):
    holders = lax.axis_size("pairs")
    core = lax.axis_index("aux")
    owned, width, depth = blocks.shape
    stacked = blocks.reshape(owned * width, depth)
    place = lax.axis_index("pairs").reshape(1).astype(jnp.int32)
    core_id = core.reshape(1).astype(jnp.int32)
    orders = exchange_orders(holders)
    slot_tables = [[0] * holders for _ in orders]
    for table, ks in zip(slot_tables, orders):
        for n, k in enumerate(ks, 1):
            table[k] = n
    slot = jnp.asarray(slot_tables, jnp.int32)[core % 2]
    chunks = depth // holders // TILE
    cores = lax.axis_size("aux")

    def exchange(parts):
        arrived = []
        for n, part in enumerate(parts):
            moves = [
                (p * cores + c, (p ^ orders[c % 2][n]) * cores + c)
                for p in range(holders)
                for c in range(cores)
            ]
            arrived.append(lax.ppermute(part, ("pairs", "aux"), moves))
        return arrived

    cut = max(1, chunks - LATE)
    first, second = (0, cut), (cut, chunks)
    early = exchange(column_parts(orders, first, True, wanted, place, core_id, stacked))
    tied = len(early) // 2
    early[tied], later = lax.optimization_barrier((early[tied], stacked))
    late = exchange(column_parts(orders, second, False, wanted, place, core_id, later))
    pairs_here = fock.shape[0]
    slots = lax.dynamic_slice_in_dim(pair_slots, core * pairs_here, pairs_here, axis=0)
    offsets = jnp.arange(width, dtype=jnp.int32)
    right_rows = (slots[:, DOM:, None] * width + offsets).reshape(pairs_here, 1, DOM * width)
    terms, choose = pair_terms(right_rows, fock, correlation, amplitudes)
    early, terms, choose, slots = lax.optimization_barrier((early, terms, choose, slots))
    order = (*range(0, holders, 2), *range(1, holders, 2))
    acc, spots = early_grams(order, first, owned, wanted, place, slot, stacked, early)
    keep, send = late_grams(second, owned, spots, core_id, place, stacked, acc, late)
    mine = to_owner(keep, swap(send, "aux", 1))
    other = swap(mine, "aux", 1)
    return finish(slots, core_id, mine, other, choose, terms)


def pick_tiles(gram, left_ids, right_ids):
    count = left_ids.shape[0]
    sides = left_ids.shape[1]
    width = gram.shape[2]
    tiles = gram[left_ids[:, :, None], right_ids[:, None, :]]
    return tiles.transpose(0, 1, 3, 2, 4).reshape(count, sides * width, sides * width)


def pair_integrals(held, left_ids, right_ids):
    units, width, depth = held.shape
    stacked = held.reshape(units * width, depth)
    gram = lax.dot_general(
        stacked, stacked, (((1,), (1,)), ((), ())), preferred_element_type=jnp.float32
    )
    gram = gram.reshape(units, width, units, width).transpose(0, 2, 1, 3)
    return pick_tiles(gram, left_ids, right_ids)


def by_request(blocks, wanted, pair_slots, fock, correlation, amplitudes):
    holders = lax.axis_size("pairs")
    owned, width, depth = blocks.shape
    capacity = max(2, (2 * UNIQ + holders - 1) // holders)
    holder = wanted // owned
    local_ids = wanted - holder * owned
    order_ids = jnp.arange(wanted.shape[0])
    earlier = (holder[None, :] == holder[:, None]) & (order_ids[None, :] < order_ids[:, None])
    rank = jnp.sum(earlier.astype(jnp.int32), axis=1)
    slot = holder * capacity + rank
    places = jnp.arange(holders * capacity)
    table = jnp.sum(jnp.where(places[:, None] == slot[None, :], local_ids[None, :], 0), axis=1)
    table = table.reshape(holders, capacity)
    asked = lax.all_to_all(table, "pairs", split_axis=0, concat_axis=0, tiled=True)
    outgoing = jnp.take(blocks, asked.reshape(-1), axis=0).reshape(holders, capacity, width, depth)
    arrived = lax.all_to_all(outgoing, "pairs", split_axis=0, concat_axis=0, tiled=True)
    held = jnp.take(arrived.reshape(holders * capacity, width, depth), slot, axis=0)
    partial_value = pair_integrals(held, pair_slots[:, :DOM], pair_slots[:, DOM:])
    integrals = lax.psum_scatter(
        partial_value.astype(jnp.bfloat16), "aux", scatter_dimension=0, tiled=True
    ).astype(jnp.float32)
    products = functools.partial(
        jnp.einsum, "pab,pbc->pac", preferred_element_type=jnp.float32
    )
    fock_amp = products(fock, amplitudes).astype(jnp.bfloat16)
    over_amp = products(correlation, amplitudes).astype(jnp.bfloat16)
    terms = products(fock_amp, correlation) + products(over_amp, fock)
    return (integrals + terms).astype(jnp.bfloat16)


def on_device(blocks, *others):
    holders = lax.axis_size("pairs")
    owned, width, depth = blocks.shape
    fits = holders > 1 and holders & (holders - 1) == 0 and width & (width - 1) == 0
    fits = fits and depth % (TILE * holders) == 0 and depth // holders >= 2 * TILE
    fits = fits and holders * owned <= 256 and UNIQ * width == SIDE * TILE
    return (split_by_columns if fits else by_request)(blocks, *others)


def solution(mesh):
    return jax.shard_map(
        on_device,
        mesh=mesh,
        in_specs=(
            P(("groups", "pairs"), None, "aux"),
            P(("groups", "pairs")),
            P(("groups", "pairs"), None),
            P(("groups", "pairs", "aux"), None, None),
            P(("groups", "pairs", "aux"), None, None),
            P(("groups", "pairs", "aux"), None, None),
        ),
        out_specs=P(("groups", "pairs", "aux"), None, None),
        check_vma=False,
    )
```

```python
import functools

import jax
import jax.numpy as jnp
from jax import lax
from jax.experimental import pallas as pl
from jax.experimental.pallas import tpu as pltpu
from jax.sharding import PartitionSpec as P

DOM = 8
UNIQ = 16
TILE = 128
SIDE = 4
LATE = 2
STRIP = 256
LIST_ROWS = 16
VMEM_BYTES = 60 * 1024 * 1024
LAST_VMEM = 24 * 1024 * 1024
FIRST = 416
SMEM_SPEC = pl.BlockSpec(memory_space=pltpu.SMEM)
VMEM_SPEC = pl.BlockSpec(memory_space=pltpu.VMEM)
HBM_SPEC = pl.BlockSpec(memory_space=pltpu.HBM)


def terms_kernel(right_ref, fock_ref, corr_ref, amp_ref, out_ref, choose_ref):
    fock, corr, amp = fock_ref[0], corr_ref[0], amp_ref[0]
    fock_amp = jnp.dot(fock, amp, preferred_element_type=jnp.float32).astype(jnp.bfloat16)
    over_amp = jnp.dot(corr, amp, preferred_element_type=jnp.float32).astype(jnp.bfloat16)
    first = jnp.dot(fock_amp, corr, preferred_element_type=jnp.float32)
    out_ref[0] = first + jnp.dot(over_amp, fock, preferred_element_type=jnp.float32)
    rows = lax.broadcasted_iota(jnp.int32, choose_ref.shape[1:], 0)
    choose_ref[0] = (rows == right_ref[0]).astype(jnp.float32).astype(jnp.bfloat16)


def pair_terms(right_rows, fock, correlation, amplitudes):
    pairs, rows, cols = fock.shape
    spec = pl.BlockSpec((1, rows, cols), lambda p: (p, 0, 0))
    side = UNIQ * rows // DOM
    return pl.pallas_call(
        terms_kernel,
        grid=(pairs,),
        in_specs=[pl.BlockSpec((1, 1, cols), lambda p: (p, 0, 0))] + [spec] * 3,
        out_specs=[spec, pl.BlockSpec((1, side, cols), lambda p: (p, 0, 0))],
        out_shape=[
            jax.ShapeDtypeStruct(fock.shape, jnp.float32),
            jax.ShapeDtypeStruct((pairs, side, cols), jnp.bfloat16),
        ],
        compiler_params=pltpu.CompilerParams(vmem_limit_bytes=VMEM_BYTES),
        cost_estimate=pl.CostEstimate(
            flops=8 * pairs * rows * rows * cols,
            bytes_accessed=14 * pairs * rows * cols,
            transcendentals=0,
        ),
    )(right_rows, fock, correlation, amplitudes)


def split_kernel(orders, span, own, wanted_ref, place_ref, core_ref, blocks_ref, *rest):
    outs, (bufs, own_buf, tail, in_sems, out_sems) = rest[:-5], rest[-5:]
    rows, depth = blocks_ref.shape
    columns = own_buf.shape[1]
    chunks = span[1] - span[0]
    count = len(orders[0])
    fetches, stores = [], []

    def fetch(n, offset, first, buf):
        start = pl.multiple_of((place_ref[0] ^ offset) * columns + first * TILE, TILE)
        source = blocks_ref.at[:, pl.ds(start, buf.shape[1])]
        fetches.append(pltpu.make_async_copy(source, buf, in_sems.at[n]))
        fetches[-1].start()

    def store(n, c, source, out, row):
        target = out.at[pl.ds(row, source.shape[0])]
        stores.append(pltpu.make_async_copy(source, target, out_sems.at[n, c]))
        stores[-1].start()

    for n, ks in enumerate(zip(*orders)):
        offset = jnp.where(core_ref[0] % 2 == 0, *ks)
        fetch(n, offset, span[0], bufs.at[n])
    if own:
        fetch(count, 0, 0, own_buf)
    else:
        lane = lax.broadcasted_iota(jnp.int32, tail.shape, 1)
        ids = jnp.zeros(tail.shape, jnp.int32)
        for m in range(UNIQ):
            ids = jnp.where(lane == m, wanted_ref[m], ids)
        tail[...] = ids.astype(jnp.float32).astype(jnp.bfloat16)
        for n in range(count):
            store(n, chunks, tail, outs[n], chunks * rows)
    for n in range(count):
        fetches[n].wait()
        for c in range(chunks):
            store(n, c, bufs.at[n, :, pl.ds(c * TILE, TILE)], outs[n], c * rows)
    if own:
        fetches[count].wait()
        for c in range(columns // TILE):
            early = c < span[0]
            out = outs[count] if early else outs[count + 1]
            row = (c if early else c - span[0]) * rows
            store(count, c, own_buf.at[:, pl.ds(c * TILE, TILE)], out, row)
    for copy in stores:
        copy.wait()


def column_parts(orders, span, own, wanted, place, core, blocks):
    rows, depth = blocks.shape
    count = len(orders[0])
    columns = depth // (count + 1)
    chunks = span[1] - span[0]
    heights = [chunks * rows + LIST_ROWS * (not own)] * count
    if own:
        heights += [span[0] * rows, chunks * rows]
    return pl.pallas_call(
        functools.partial(split_kernel, orders, span, own),
        in_specs=[SMEM_SPEC] * 3 + [HBM_SPEC],
        out_specs=[HBM_SPEC] * len(heights),
        out_shape=[jax.ShapeDtypeStruct((height, TILE), blocks.dtype) for height in heights],
        scratch_shapes=[
            pltpu.VMEM((count, rows, chunks * TILE), blocks.dtype),
            pltpu.VMEM((rows, columns), blocks.dtype),
            pltpu.VMEM((LIST_ROWS, TILE), blocks.dtype),
            pltpu.SemaphoreType.DMA((count + 1,)),
            pltpu.SemaphoreType.DMA((count + 1, columns // TILE + 1)),
        ],
        compiler_params=pltpu.CompilerParams(vmem_limit_bytes=VMEM_BYTES),
    )(wanted, place, core, blocks)


def block_order(width):
    bits = width.bit_length() - 1
    row = lax.broadcasted_iota(jnp.int32, (TILE, TILE), 0) >> bits
    col = lax.broadcasted_iota(jnp.int32, (TILE, TILE), 1) >> bits
    return row, col


def packed_gram(held, width):
    tile = {}
    for top in range(0, SIDE * TILE, STRIP):
        strip = lax.dot_general(
            held[top : top + STRIP],
            held[top:],
            (((1,), (1,)), ((), ())),
            preferred_element_type=jnp.float32,
        )
        for i in range(top // TILE, (top + STRIP) // TILE):
            for j in range(i, SIDE):
                r, c = i * TILE - top, j * TILE - top
                tile[i, j] = strip[r : r + TILE, c : c + TILE]
    row, col = block_order(width)

    def diagonal(value):
        found = value[:width]
        for r in range(1, TILE // width):
            here = col[:width] == r
            found = jnp.where(here, value[r * width : (r + 1) * width], found)
        return found

    both = [jnp.where(row <= col, tile[i, i], tile[i + 1, i + 1]) for i in (0, 2)]
    first = [tile[0, 1], tile[0, 2], tile[0, 3], tile[1, 2], diagonal(tile[1, 1])]
    second = [tile[1, 3], tile[2, 3], *both, diagonal(tile[3, 3])]
    return first, second


def gather_rows(pool, places, rows, width, chunks):
    return jnp.concatenate(
        [
            jnp.concatenate(
                [
                    pool[pl.ds(pl.multiple_of(place + c * rows, width), width), :]
                    for place in places
                ],
                axis=0,
            )
            for c in range(chunks)
        ],
        axis=1,
    )


def pool_copies(refs, part, pool, sems):
    return [
        pltpu.make_async_copy(ref.at[pl.ds(0, part)], pool.at[pl.ds(k * part, part)], sems.at[k])
        for k, ref in enumerate(refs)
    ]


def early_kernel(ks, owned, width, wanted_ref, place_ref, slot_ref, *rest):
    refs, rest = rest[:-8], rest[-8:]
    acc_ref, spots_ref, pool, lists, ids_vmem, ids, sems, list_sems = rest
    rows = owned * width
    part = refs[0].shape[0]
    chunks = part // rows
    me = place_ref[0]
    tails = [
        pltpu.make_async_copy(ref.at[pl.ds(part, LIST_ROWS)], lists.at[k], list_sems.at[k])
        for k, ref in enumerate(refs[1:], 1)
    ]
    copies = pool_copies(refs, part, pool, sems)
    for copy in tails + copies:
        copy.start()
    for copy in tails:
        copy.wait()
    ids_vmem[...] = jnp.zeros_like(ids_vmem)
    for n, k in enumerate(ks):
        if k > 0:
            ids_vmem[n, :] = lists[slot_ref[k]].astype(jnp.float32).astype(jnp.int32)[0]
    to_scalars = pltpu.make_async_copy(ids_vmem, ids, list_sems.at[0])
    to_scalars.start()
    to_scalars.wait()
    for n, k in enumerate(ks):
        for m in range(UNIQ):
            entry = wanted_ref[m] if k == 0 else ids[n, m]
            holder = lax.div(entry, owned)
            spots_ref[n, m] = slot_ref[holder ^ me] * owned + (entry - holder * owned)
    for copy in copies:
        copy.wait()

    @pl.loop(0, len(ks))
    def _(n):
        places = []
        for m in range(UNIQ):
            where = lax.div(spots_ref[n, m], owned)
            places.append(where * part + (spots_ref[n, m] - where * owned) * width)
        held = gather_rows(pool, places, rows, width, chunks)
        at = 0
        for value in sum(packed_gram(held, width), []):
            acc_ref[n, at : at + value.shape[0], :] = value
            at += value.shape[0]


def late_kernel(owned, width, spots_ref, core_ref, acc_ref, *rest):
    refs, rest = rest[:-4], rest[-4:]
    keep_ref, send_ref, pool, sems = rest
    rows = owned * width
    part = refs[0].shape[0]
    chunks = part // rows
    owners = acc_ref.shape[0]
    half = acc_ref.shape[1] // 2
    core = core_ref[0]
    copies = pool_copies(refs, part, pool, sems)
    for copy in copies:
        copy.start()
    for copy in copies:
        copy.wait()
    for n in range(owners):
        places = []
        for m in range(UNIQ):
            where = lax.div(spots_ref[n, m], owned)
            places.append(where * part + (spots_ref[n, m] - where * owned) * width)
        halves = packed_gram(gather_rows(pool, places, rows, width, chunks), width)
        at = 0
        for first, second in zip(*halves):
            height = first.shape[0]
            first += acc_ref[n, at : at + height, :]
            second += acc_ref[n, half + at : half + at + height, :]
            keep = jnp.where(core == 0, first, second)
            send = jnp.where(core == 0, second, first)
            keep_ref[n, at : at + height, :] = keep.astype(jnp.bfloat16)
            send_ref[n, at : at + height, :] = send.astype(jnp.bfloat16)
            at += height


def half_rows(width):
    return SIDE * TILE + width


def early_grams(ks, owned, width, wanted, place, slot, parts):
    holders = len(parts)
    rows = owned * width
    chunks = parts[0].shape[0] // rows
    return pl.pallas_call(
        functools.partial(early_kernel, ks, owned, width),
        in_specs=[SMEM_SPEC] * 3 + [HBM_SPEC] * holders,
        out_specs=[VMEM_SPEC, SMEM_SPEC],
        out_shape=[
            jax.ShapeDtypeStruct((len(ks), 2 * half_rows(width), TILE), jnp.float32),
            jax.ShapeDtypeStruct((len(ks), UNIQ), jnp.int32),
        ],
        scratch_shapes=[
            pltpu.VMEM((holders * rows * chunks, TILE), jnp.bfloat16),
            pltpu.VMEM((holders, LIST_ROWS, TILE), jnp.bfloat16),
            pltpu.VMEM((len(ks), TILE), jnp.int32),
            pltpu.SMEM((len(ks), TILE), jnp.int32),
            pltpu.SemaphoreType.DMA((holders,)),
            pltpu.SemaphoreType.DMA((holders,)),
        ],
        compiler_params=pltpu.CompilerParams(vmem_limit_bytes=24 * 1024 * 1024),
        cost_estimate=pl.CostEstimate(
            flops=2 * len(ks) * (SIDE * TILE) ** 2 * chunks * TILE,
            bytes_accessed=2 * holders * rows * chunks * TILE,
            transcendentals=0,
        ),
    )(wanted, place, slot, *parts)


def late_grams(owned, width, spots, core, acc, parts):
    holders = len(parts)
    rows = owned * width
    chunks = parts[0].shape[0] // rows
    half = half_rows(width)
    out = jax.ShapeDtypeStruct((acc.shape[0], half, TILE), jnp.bfloat16)
    owners = acc.shape[0]
    return pl.pallas_call(
        functools.partial(late_kernel, owned, width),
        in_specs=[SMEM_SPEC] * 2 + [VMEM_SPEC] + [HBM_SPEC] * holders,
        out_specs=[VMEM_SPEC] * 2,
        out_shape=[out, out],
        scratch_shapes=[
            pltpu.VMEM((holders * rows * chunks, TILE), jnp.bfloat16),
            pltpu.SemaphoreType.DMA((holders,)),
        ],
        compiler_params=pltpu.CompilerParams(vmem_limit_bytes=16 * 1024 * 1024),
        cost_estimate=pl.CostEstimate(
            flops=2 * owners * (SIDE * TILE) ** 2 * chunks * TILE,
            bytes_accessed=2 * holders * rows * chunks * TILE,
            transcendentals=0,
        ),
    )(spots, core, acc, *parts)


def finish_kernel(slots_ref, core_ref, mine_ref, other_ref, choose_ref, terms_ref, out_ref, gram, stage, sems):
    core = core_ref[0]
    width = gram.shape[0] // UNIQ
    pairs = out_ref.shape[0]

    def put(i, j, value):
        gram[i * TILE : (i + 1) * TILE, j * TILE : (j + 1) * TILE] = value.astype(jnp.bfloat16)

    mine, other = mine_ref[...], other_ref[...]
    first = jnp.where(core == 0, mine, other).astype(jnp.float32)
    second = jnp.where(core == 0, other, mine).astype(jnp.float32)
    pieces = [v[t * TILE : (t + 1) * TILE] for v in (first, second) for t in range(SIDE)]
    places = [(0, 1), (0, 2), (0, 3), (1, 2), (1, 3), (2, 3)]
    for (i, j), value in zip(places, pieces):
        put(i, j, value)
        put(j, i, value.T)
    row, col = block_order(width)
    for i, value, diagonal in zip((0, 2), pieces[6:], (first, second)):
        flipped = value.T
        squares = jnp.concatenate([diagonal[SIDE * TILE :]] * (TILE // width), axis=0)
        put(i, i, jnp.where(row <= col, value, flipped))
        lower = jnp.where(row > col, value, flipped)
        put(i + 1, i + 1, jnp.where(row == col, squares, lower))

    def result(pair):
        return pltpu.make_async_copy(stage.at[pair], out_ref.at[pair], sems.at[pair])

    for pair in range(pairs):
        left = jnp.concatenate(
            [gram[pl.ds(slots_ref[pair, m] * width, width), :] for m in range(DOM)], axis=0
        )
        integrals = jnp.dot(left, choose_ref[pair], preferred_element_type=jnp.float32)
        stage[pair] = (integrals + terms_ref[pair]).astype(jnp.bfloat16)
        result(pair).start()
    for pair in range(pairs):
        result(pair).wait()


def finish(slots, core, mine, other, choose, terms):
    pairs, rows, cols = terms.shape
    gram_side = UNIQ * rows // DOM
    return pl.pallas_call(
        finish_kernel,
        in_specs=[SMEM_SPEC] * 2 + [VMEM_SPEC] * 4,
        out_specs=HBM_SPEC,
        out_shape=jax.ShapeDtypeStruct(terms.shape, jnp.bfloat16),
        scratch_shapes=[
            pltpu.VMEM((gram_side, gram_side), jnp.bfloat16),
            pltpu.VMEM(terms.shape, jnp.bfloat16),
            pltpu.SemaphoreType.DMA((pairs,)),
        ],
        compiler_params=pltpu.CompilerParams(vmem_limit_bytes=LAST_VMEM),
        cost_estimate=pl.CostEstimate(
            flops=2 * pairs * rows * cols * gram_side,
            bytes_accessed=10 * pairs * rows * cols,
            transcendentals=0,
        ),
    )(slots, core, mine, other, choose, terms)


def swap(value, axis, bit):
    size = lax.axis_size(axis)
    return lax.ppermute(value, axis, [(i, i ^ bit) for i in range(size)])


def add(*values):
    return sum(value.astype(jnp.float32) for value in values)


def to_owner(keep, came):
    half = keep.shape[0] // 2
    keep, came = (v.reshape(2, half, *v.shape[1:]) for v in (keep, came))

    def both(bits, offsets, rows):
        return add(keep[bits, offsets, rows], came[bits, offsets, rows]).astype(jnp.bfloat16)

    every, top, rest = slice(None), slice(0, FIRST), slice(FIRST, None)
    far_first = range(half - 1, 0, -1)
    rest_far = [swap(both(every, j, rest), "pairs", 2 * j) for j in far_first]
    top_near = swap(both(1, every, top), "pairs", 1)
    top_sums = [
        add(keep[0, j, top], came[0, j, top], top_near[j]).astype(jnp.bfloat16)
        for j in range(half)
    ]
    top_far = [swap(top_sums[j], "pairs", 2 * j) for j in far_first]
    rest_sums = [
        add(keep[b, 0, rest], came[b, 0, rest], *(v[b] for v in rest_far)).astype(jnp.bfloat16)
        for b in range(2)
    ]
    rest_near = swap(rest_sums[1], "pairs", 1)
    top_total = add(top_sums[0], *top_far).astype(jnp.bfloat16)
    rest_total = add(rest_sums[0], rest_near).astype(jnp.bfloat16)
    return jnp.concatenate([top_total, rest_total], axis=0)


def exchange_orders(holders):
    light, heavy = [*range(1, holders // 2)], [*range(holders // 2, holders)]
    first = heavy[:1]
    for pair in zip(heavy[1:], light):
        first += pair
    second = [k for pair in zip(light, heavy) for k in pair] + heavy[-1:]
    return [first, second]


def split_by_columns(blocks, wanted, pair_slots, fock, correlation, amplitudes):
    holders = lax.axis_size("pairs")
    core = lax.axis_index("aux")
    owned, width, depth = blocks.shape
    stacked = blocks.reshape(owned * width, depth)
    place = lax.axis_index("pairs").reshape(1).astype(jnp.int32)
    core_id = core.reshape(1).astype(jnp.int32)
    orders = exchange_orders(holders)
    slot_tables = [[0] * holders for _ in orders]
    for table, ks in zip(slot_tables, orders):
        for n, k in enumerate(ks, 1):
            table[k] = n
    slot = jnp.asarray(slot_tables, jnp.int32)[core % 2]
    chunks = depth // holders // TILE
    cores = lax.axis_size("aux")

    def exchange(parts):
        arrived = []
        for n, part in enumerate(parts):
            moves = [
                (p * cores + c, (p ^ orders[c % 2][n]) * cores + c)
                for p in range(holders)
                for c in range(cores)
            ]
            arrived.append(lax.ppermute(part, ("pairs", "aux"), moves))
        return arrived

    cut = max(1, chunks - LATE)
    first, second = (0, cut), (cut, chunks)
    early = exchange(column_parts(orders, first, False, wanted, place, core_id, stacked))
    tied = 5
    early[tied], later = lax.optimization_barrier((early[tied], stacked))
    *late, own_early, own_late = column_parts(orders, second, True, wanted, place, core_id, later)
    late = exchange(late)
    pairs_here = fock.shape[0]
    slots = lax.dynamic_slice_in_dim(pair_slots, core * pairs_here, pairs_here, axis=0)
    offsets = jnp.arange(width, dtype=jnp.int32)
    right_rows = (slots[:, DOM:, None] * width + offsets).reshape(pairs_here, 1, DOM * width)
    terms, choose = pair_terms(right_rows, fock, correlation, amplitudes)
    early, terms, choose, slots = lax.optimization_barrier((early, terms, choose, slots))
    order = (*range(0, holders, 2), *range(1, holders, 2))
    acc, spots = early_grams(order, owned, width, wanted, place, slot, [own_early, *early])
    keep, send = late_grams(owned, width, spots, core_id, acc, [own_late, *late])
    mine = to_owner(keep, swap(send, "aux", 1))
    other = swap(mine, "aux", 1)
    return finish(slots, core_id, mine, other, choose, terms)


def pick_tiles(gram, left_ids, right_ids):
    count = left_ids.shape[0]
    sides = left_ids.shape[1]
    width = gram.shape[2]
    tiles = gram[left_ids[:, :, None], right_ids[:, None, :]]
    return tiles.transpose(0, 1, 3, 2, 4).reshape(count, sides * width, sides * width)


def pair_integrals(held, left_ids, right_ids):
    units, width, depth = held.shape
    stacked = held.reshape(units * width, depth)
    gram = lax.dot_general(
        stacked, stacked, (((1,), (1,)), ((), ())), preferred_element_type=jnp.float32
    )
    gram = gram.reshape(units, width, units, width).transpose(0, 2, 1, 3)
    return pick_tiles(gram, left_ids, right_ids)


def by_request(blocks, wanted, pair_slots, fock, correlation, amplitudes):
    holders = lax.axis_size("pairs")
    owned, width, depth = blocks.shape
    capacity = max(2, (2 * UNIQ + holders - 1) // holders)
    holder = wanted // owned
    local_ids = wanted - holder * owned
    order_ids = jnp.arange(wanted.shape[0])
    earlier = (holder[None, :] == holder[:, None]) & (order_ids[None, :] < order_ids[:, None])
    rank = jnp.sum(earlier.astype(jnp.int32), axis=1)
    slot = holder * capacity + rank
    places = jnp.arange(holders * capacity)
    table = jnp.sum(jnp.where(places[:, None] == slot[None, :], local_ids[None, :], 0), axis=1)
    table = table.reshape(holders, capacity)
    asked = lax.all_to_all(table, "pairs", split_axis=0, concat_axis=0, tiled=True)
    outgoing = jnp.take(blocks, asked.reshape(-1), axis=0).reshape(holders, capacity, width, depth)
    arrived = lax.all_to_all(outgoing, "pairs", split_axis=0, concat_axis=0, tiled=True)
    held = jnp.take(arrived.reshape(holders * capacity, width, depth), slot, axis=0)
    partial_value = pair_integrals(held, pair_slots[:, :DOM], pair_slots[:, DOM:])
    integrals = lax.psum_scatter(
        partial_value.astype(jnp.bfloat16), "aux", scatter_dimension=0, tiled=True
    ).astype(jnp.float32)
    products = functools.partial(
        jnp.einsum, "pab,pbc->pac", preferred_element_type=jnp.float32
    )
    fock_amp = products(fock, amplitudes).astype(jnp.bfloat16)
    over_amp = products(correlation, amplitudes).astype(jnp.bfloat16)
    terms = products(fock_amp, correlation) + products(over_amp, fock)
    return (integrals + terms).astype(jnp.bfloat16)


def on_device(blocks, *others):
    holders = lax.axis_size("pairs")
    owned, width, depth = blocks.shape
    fits = holders > 1 and holders & (holders - 1) == 0 and width & (width - 1) == 0
    fits = fits and depth % (TILE * holders) == 0 and depth // holders >= 2 * TILE
    fits = fits and holders * owned <= 256 and UNIQ * width == SIDE * TILE
    return (split_by_columns if fits else by_request)(blocks, *others)


def solution(mesh):
    return jax.shard_map(
        on_device,
        mesh=mesh,
        in_specs=(
            P(("groups", "pairs"), None, "aux"),
            P(("groups", "pairs")),
            P(("groups", "pairs"), None),
            P(("groups", "pairs", "aux"), None, None),
            P(("groups", "pairs", "aux"), None, None),
            P(("groups", "pairs", "aux"), None, None),
        ),
        out_specs=P(("groups", "pairs", "aux"), None, None),
        check_vma=False,
    )
```

```python
import functools

import jax
import jax.numpy as jnp
from jax import lax
from jax.experimental import pallas as pl
from jax.experimental.pallas import tpu as pltpu
from jax.sharding import PartitionSpec as P

DOM = 8
UNIQ = 16
TILE = 128
SIDE = 4
LATE = 2

STRIP = 256
LIST_ROWS = 16
VMEM_BYTES = 60 * 1024 * 1024
LAST_VMEM = 24 * 1024 * 1024
FIRST = 384
SMEM_SPEC = pl.BlockSpec(memory_space=pltpu.SMEM)
VMEM_SPEC = pl.BlockSpec(memory_space=pltpu.VMEM)
HBM_SPEC = pl.BlockSpec(memory_space=pltpu.HBM)


def terms_kernel(right_ref, fock_ref, corr_ref, amp_ref, out_ref, choose_ref):
    fock, corr, amp = fock_ref[0], corr_ref[0], amp_ref[0]
    fock_amp = jnp.dot(fock, amp, preferred_element_type=jnp.float32).astype(jnp.bfloat16)
    over_amp = jnp.dot(corr, amp, preferred_element_type=jnp.float32).astype(jnp.bfloat16)
    first = jnp.dot(fock_amp, corr, preferred_element_type=jnp.float32)
    out_ref[0] = first + jnp.dot(over_amp, fock, preferred_element_type=jnp.float32)
    rows = lax.broadcasted_iota(jnp.int32, choose_ref.shape[1:], 0)
    choose_ref[0] = (rows == right_ref[0]).astype(jnp.float32).astype(jnp.bfloat16)


def pair_terms(right_rows, fock, correlation, amplitudes):
    pairs, rows, cols = fock.shape
    spec = pl.BlockSpec((1, rows, cols), lambda p: (p, 0, 0))
    side = UNIQ * rows // DOM
    return pl.pallas_call(
        terms_kernel,
        grid=(pairs,),
        in_specs=[pl.BlockSpec((1, 1, cols), lambda p: (p, 0, 0))] + [spec] * 3,
        out_specs=[spec, pl.BlockSpec((1, side, cols), lambda p: (p, 0, 0))],
        out_shape=[
            jax.ShapeDtypeStruct(fock.shape, jnp.float32),
            jax.ShapeDtypeStruct((pairs, side, cols), jnp.bfloat16),
        ],
        compiler_params=pltpu.CompilerParams(vmem_limit_bytes=VMEM_BYTES),
        cost_estimate=pl.CostEstimate(
            flops=8 * pairs * rows * rows * cols,
            bytes_accessed=14 * pairs * rows * cols,
            transcendentals=0,
        ),
    )(right_rows, fock, correlation, amplitudes)


def split_kernel(orders, span, own, wanted_ref, place_ref, core_ref, blocks_ref, *rest):
    outs, (bufs, own_buf, tail, in_sems, out_sems) = rest[:-5], rest[-5:]
    rows, depth = blocks_ref.shape
    columns = own_buf.shape[1]
    chunks = span[1] - span[0]
    count = len(orders[0])
    fetches, stores = [], []

    def fetch(n, offset, first, buf):
        start = pl.multiple_of((place_ref[0] ^ offset) * columns + first * TILE, TILE)
        source = blocks_ref.at[:, pl.ds(start, buf.shape[1])]
        fetches.append(pltpu.make_async_copy(source, buf, in_sems.at[n]))
        fetches[-1].start()

    def store(n, c, source, out, row):
        target = out.at[pl.ds(row, source.shape[0])]
        stores.append(pltpu.make_async_copy(source, target, out_sems.at[n, c]))
        stores[-1].start()

    for n, ks in enumerate(zip(*orders)):
        offset = jnp.where(core_ref[0] % 2 == 0, *ks)
        fetch(n, offset, span[0], bufs.at[n])
    if own:
        fetch(count, 0, 0, own_buf)
    else:
        lane = lax.broadcasted_iota(jnp.int32, tail.shape, 1)
        ids = jnp.zeros(tail.shape, jnp.int32)
        for m in range(UNIQ):
            ids = jnp.where(lane == m, wanted_ref[m], ids)
        tail[...] = ids.astype(jnp.float32).astype(jnp.bfloat16)
        for n in range(count):
            store(n, chunks, tail, outs[n], chunks * rows)
    for n in range(count):
        fetches[n].wait()
        for c in range(chunks):
            store(n, c, bufs.at[n, :, pl.ds(c * TILE, TILE)], outs[n], c * rows)
    if own:
        fetches[count].wait()
        for c in range(columns // TILE):
            early = c < span[0]
            out = outs[count] if early else outs[count + 1]
            row = (c if early else c - span[0]) * rows
            store(count, c, own_buf.at[:, pl.ds(c * TILE, TILE)], out, row)
    for copy in stores:
        copy.wait()


def column_parts(orders, span, own, wanted, place, core, blocks):
    rows, depth = blocks.shape
    count = len(orders[0])
    columns = depth // (count + 1)
    chunks = span[1] - span[0]
    heights = [chunks * rows + LIST_ROWS * (not own)] * count
    if own:
        heights += [span[0] * rows, chunks * rows]
    return pl.pallas_call(
        functools.partial(split_kernel, orders, span, own),
        in_specs=[SMEM_SPEC] * 3 + [HBM_SPEC],
        out_specs=[HBM_SPEC] * len(heights),
        out_shape=[jax.ShapeDtypeStruct((height, TILE), blocks.dtype) for height in heights],
        scratch_shapes=[
            pltpu.VMEM((count, rows, chunks * TILE), blocks.dtype),
            pltpu.VMEM((rows, columns), blocks.dtype),
            pltpu.VMEM((LIST_ROWS, TILE), blocks.dtype),
            pltpu.SemaphoreType.DMA((count + 1,)),
            pltpu.SemaphoreType.DMA((count + 1, columns // TILE + 1)),
        ],
        compiler_params=pltpu.CompilerParams(vmem_limit_bytes=VMEM_BYTES),
    )(wanted, place, core, blocks)


def block_order(width):
    bits = width.bit_length() - 1
    row = lax.broadcasted_iota(jnp.int32, (TILE, TILE), 0) >> bits
    col = lax.broadcasted_iota(jnp.int32, (TILE, TILE), 1) >> bits
    return row, col


def packed_gram(held, width):
    tile = {}
    for top in range(0, SIDE * TILE, STRIP):
        strip = lax.dot_general(
            held[top : top + STRIP],
            held[top:],
            (((1,), (1,)), ((), ())),
            preferred_element_type=jnp.float32,
        )
        for i in range(top // TILE, (top + STRIP) // TILE):
            for j in range(i, SIDE):
                r, c = i * TILE - top, j * TILE - top
                tile[i, j] = strip[r : r + TILE, c : c + TILE]
    row, col = block_order(width)

    def diagonal(value):
        found = value[:width]
        for r in range(1, TILE // width):
            here = col[:width] == r
            found = jnp.where(here, value[r * width : (r + 1) * width], found)
        return found

    both = [jnp.where(row <= col, tile[i, i], tile[i + 1, i + 1]) for i in (0, 2)]
    first = [tile[0, 1], tile[0, 2], tile[0, 3], tile[1, 2], diagonal(tile[1, 1])]
    second = [tile[1, 3], tile[2, 3], *both, diagonal(tile[3, 3])]
    return first, second


def gather_rows(pool, places, rows, width, chunks):
    return jnp.concatenate(
        [
            jnp.concatenate(
                [
                    pool[pl.ds(pl.multiple_of(place + c * rows, width), width), :]
                    for place in places
                ],
                axis=0,
            )
            for c in range(chunks)
        ],
        axis=1,
    )


def pool_copies(refs, slots, part, pool, sems):
    return [
        pltpu.make_async_copy(
            ref.at[pl.ds(0, part)],
            pool.at[pl.ds(pl.multiple_of(slot * part, part), part)],
            sems.at[k],
        )
        for k, (ref, slot) in enumerate(zip(refs, slots))
    ]


def early_kernel(ks, owned, width, wanted_ref, place_ref, slot_ref, *rest):
    refs, rest = rest[:-8], rest[-8:]
    acc_ref, spots_ref, pool, lists, ids_vmem, ids, sems, list_sems = rest
    rows = owned * width
    part = refs[0].shape[0]
    chunks = part // rows
    me = place_ref[0]
    tails = [
        pltpu.make_async_copy(ref.at[pl.ds(part, LIST_ROWS)], lists.at[k], list_sems.at[k])
        for k, ref in enumerate(refs[1:], 1)
    ]
    copies = pool_copies(refs, range(len(refs)), part, pool, sems)
    for copy in tails + copies:
        copy.start()
    for copy in tails:
        copy.wait()
    ids_vmem[...] = jnp.zeros_like(ids_vmem)
    for n, k in enumerate(ks):
        if k > 0:
            ids_vmem[n, :] = lists[slot_ref[k]].astype(jnp.float32).astype(jnp.int32)[0]
    to_scalars = pltpu.make_async_copy(ids_vmem, ids, list_sems.at[0])
    to_scalars.start()
    to_scalars.wait()
    for n, k in enumerate(ks):
        for m in range(UNIQ):
            entry = wanted_ref[m] if k == 0 else ids[n, m]
            holder = lax.div(entry, owned)
            spots_ref[n, m] = slot_ref[holder ^ me] * owned + (entry - holder * owned)
    for copy in copies:
        copy.wait()

    @pl.loop(0, len(ks))
    def _(n):
        places = []
        for m in range(UNIQ):
            where = lax.div(spots_ref[n, m], owned)
            places.append(where * part + (spots_ref[n, m] - where * owned) * width)
        held = gather_rows(pool, places, rows, width, chunks)
        at = 0
        for value in sum(packed_gram(held, width), []):
            acc_ref[n, at : at + value.shape[0], :] = value
            at += value.shape[0]


def late_kernel(slots, owned, width, spots_ref, core_ref, acc_ref, *rest):
    refs, rest = rest[:-4], rest[-4:]
    keep_ref, send_ref, pool, sems = rest
    rows = owned * width
    part = refs[0].shape[0]
    chunks = part // rows
    owners = acc_ref.shape[0]
    half = acc_ref.shape[1] // 2
    core = core_ref[0]
    targets = [jnp.where(core % 2 == 0, *pair) for pair in zip(*slots)]
    copies = pool_copies(refs, targets, part, pool, sems)
    for copy in copies:
        copy.start()
    for copy in copies:
        copy.wait()
    for n in range(owners):
        places = []
        for m in range(UNIQ):
            where = lax.div(spots_ref[n, m], owned)
            places.append(where * part + (spots_ref[n, m] - where * owned) * width)
        halves = packed_gram(gather_rows(pool, places, rows, width, chunks), width)
        at = 0
        for first, second in zip(*halves):
            height = first.shape[0]
            first += acc_ref[n, at : at + height, :]
            second += acc_ref[n, half + at : half + at + height, :]
            keep = jnp.where(core == 0, first, second)
            send = jnp.where(core == 0, second, first)
            keep_ref[n, at : at + height, :] = keep.astype(jnp.bfloat16)
            send_ref[n, at : at + height, :] = send.astype(jnp.bfloat16)
            at += height


def half_rows(width):
    return SIDE * TILE + width


def early_grams(ks, owned, width, wanted, place, slot, parts):
    holders = len(parts)
    rows = owned * width
    chunks = parts[0].shape[0] // rows
    return pl.pallas_call(
        functools.partial(early_kernel, ks, owned, width),
        in_specs=[SMEM_SPEC] * 3 + [HBM_SPEC] * holders,
        out_specs=[VMEM_SPEC, SMEM_SPEC],
        out_shape=[
            jax.ShapeDtypeStruct((len(ks), 2 * half_rows(width), TILE), jnp.float32),
            jax.ShapeDtypeStruct((len(ks), UNIQ), jnp.int32),
        ],
        scratch_shapes=[
            pltpu.VMEM((holders * rows * chunks, TILE), jnp.bfloat16),
            pltpu.VMEM((holders, LIST_ROWS, TILE), jnp.bfloat16),
            pltpu.VMEM((len(ks), TILE), jnp.int32),
            pltpu.SMEM((len(ks), TILE), jnp.int32),
            pltpu.SemaphoreType.DMA((holders,)),
            pltpu.SemaphoreType.DMA((holders,)),
        ],
        compiler_params=pltpu.CompilerParams(vmem_limit_bytes=24 * 1024 * 1024),
        cost_estimate=pl.CostEstimate(
            flops=2 * len(ks) * (SIDE * TILE) ** 2 * chunks * TILE,
            bytes_accessed=2 * holders * rows * chunks * TILE,
            transcendentals=0,
        ),
    )(wanted, place, slot, *parts)


def late_grams(slots, owned, width, spots, core, acc, parts):
    holders = len(parts)
    rows = owned * width
    chunks = parts[0].shape[0] // rows
    half = half_rows(width)
    out = jax.ShapeDtypeStruct((acc.shape[0], half, TILE), jnp.bfloat16)
    owners = acc.shape[0]
    return pl.pallas_call(
        functools.partial(late_kernel, slots, owned, width),
        in_specs=[SMEM_SPEC] * 2 + [VMEM_SPEC] + [HBM_SPEC] * holders,
        out_specs=[VMEM_SPEC] * 2,
        out_shape=[out, out],
        scratch_shapes=[
            pltpu.VMEM((holders * rows * chunks, TILE), jnp.bfloat16),
            pltpu.SemaphoreType.DMA((holders,)),
        ],
        compiler_params=pltpu.CompilerParams(vmem_limit_bytes=16 * 1024 * 1024),
        cost_estimate=pl.CostEstimate(
            flops=2 * owners * (SIDE * TILE) ** 2 * chunks * TILE,
            bytes_accessed=2 * holders * rows * chunks * TILE,
            transcendentals=0,
        ),
    )(spots, core, acc, *parts)


def finish_kernel(slots_ref, core_ref, mine_ref, other_ref, choose_ref, terms_ref, out_ref, gram, stage, sems):
    core = core_ref[0]
    width = gram.shape[0] // UNIQ
    pairs = out_ref.shape[0]

    def put(i, j, value):
        gram[i * TILE : (i + 1) * TILE, j * TILE : (j + 1) * TILE] = value.astype(jnp.bfloat16)

    mine, other = mine_ref[...], other_ref[...]
    first = jnp.where(core == 0, mine, other).astype(jnp.float32)
    second = jnp.where(core == 0, other, mine).astype(jnp.float32)
    pieces = [v[t * TILE : (t + 1) * TILE] for v in (first, second) for t in range(SIDE)]
    places = [(0, 1), (0, 2), (0, 3), (1, 2), (1, 3), (2, 3)]
    for (i, j), value in zip(places, pieces):
        put(i, j, value)
        put(j, i, value.T)
    row, col = block_order(width)
    for i, value, diagonal in zip((0, 2), pieces[6:], (first, second)):
        flipped = value.T
        squares = jnp.concatenate([diagonal[SIDE * TILE :]] * (TILE // width), axis=0)
        put(i, i, jnp.where(row <= col, value, flipped))
        lower = jnp.where(row > col, value, flipped)
        put(i + 1, i + 1, jnp.where(row == col, squares, lower))

    def result(pair):
        return pltpu.make_async_copy(stage.at[pair], out_ref.at[pair], sems.at[pair])

    for pair in range(pairs):
        left = jnp.concatenate(
            [gram[pl.ds(slots_ref[pair, m] * width, width), :] for m in range(DOM)], axis=0
        )
        integrals = jnp.dot(left, choose_ref[pair], preferred_element_type=jnp.float32)
        stage[pair] = (integrals + terms_ref[pair]).astype(jnp.bfloat16)
        result(pair).start()
    for pair in range(pairs):
        result(pair).wait()


def finish(slots, core, mine, other, choose, terms):
    pairs, rows, cols = terms.shape
    gram_side = UNIQ * rows // DOM
    return pl.pallas_call(
        finish_kernel,
        in_specs=[SMEM_SPEC] * 2 + [VMEM_SPEC] * 4,
        out_specs=HBM_SPEC,
        out_shape=jax.ShapeDtypeStruct(terms.shape, jnp.bfloat16),
        scratch_shapes=[
            pltpu.VMEM((gram_side, gram_side), jnp.bfloat16),
            pltpu.VMEM(terms.shape, jnp.bfloat16),
            pltpu.SemaphoreType.DMA((pairs,)),
        ],
        compiler_params=pltpu.CompilerParams(vmem_limit_bytes=LAST_VMEM),
        cost_estimate=pl.CostEstimate(
            flops=2 * pairs * rows * cols * gram_side,
            bytes_accessed=10 * pairs * rows * cols,
            transcendentals=0,
        ),
    )(slots, core, mine, other, choose, terms)


def swap(value, axis, bit):
    size = lax.axis_size(axis)
    return lax.ppermute(value, axis, [(i, i ^ bit) for i in range(size)])


def add(*values):
    return sum(value.astype(jnp.float32) for value in values)


def to_owner(keep, came):
    half = keep.shape[0] // 2
    keep, came = (v.reshape(2, half, *v.shape[1:]) for v in (keep, came))

    def both(bits, offsets, rows):
        return add(keep[bits, offsets, rows], came[bits, offsets, rows]).astype(jnp.bfloat16)

    every, top, rest = slice(None), slice(0, FIRST), slice(FIRST, None)
    far_first = range(half - 1, 0, -1)
    rest_far = [swap(both(every, j, rest), "pairs", 2 * j) for j in far_first]
    top_near = swap(both(1, every, top), "pairs", 1)
    top_sums = [
        add(keep[0, j, top], came[0, j, top], top_near[j]).astype(jnp.bfloat16)
        for j in range(half)
    ]
    top_far = [swap(top_sums[j], "pairs", 2 * j) for j in far_first]
    rest_sums = [
        add(keep[b, 0, rest], came[b, 0, rest], *(v[b] for v in rest_far)).astype(jnp.bfloat16)
        for b in range(2)
    ]
    rest_near = swap(rest_sums[1], "pairs", 1)
    top_total = add(top_sums[0], *top_far).astype(jnp.bfloat16)
    rest_total = add(rest_sums[0], rest_near).astype(jnp.bfloat16)
    return jnp.concatenate([top_total, rest_total], axis=0)


def exchange_orders(holders):
    light, heavy = [*range(1, holders // 2)], [*range(holders // 2, holders)]
    first = heavy[:1]
    for pair in zip(heavy[1:], light):
        first += pair
    second = [k for pair in zip(light, heavy) for k in pair] + heavy[-1:]
    return [first, second]


def split_by_columns(blocks, wanted, pair_slots, fock, correlation, amplitudes):
    holders = lax.axis_size("pairs")
    core = lax.axis_index("aux")
    owned, width, depth = blocks.shape
    stacked = blocks.reshape(owned * width, depth)
    place = lax.axis_index("pairs").reshape(1).astype(jnp.int32)
    core_id = core.reshape(1).astype(jnp.int32)
    orders = exchange_orders(holders)
    slot_tables = [[0] * holders for _ in orders]
    for table, ks in zip(slot_tables, orders):
        for n, k in enumerate(ks, 1):
            table[k] = n
    slot = jnp.asarray(slot_tables, jnp.int32)[core % 2]
    chunks = depth // holders // TILE
    cores = lax.axis_size("aux")

    def exchange(parts, orders):
        arrived = []
        for n, part in enumerate(parts):
            moves = [
                (p * cores + c, (p ^ orders[c % 2][n]) * cores + c)
                for p in range(holders)
                for c in range(cores)
            ]
            arrived.append(lax.ppermute(part, ("pairs", "aux"), moves))
        return arrived

    cut = max(1, chunks - LATE)
    first, second = (0, cut), (cut, chunks)
    early = exchange(column_parts(orders, first, False, wanted, place, core_id, stacked), orders)
    tied = 5
    early[tied], later = lax.optimization_barrier((early[tied], stacked))
    late_orders = orders[::-1]
    late_slots = [[0] + [t[k] for k in ks] for t, ks in zip(slot_tables, late_orders)]
    *late, own_early, own_late = column_parts(late_orders, second, True, wanted, place, core_id, later)
    late = exchange(late, late_orders)
    pairs_here = fock.shape[0]
    slots = lax.dynamic_slice_in_dim(pair_slots, core * pairs_here, pairs_here, axis=0)
    offsets = jnp.arange(width, dtype=jnp.int32)
    right_rows = (slots[:, DOM:, None] * width + offsets).reshape(pairs_here, 1, DOM * width)
    terms, choose = pair_terms(right_rows, fock, correlation, amplitudes)
    early, terms, choose, slots = lax.optimization_barrier((early, terms, choose, slots))
    order = (*range(0, holders, 2), *range(1, holders, 2))
    acc, spots = early_grams(order, owned, width, wanted, place, slot, [own_early, *early])
    keep, send = late_grams(late_slots, owned, width, spots, core_id, acc, [own_late, *late])
    mine = to_owner(keep, swap(send, "aux", 1))
    other = swap(mine, "aux", 1)
    return finish(slots, core_id, mine, other, choose, terms)


def pick_tiles(gram, left_ids, right_ids):
    count = left_ids.shape[0]
    sides = left_ids.shape[1]
    width = gram.shape[2]
    tiles = gram[left_ids[:, :, None], right_ids[:, None, :]]
    return tiles.transpose(0, 1, 3, 2, 4).reshape(count, sides * width, sides * width)


def pair_integrals(held, left_ids, right_ids):
    units, width, depth = held.shape
    stacked = held.reshape(units * width, depth)
    gram = lax.dot_general(
        stacked, stacked, (((1,), (1,)), ((), ())), preferred_element_type=jnp.float32
    )
    gram = gram.reshape(units, width, units, width).transpose(0, 2, 1, 3)
    return pick_tiles(gram, left_ids, right_ids)


def by_request(blocks, wanted, pair_slots, fock, correlation, amplitudes):
    holders = lax.axis_size("pairs")
    owned, width, depth = blocks.shape
    capacity = max(2, (2 * UNIQ + holders - 1) // holders)
    holder = wanted // owned
    local_ids = wanted - holder * owned
    order_ids = jnp.arange(wanted.shape[0])
    earlier = (holder[None, :] == holder[:, None]) & (order_ids[None, :] < order_ids[:, None])
    rank = jnp.sum(earlier.astype(jnp.int32), axis=1)
    slot = holder * capacity + rank
    places = jnp.arange(holders * capacity)
    table = jnp.sum(jnp.where(places[:, None] == slot[None, :], local_ids[None, :], 0), axis=1)
    table = table.reshape(holders, capacity)
    asked = lax.all_to_all(table, "pairs", split_axis=0, concat_axis=0, tiled=True)
    outgoing = jnp.take(blocks, asked.reshape(-1), axis=0).reshape(holders, capacity, width, depth)
    arrived = lax.all_to_all(outgoing, "pairs", split_axis=0, concat_axis=0, tiled=True)
    held = jnp.take(arrived.reshape(holders * capacity, width, depth), slot, axis=0)
    partial_value = pair_integrals(held, pair_slots[:, :DOM], pair_slots[:, DOM:])
    integrals = lax.psum_scatter(
        partial_value.astype(jnp.bfloat16), "aux", scatter_dimension=0, tiled=True
    ).astype(jnp.float32)
    products = functools.partial(
        jnp.einsum, "pab,pbc->pac", preferred_element_type=jnp.float32
    )
    fock_amp = products(fock, amplitudes).astype(jnp.bfloat16)
    over_amp = products(correlation, amplitudes).astype(jnp.bfloat16)
    terms = products(fock_amp, correlation) + products(over_amp, fock)
    return (integrals + terms).astype(jnp.bfloat16)


def on_device(blocks, *others):
    holders = lax.axis_size("pairs")
    owned, width, depth = blocks.shape
    fits = holders > 1 and holders & (holders - 1) == 0 and width & (width - 1) == 0
    fits = fits and depth % (TILE * holders) == 0 and depth // holders >= 2 * TILE
    fits = fits and holders * owned <= 256 and UNIQ * width == SIDE * TILE
    return (split_by_columns if fits else by_request)(blocks, *others)


def solution(mesh):
    return jax.shard_map(
        on_device,
        mesh=mesh,
        in_specs=(
            P(("groups", "pairs"), None, "aux"),
            P(("groups", "pairs")),
            P(("groups", "pairs"), None),
            P(("groups", "pairs", "aux"), None, None),
            P(("groups", "pairs", "aux"), None, None),
            P(("groups", "pairs", "aux"), None, None),
        ),
        out_specs=P(("groups", "pairs", "aux"), None, None),
        check_vma=False,
    )
```

```python
import functools

import jax
import jax.numpy as jnp
from jax import lax
from jax.experimental import pallas as pl
from jax.experimental.pallas import tpu as pltpu
from jax.sharding import PartitionSpec as P

DOM = 8
UNIQ = 16
TILE = 128
SIDE = 4
LATE = 2

STRIP = 256
LIST_ROWS = 16
VMEM_BYTES = 60 * 1024 * 1024
LAST_VMEM = 24 * 1024 * 1024
FIRST = 384
SMEM_SPEC = pl.BlockSpec(memory_space=pltpu.SMEM)
VMEM_SPEC = pl.BlockSpec(memory_space=pltpu.VMEM)
HBM_SPEC = pl.BlockSpec(memory_space=pltpu.HBM)


def terms_kernel(right_ref, fock_ref, corr_ref, amp_ref, out_ref, choose_ref):
    fock, corr, amp = fock_ref[0], corr_ref[0], amp_ref[0]
    fock_amp = jnp.dot(fock, amp, preferred_element_type=jnp.float32).astype(jnp.bfloat16)
    over_amp = jnp.dot(corr, amp, preferred_element_type=jnp.float32).astype(jnp.bfloat16)
    first = jnp.dot(fock_amp, corr, preferred_element_type=jnp.float32)
    out_ref[0] = first + jnp.dot(over_amp, fock, preferred_element_type=jnp.float32)
    rows = lax.broadcasted_iota(jnp.int32, choose_ref.shape[1:], 0)
    choose_ref[0] = (rows == right_ref[0]).astype(jnp.float32).astype(jnp.bfloat16)


def pair_terms(right_rows, fock, correlation, amplitudes):
    pairs, rows, cols = fock.shape
    spec = pl.BlockSpec((1, rows, cols), lambda p: (p, 0, 0))
    side = UNIQ * rows // DOM
    return pl.pallas_call(
        terms_kernel,
        grid=(pairs,),
        in_specs=[pl.BlockSpec((1, 1, cols), lambda p: (p, 0, 0))] + [spec] * 3,
        out_specs=[spec, pl.BlockSpec((1, side, cols), lambda p: (p, 0, 0))],
        out_shape=[
            jax.ShapeDtypeStruct(fock.shape, jnp.float32),
            jax.ShapeDtypeStruct((pairs, side, cols), jnp.bfloat16),
        ],
        compiler_params=pltpu.CompilerParams(vmem_limit_bytes=VMEM_BYTES),
        cost_estimate=pl.CostEstimate(
            flops=8 * pairs * rows * rows * cols,
            bytes_accessed=14 * pairs * rows * cols,
            transcendentals=0,
        ),
    )(right_rows, fock, correlation, amplitudes)


def split_kernel(orders, span, own, wanted_ref, place_ref, core_ref, blocks_ref, *rest):
    outs, (bufs, own_buf, tail, ids_smem, in_sems, out_sems) = rest[:-6], rest[-6:]
    rows, depth = blocks_ref.shape
    columns = own_buf.shape[1]
    chunks = span[1] - span[0]
    count = len(orders[0])
    fetches, stores = [], []

    def fetch(n, offset, first, buf):
        start = pl.multiple_of((place_ref[0] ^ offset) * columns + first * TILE, TILE)
        source = blocks_ref.at[:, pl.ds(start, buf.shape[1])]
        fetches.append(pltpu.make_async_copy(source, buf, in_sems.at[n]))
        fetches[-1].start()

    def store(n, c, source, out, row):
        target = out.at[pl.ds(row, source.shape[0])]
        stores.append(pltpu.make_async_copy(source, target, out_sems.at[n, c]))
        stores[-1].start()

    lists = pltpu.make_async_copy(wanted_ref, ids_smem, in_sems.at[count])
    if not own:
        lists.start()
    for n, ks in enumerate(zip(*orders)):
        offset = jnp.where(core_ref[0] % 2 == 0, *ks)
        fetch(n, offset, span[0], bufs.at[n])
    if own:
        fetch(count, 0, 0, own_buf)
    else:
        lists.wait()
        lane = lax.broadcasted_iota(jnp.int32, tail.shape, 1)
        ids = jnp.zeros(tail.shape, jnp.int32)
        for m in range(UNIQ):
            ids = jnp.where(lane == m, ids_smem[m], ids)
        tail[...] = ids.astype(jnp.float32).astype(jnp.bfloat16)
        for n in range(count):
            store(n, chunks, tail, outs[n], chunks * rows)
    for n in range(count):
        fetches[n].wait()
        for c in range(chunks):
            store(n, c, bufs.at[n, :, pl.ds(c * TILE, TILE)], outs[n], c * rows)
    if own:
        fetches[count].wait()
        for c in range(columns // TILE):
            early = c < span[0]
            out = outs[count] if early else outs[count + 1]
            row = (c if early else c - span[0]) * rows
            store(count, c, own_buf.at[:, pl.ds(c * TILE, TILE)], out, row)
    for copy in stores:
        copy.wait()


def column_parts(orders, span, own, wanted, place, core, blocks):
    rows, depth = blocks.shape
    count = len(orders[0])
    columns = depth // (count + 1)
    chunks = span[1] - span[0]
    heights = [chunks * rows + LIST_ROWS * (not own)] * count
    if own:
        heights += [span[0] * rows, chunks * rows]
    return pl.pallas_call(
        functools.partial(split_kernel, orders, span, own),
        in_specs=[HBM_SPEC, SMEM_SPEC, SMEM_SPEC, HBM_SPEC],
        out_specs=[HBM_SPEC] * len(heights),
        out_shape=[jax.ShapeDtypeStruct((height, TILE), blocks.dtype) for height in heights],
        scratch_shapes=[
            pltpu.VMEM((count, rows, chunks * TILE), blocks.dtype),
            pltpu.VMEM((rows, columns), blocks.dtype),
            pltpu.VMEM((LIST_ROWS, TILE), blocks.dtype),
            pltpu.SMEM(wanted.shape, wanted.dtype),
            pltpu.SemaphoreType.DMA((count + 1,)),
            pltpu.SemaphoreType.DMA((count + 1, columns // TILE + 1)),
        ],
        compiler_params=pltpu.CompilerParams(vmem_limit_bytes=VMEM_BYTES),
    )(wanted, place, core, blocks)


def block_order(width):
    bits = width.bit_length() - 1
    row = lax.broadcasted_iota(jnp.int32, (TILE, TILE), 0) >> bits
    col = lax.broadcasted_iota(jnp.int32, (TILE, TILE), 1) >> bits
    return row, col


def packed_gram(held, width):
    tile = {}
    for top in range(0, SIDE * TILE, STRIP):
        strip = lax.dot_general(
            held[top : top + STRIP],
            held[top:],
            (((1,), (1,)), ((), ())),
            preferred_element_type=jnp.float32,
        )
        for i in range(top // TILE, (top + STRIP) // TILE):
            for j in range(i, SIDE):
                r, c = i * TILE - top, j * TILE - top
                tile[i, j] = strip[r : r + TILE, c : c + TILE]
    row, col = block_order(width)

    def diagonal(value):
        found = value[:width]
        for r in range(1, TILE // width):
            here = col[:width] == r
            found = jnp.where(here, value[r * width : (r + 1) * width], found)
        return found

    both = [jnp.where(row <= col, tile[i, i], tile[i + 1, i + 1]) for i in (0, 2)]
    first = [tile[0, 1], tile[0, 2], tile[0, 3], tile[1, 2], diagonal(tile[1, 1])]
    second = [tile[1, 3], tile[2, 3], *both, diagonal(tile[3, 3])]
    return first, second


def gather_rows(pool, places, rows, width, chunks):
    return jnp.concatenate(
        [
            jnp.concatenate(
                [
                    pool[pl.ds(pl.multiple_of(place + c * rows, width), width), :]
                    for place in places
                ],
                axis=0,
            )
            for c in range(chunks)
        ],
        axis=1,
    )


def pool_copies(refs, slots, part, pool, sems):
    return [
        pltpu.make_async_copy(
            ref.at[pl.ds(0, part)],
            pool.at[pl.ds(pl.multiple_of(slot * part, part), part)],
            sems.at[k],
        )
        for k, (ref, slot) in enumerate(zip(refs, slots))
    ]


def early_kernel(ks, owned, width, wanted_ref, place_ref, slot_ref, *rest):
    refs, rest = rest[:-8], rest[-8:]
    acc_ref, spots_ref, pool, lists, ids_vmem, ids, sems, list_sems = rest
    rows = owned * width
    part = refs[0].shape[0]
    chunks = part // rows
    me = place_ref[0]
    tails = [
        pltpu.make_async_copy(ref.at[pl.ds(part, LIST_ROWS)], lists.at[k], list_sems.at[k])
        for k, ref in enumerate(refs[1:], 1)
    ]
    copies = pool_copies(refs, range(len(refs)), part, pool, sems)
    for copy in tails + copies:
        copy.start()
    for copy in tails:
        copy.wait()
    ids_vmem[...] = jnp.zeros_like(ids_vmem)
    for n, k in enumerate(ks):
        if k > 0:
            ids_vmem[n, :] = lists[slot_ref[k]].astype(jnp.float32).astype(jnp.int32)[0]
    to_scalars = pltpu.make_async_copy(ids_vmem, ids, list_sems.at[0])
    to_scalars.start()
    to_scalars.wait()
    for n, k in enumerate(ks):
        for m in range(UNIQ):
            entry = wanted_ref[m] if k == 0 else ids[n, m]
            holder = lax.div(entry, owned)
            spots_ref[n, m] = slot_ref[holder ^ me] * owned + (entry - holder * owned)
    for copy in copies:
        copy.wait()

    @pl.loop(0, len(ks))
    def _(n):
        places = []
        for m in range(UNIQ):
            where = lax.div(spots_ref[n, m], owned)
            places.append(where * part + (spots_ref[n, m] - where * owned) * width)
        held = gather_rows(pool, places, rows, width, chunks)
        at = 0
        for value in sum(packed_gram(held, width), []):
            acc_ref[n, at : at + value.shape[0], :] = value
            at += value.shape[0]


def late_kernel(slots, owned, width, spots_hbm, core_ref, acc_ref, *rest):
    refs, rest = rest[:-6], rest[-6:]
    keep_ref, send_ref, pool, spots_ref, spots_sem, sems = rest
    rows = owned * width
    part = refs[0].shape[0]
    chunks = part // rows
    owners = acc_ref.shape[0]
    half = acc_ref.shape[1] // 2
    core = core_ref[0]
    targets = [jnp.where(core % 2 == 0, *pair) for pair in zip(*slots)]
    copies = pool_copies(refs, targets, part, pool, sems)
    copies.append(pltpu.make_async_copy(spots_hbm, spots_ref, spots_sem))
    for copy in reversed(copies):
        copy.start()
    for copy in copies:
        copy.wait()
    for n in range(owners):
        places = []
        for m in range(UNIQ):
            where = lax.div(spots_ref[n, m], owned)
            places.append(where * part + (spots_ref[n, m] - where * owned) * width)
        halves = packed_gram(gather_rows(pool, places, rows, width, chunks), width)
        at = 0
        for first, second in zip(*halves):
            height = first.shape[0]
            first += acc_ref[n, at : at + height, :]
            second += acc_ref[n, half + at : half + at + height, :]
            keep = jnp.where(core == 0, first, second)
            send = jnp.where(core == 0, second, first)
            keep_ref[n, at : at + height, :] = keep.astype(jnp.bfloat16)
            send_ref[n, at : at + height, :] = send.astype(jnp.bfloat16)
            at += height


def half_rows(width):
    return SIDE * TILE + width


def early_grams(ks, owned, width, wanted, place, slot, parts):
    holders = len(parts)
    rows = owned * width
    chunks = parts[0].shape[0] // rows
    return pl.pallas_call(
        functools.partial(early_kernel, ks, owned, width),
        in_specs=[SMEM_SPEC] * 3 + [HBM_SPEC] * holders,
        out_specs=[VMEM_SPEC, SMEM_SPEC],
        out_shape=[
            jax.ShapeDtypeStruct((len(ks), 2 * half_rows(width), TILE), jnp.float32),
            jax.ShapeDtypeStruct((len(ks), UNIQ), jnp.int32),
        ],
        scratch_shapes=[
            pltpu.VMEM((holders * rows * chunks, TILE), jnp.bfloat16),
            pltpu.VMEM((holders, LIST_ROWS, TILE), jnp.bfloat16),
            pltpu.VMEM((len(ks), TILE), jnp.int32),
            pltpu.SMEM((len(ks), TILE), jnp.int32),
            pltpu.SemaphoreType.DMA((holders,)),
            pltpu.SemaphoreType.DMA((holders,)),
        ],
        compiler_params=pltpu.CompilerParams(vmem_limit_bytes=24 * 1024 * 1024),
        cost_estimate=pl.CostEstimate(
            flops=2 * len(ks) * (SIDE * TILE) ** 2 * chunks * TILE,
            bytes_accessed=2 * holders * rows * chunks * TILE,
            transcendentals=0,
        ),
    )(wanted, place, slot, *parts)


def late_grams(slots, owned, width, spots, core, acc, parts):
    holders = len(parts)
    rows = owned * width
    chunks = parts[0].shape[0] // rows
    half = half_rows(width)
    out = jax.ShapeDtypeStruct((acc.shape[0], half, TILE), jnp.bfloat16)
    owners = acc.shape[0]
    return pl.pallas_call(
        functools.partial(late_kernel, slots, owned, width),
        in_specs=[HBM_SPEC, SMEM_SPEC, VMEM_SPEC] + [HBM_SPEC] * holders,
        out_specs=[VMEM_SPEC] * 2,
        out_shape=[out, out],
        scratch_shapes=[
            pltpu.VMEM((holders * rows * chunks, TILE), jnp.bfloat16),
            pltpu.SMEM(spots.shape, spots.dtype),
            pltpu.SemaphoreType.DMA,
            pltpu.SemaphoreType.DMA((holders,)),
        ],
        compiler_params=pltpu.CompilerParams(vmem_limit_bytes=16 * 1024 * 1024),
        cost_estimate=pl.CostEstimate(
            flops=2 * owners * (SIDE * TILE) ** 2 * chunks * TILE,
            bytes_accessed=2 * holders * rows * chunks * TILE,
            transcendentals=0,
        ),
    )(spots, core, acc, *parts)


def finish_kernel(slots_hbm, core_ref, mine_ref, other_ref, choose_ref, terms_ref, out_ref, *rest):
    slots_ref, slots_sem, gram, stage, sems = rest
    fetch = pltpu.make_async_copy(slots_hbm, slots_ref, slots_sem)
    fetch.start()
    core = core_ref[0]
    width = gram.shape[0] // UNIQ
    pairs = out_ref.shape[0]

    def put(i, j, value):
        gram[i * TILE : (i + 1) * TILE, j * TILE : (j + 1) * TILE] = value.astype(jnp.bfloat16)

    mine, other = mine_ref[...], other_ref[...]
    first = jnp.where(core == 0, mine, other).astype(jnp.float32)
    second = jnp.where(core == 0, other, mine).astype(jnp.float32)
    pieces = [v[t * TILE : (t + 1) * TILE] for v in (first, second) for t in range(SIDE)]
    places = [(0, 1), (0, 2), (0, 3), (1, 2), (1, 3), (2, 3)]
    for (i, j), value in zip(places, pieces):
        put(i, j, value)
        put(j, i, value.T)
    row, col = block_order(width)
    for i, value, diagonal in zip((0, 2), pieces[6:], (first, second)):
        flipped = value.T
        squares = jnp.concatenate([diagonal[SIDE * TILE :]] * (TILE // width), axis=0)
        put(i, i, jnp.where(row <= col, value, flipped))
        lower = jnp.where(row > col, value, flipped)
        put(i + 1, i + 1, jnp.where(row == col, squares, lower))

    fetch.wait()

    def result(pair):
        return pltpu.make_async_copy(stage.at[pair], out_ref.at[pair], sems.at[pair])

    for pair in range(pairs):
        left = jnp.concatenate(
            [gram[pl.ds(slots_ref[pair, m] * width, width), :] for m in range(DOM)], axis=0
        )
        integrals = jnp.dot(left, choose_ref[pair], preferred_element_type=jnp.float32)
        stage[pair] = (integrals + terms_ref[pair]).astype(jnp.bfloat16)
        result(pair).start()
    for pair in range(pairs):
        result(pair).wait()


def finish(slots, core, mine, other, choose, terms):
    pairs, rows, cols = terms.shape
    gram_side = UNIQ * rows // DOM
    return pl.pallas_call(
        finish_kernel,
        in_specs=[HBM_SPEC, SMEM_SPEC] + [VMEM_SPEC] * 4,
        out_specs=HBM_SPEC,
        out_shape=jax.ShapeDtypeStruct(terms.shape, jnp.bfloat16),
        scratch_shapes=[
            pltpu.SMEM(slots.shape, slots.dtype),
            pltpu.SemaphoreType.DMA,
            pltpu.VMEM((gram_side, gram_side), jnp.bfloat16),
            pltpu.VMEM(terms.shape, jnp.bfloat16),
            pltpu.SemaphoreType.DMA((pairs,)),
        ],
        compiler_params=pltpu.CompilerParams(vmem_limit_bytes=LAST_VMEM),
        cost_estimate=pl.CostEstimate(
            flops=2 * pairs * rows * cols * gram_side,
            bytes_accessed=10 * pairs * rows * cols,
            transcendentals=0,
        ),
    )(slots, core, mine, other, choose, terms)


def swap(value, axis, bit):
    size = lax.axis_size(axis)
    return lax.ppermute(value, axis, [(i, i ^ bit) for i in range(size)])


def add(*values):
    return sum(value.astype(jnp.float32) for value in values)


def to_owner(keep, came):
    half = keep.shape[0] // 2
    keep, came = (v.reshape(2, half, *v.shape[1:]) for v in (keep, came))

    def both(bits, offsets, rows):
        return add(keep[bits, offsets, rows], came[bits, offsets, rows]).astype(jnp.bfloat16)

    every, top, rest = slice(None), slice(0, FIRST), slice(FIRST, None)
    far_first = range(half - 1, 0, -1)
    rest_far = [swap(both(every, j, rest), "pairs", 2 * j) for j in far_first]
    top_near = swap(both(1, every, top), "pairs", 1)
    top_sums = [
        add(keep[0, j, top], came[0, j, top], top_near[j]).astype(jnp.bfloat16)
        for j in range(half)
    ]
    top_far = [swap(top_sums[j], "pairs", 2 * j) for j in far_first]
    rest_sums = [
        add(keep[b, 0, rest], came[b, 0, rest], *(v[b] for v in rest_far)).astype(jnp.bfloat16)
        for b in range(2)
    ]
    rest_near = swap(rest_sums[1], "pairs", 1)
    top_total = add(top_sums[0], *top_far).astype(jnp.bfloat16)
    rest_total = add(rest_sums[0], rest_near).astype(jnp.bfloat16)
    return jnp.concatenate([top_total, rest_total], axis=0)


def exchange_orders(holders):
    light, heavy = [*range(1, holders // 2)], [*range(holders // 2, holders)]
    first = heavy[:1]
    for pair in zip(heavy[1:], light):
        first += pair
    second = [k for pair in zip(light, heavy) for k in pair] + heavy[-1:]
    return [first, second]


def split_by_columns(blocks, wanted, pair_slots, fock, correlation, amplitudes):
    holders = lax.axis_size("pairs")
    core = lax.axis_index("aux")
    owned, width, depth = blocks.shape
    stacked = blocks.reshape(owned * width, depth)
    place = lax.axis_index("pairs").reshape(1).astype(jnp.int32)
    core_id = core.reshape(1).astype(jnp.int32)
    orders = exchange_orders(holders)
    slot_tables = [[0] * holders for _ in orders]
    for table, ks in zip(slot_tables, orders):
        for n, k in enumerate(ks, 1):
            table[k] = n
    slot = jnp.asarray(slot_tables, jnp.int32)[core % 2]
    chunks = depth // holders // TILE
    cores = lax.axis_size("aux")

    def exchange(parts, orders):
        arrived = []
        for n, part in enumerate(parts):
            moves = [
                (p * cores + c, (p ^ orders[c % 2][n]) * cores + c)
                for p in range(holders)
                for c in range(cores)
            ]
            arrived.append(lax.ppermute(part, ("pairs", "aux"), moves))
        return arrived

    cut = max(1, chunks - LATE)
    first, second = (0, cut), (cut, chunks)
    early = exchange(column_parts(orders, first, False, wanted, place, core_id, stacked), orders)
    tied = 5
    early[tied], later = lax.optimization_barrier((early[tied], stacked))
    late_orders = orders[::-1]
    late_slots = [[0] + [t[k] for k in ks] for t, ks in zip(slot_tables, late_orders)]
    *late, own_early, own_late = column_parts(late_orders, second, True, wanted, place, core_id, later)
    late = exchange(late, late_orders)
    pairs_here = fock.shape[0]
    slots = lax.dynamic_slice_in_dim(pair_slots, core * pairs_here, pairs_here, axis=0)
    offsets = jnp.arange(width, dtype=jnp.int32)
    right_rows = (slots[:, DOM:, None] * width + offsets).reshape(pairs_here, 1, DOM * width)
    terms, choose = pair_terms(right_rows, fock, correlation, amplitudes)
    early, terms, choose, slots = lax.optimization_barrier((early, terms, choose, slots))
    order = (*range(0, holders, 2), *range(1, holders, 2))
    acc, spots = early_grams(order, owned, width, wanted, place, slot, [own_early, *early])
    keep, send = late_grams(late_slots, owned, width, spots, core_id, acc, [own_late, *late])
    mine = to_owner(keep, swap(send, "aux", 1))
    other = swap(mine, "aux", 1)
    return finish(slots, core_id, mine, other, choose, terms)


def pick_tiles(gram, left_ids, right_ids):
    count = left_ids.shape[0]
    sides = left_ids.shape[1]
    width = gram.shape[2]
    tiles = gram[left_ids[:, :, None], right_ids[:, None, :]]
    return tiles.transpose(0, 1, 3, 2, 4).reshape(count, sides * width, sides * width)


def pair_integrals(held, left_ids, right_ids):
    units, width, depth = held.shape
    stacked = held.reshape(units * width, depth)
    gram = lax.dot_general(
        stacked, stacked, (((1,), (1,)), ((), ())), preferred_element_type=jnp.float32
    )
    gram = gram.reshape(units, width, units, width).transpose(0, 2, 1, 3)
    return pick_tiles(gram, left_ids, right_ids)


def by_request(blocks, wanted, pair_slots, fock, correlation, amplitudes):
    holders = lax.axis_size("pairs")
    owned, width, depth = blocks.shape
    capacity = max(2, (2 * UNIQ + holders - 1) // holders)
    holder = wanted // owned
    local_ids = wanted - holder * owned
    order_ids = jnp.arange(wanted.shape[0])
    earlier = (holder[None, :] == holder[:, None]) & (order_ids[None, :] < order_ids[:, None])
    rank = jnp.sum(earlier.astype(jnp.int32), axis=1)
    slot = holder * capacity + rank
    places = jnp.arange(holders * capacity)
    table = jnp.sum(jnp.where(places[:, None] == slot[None, :], local_ids[None, :], 0), axis=1)
    table = table.reshape(holders, capacity)
    asked = lax.all_to_all(table, "pairs", split_axis=0, concat_axis=0, tiled=True)
    outgoing = jnp.take(blocks, asked.reshape(-1), axis=0).reshape(holders, capacity, width, depth)
    arrived = lax.all_to_all(outgoing, "pairs", split_axis=0, concat_axis=0, tiled=True)
    held = jnp.take(arrived.reshape(holders * capacity, width, depth), slot, axis=0)
    partial_value = pair_integrals(held, pair_slots[:, :DOM], pair_slots[:, DOM:])
    integrals = lax.psum_scatter(
        partial_value.astype(jnp.bfloat16), "aux", scatter_dimension=0, tiled=True
    ).astype(jnp.float32)
    products = functools.partial(
        jnp.einsum, "pab,pbc->pac", preferred_element_type=jnp.float32
    )
    fock_amp = products(fock, amplitudes).astype(jnp.bfloat16)
    over_amp = products(correlation, amplitudes).astype(jnp.bfloat16)
    terms = products(fock_amp, correlation) + products(over_amp, fock)
    return (integrals + terms).astype(jnp.bfloat16)


def on_device(blocks, *others):
    holders = lax.axis_size("pairs")
    owned, width, depth = blocks.shape
    fits = holders > 1 and holders & (holders - 1) == 0 and width & (width - 1) == 0
    fits = fits and depth % (TILE * holders) == 0 and depth // holders >= 2 * TILE
    fits = fits and holders * owned <= 256 and UNIQ * width == SIDE * TILE
    return (split_by_columns if fits else by_request)(blocks, *others)


def solution(mesh):
    return jax.shard_map(
        on_device,
        mesh=mesh,
        in_specs=(
            P(("groups", "pairs"), None, "aux"),
            P(("groups", "pairs")),
            P(("groups", "pairs"), None),
            P(("groups", "pairs", "aux"), None, None),
            P(("groups", "pairs", "aux"), None, None),
            P(("groups", "pairs", "aux"), None, None),
        ),
        out_specs=P(("groups", "pairs", "aux"), None, None),
        check_vma=False,
    )
```

```python
import functools

import jax
import jax.numpy as jnp
from jax import lax
from jax.experimental import pallas as pl
from jax.experimental.pallas import tpu as pltpu
from jax.sharding import PartitionSpec as P

DOM = 8
UNIQ = 16
TILE = 128
SIDE = 4
LATE = 2

STRIP = 256
LIST_ROWS = 16
VMEM_BYTES = 60 * 1024 * 1024
LAST_VMEM = 24 * 1024 * 1024
FIRST = 416
SMEM_SPEC = pl.BlockSpec(memory_space=pltpu.SMEM)
VMEM_SPEC = pl.BlockSpec(memory_space=pltpu.VMEM)
HBM_SPEC = pl.BlockSpec(memory_space=pltpu.HBM)


def terms_kernel(right_ref, fock_ref, corr_ref, amp_ref, out_ref, choose_ref):
    fock, corr, amp = fock_ref[0], corr_ref[0], amp_ref[0]
    fock_amp = jnp.dot(fock, amp, preferred_element_type=jnp.float32).astype(jnp.bfloat16)
    over_amp = jnp.dot(corr, amp, preferred_element_type=jnp.float32).astype(jnp.bfloat16)
    first = jnp.dot(fock_amp, corr, preferred_element_type=jnp.float32)
    out_ref[0] = first + jnp.dot(over_amp, fock, preferred_element_type=jnp.float32)
    rows = lax.broadcasted_iota(jnp.int32, choose_ref.shape[1:], 0)
    choose_ref[0] = (rows == right_ref[0]).astype(jnp.float32).astype(jnp.bfloat16)


def pair_terms(right_rows, fock, correlation, amplitudes):
    pairs, rows, cols = fock.shape
    spec = pl.BlockSpec((1, rows, cols), lambda p: (p, 0, 0))
    side = UNIQ * rows // DOM
    return pl.pallas_call(
        terms_kernel,
        grid=(pairs,),
        in_specs=[pl.BlockSpec((1, 1, cols), lambda p: (p, 0, 0))] + [spec] * 3,
        out_specs=[spec, pl.BlockSpec((1, side, cols), lambda p: (p, 0, 0))],
        out_shape=[
            jax.ShapeDtypeStruct(fock.shape, jnp.float32),
            jax.ShapeDtypeStruct((pairs, side, cols), jnp.bfloat16),
        ],
        compiler_params=pltpu.CompilerParams(vmem_limit_bytes=VMEM_BYTES),
        cost_estimate=pl.CostEstimate(
            flops=8 * pairs * rows * rows * cols,
            bytes_accessed=14 * pairs * rows * cols,
            transcendentals=0,
        ),
    )(right_rows, fock, correlation, amplitudes)


def split_kernel(orders, span, own, wanted_ref, place_ref, core_ref, blocks_ref, *rest):
    outs, (bufs, own_buf, tail, ids_smem, in_sems, out_sems) = rest[:-6], rest[-6:]
    rows, depth = blocks_ref.shape
    columns = own_buf.shape[1]
    chunks = span[1] - span[0]
    count = len(orders[0])
    fetches, stores = [], []

    def fetch(n, offset, first, buf):
        start = pl.multiple_of((place_ref[0] ^ offset) * columns + first * TILE, TILE)
        source = blocks_ref.at[:, pl.ds(start, buf.shape[1])]
        fetches.append(pltpu.make_async_copy(source, buf, in_sems.at[n]))
        fetches[-1].start()

    def store(n, c, source, out, row):
        target = out.at[pl.ds(row, source.shape[0])]
        stores.append(pltpu.make_async_copy(source, target, out_sems.at[n, c]))
        stores[-1].start()

    lists = pltpu.make_async_copy(wanted_ref, ids_smem, in_sems.at[count])
    if not own:
        lists.start()
    for n, ks in enumerate(zip(*orders)):
        offset = jnp.where(core_ref[0] % 2 == 0, *ks)
        fetch(n, offset, span[0], bufs.at[n])
    if own:
        fetch(count, 0, 0, own_buf)
    else:
        lists.wait()
        lane = lax.broadcasted_iota(jnp.int32, tail.shape, 1)
        ids = jnp.zeros(tail.shape, jnp.int32)
        for m in range(UNIQ):
            ids = jnp.where(lane == m, ids_smem[m], ids)
        tail[...] = ids.astype(jnp.float32).astype(jnp.bfloat16)
        for n in range(count):
            store(n, chunks, tail, outs[n], chunks * rows)
    for n in range(count):
        fetches[n].wait()
        for c in range(chunks):
            store(n, c, bufs.at[n, :, pl.ds(c * TILE, TILE)], outs[n], c * rows)
    if own:
        fetches[count].wait()
        for c in range(columns // TILE):
            early = c < span[0]
            out = outs[count] if early else outs[count + 1]
            row = (c if early else c - span[0]) * rows
            store(count, c, own_buf.at[:, pl.ds(c * TILE, TILE)], out, row)
    for copy in stores:
        copy.wait()


def column_parts(orders, span, own, wanted, place, core, blocks):
    rows, depth = blocks.shape
    count = len(orders[0])
    columns = depth // (count + 1)
    chunks = span[1] - span[0]
    heights = [chunks * rows + LIST_ROWS * (not own)] * count
    if own:
        heights += [span[0] * rows, chunks * rows]
    return pl.pallas_call(
        functools.partial(split_kernel, orders, span, own),
        in_specs=[HBM_SPEC, SMEM_SPEC, SMEM_SPEC, HBM_SPEC],
        out_specs=[HBM_SPEC] * len(heights),
        out_shape=[jax.ShapeDtypeStruct((height, TILE), blocks.dtype) for height in heights],
        scratch_shapes=[
            pltpu.VMEM((count, rows, chunks * TILE), blocks.dtype),
            pltpu.VMEM((rows, columns), blocks.dtype),
            pltpu.VMEM((LIST_ROWS, TILE), blocks.dtype),
            pltpu.SMEM(wanted.shape, wanted.dtype),
            pltpu.SemaphoreType.DMA((count + 1,)),
            pltpu.SemaphoreType.DMA((count + 1, columns // TILE + 1)),
        ],
        compiler_params=pltpu.CompilerParams(vmem_limit_bytes=VMEM_BYTES),
    )(wanted, place, core, blocks)


def block_order(width):
    bits = width.bit_length() - 1
    row = lax.broadcasted_iota(jnp.int32, (TILE, TILE), 0) >> bits
    col = lax.broadcasted_iota(jnp.int32, (TILE, TILE), 1) >> bits
    return row, col


def packed_gram(held, width):
    tile = {}
    for top in range(0, SIDE * TILE, STRIP):
        strip = lax.dot_general(
            held[top : top + STRIP],
            held[top:],
            (((1,), (1,)), ((), ())),
            preferred_element_type=jnp.float32,
        )
        for i in range(top // TILE, (top + STRIP) // TILE):
            for j in range(i, SIDE):
                r, c = i * TILE - top, j * TILE - top
                tile[i, j] = strip[r : r + TILE, c : c + TILE]
    row, col = block_order(width)

    def diagonal(value):
        found = value[:width]
        for r in range(1, TILE // width):
            here = col[:width] == r
            found = jnp.where(here, value[r * width : (r + 1) * width], found)
        return found

    both = [jnp.where(row <= col, tile[i, i], tile[i + 1, i + 1]) for i in (0, 2)]
    first = [diagonal(tile[1, 1]), tile[0, 1], tile[0, 2], tile[0, 3], tile[1, 2]]
    second = [diagonal(tile[3, 3]), tile[1, 3], tile[2, 3], *both]
    return first, second


def gather_rows(pool, places, rows, width, chunks):
    return jnp.concatenate(
        [
            jnp.concatenate(
                [
                    pool[pl.ds(pl.multiple_of(place + c * rows, width), width), :]
                    for place in places
                ],
                axis=0,
            )
            for c in range(chunks)
        ],
        axis=1,
    )


def pool_copies(refs, slots, part, pool, sems):
    return [
        pltpu.make_async_copy(
            ref.at[pl.ds(0, part)],
            pool.at[pl.ds(pl.multiple_of(slot * part, part), part)],
            sems.at[k],
        )
        for k, (ref, slot) in enumerate(zip(refs, slots))
    ]


def early_kernel(ks, owned, width, wanted_ref, place_ref, slot_ref, *rest):
    refs, rest = rest[:-8], rest[-8:]
    acc_ref, spots_ref, pool, lists, ids_vmem, ids, sems, list_sems = rest
    rows = owned * width
    part = refs[0].shape[0]
    chunks = part // rows
    me = place_ref[0]
    tails = [
        pltpu.make_async_copy(ref.at[pl.ds(part, LIST_ROWS)], lists.at[k], list_sems.at[k])
        for k, ref in enumerate(refs[1:], 1)
    ]
    copies = pool_copies(refs, range(len(refs)), part, pool, sems)
    for copy in tails + copies:
        copy.start()
    for copy in tails:
        copy.wait()
    ids_vmem[...] = jnp.zeros_like(ids_vmem)
    for n, k in enumerate(ks):
        if k > 0:
            ids_vmem[n, :] = lists[slot_ref[k]].astype(jnp.float32).astype(jnp.int32)[0]
    to_scalars = pltpu.make_async_copy(ids_vmem, ids, list_sems.at[0])
    to_scalars.start()
    to_scalars.wait()
    for n, k in enumerate(ks):
        for m in range(UNIQ):
            entry = wanted_ref[m] if k == 0 else ids[n, m]
            holder = lax.div(entry, owned)
            spots_ref[n, m] = slot_ref[holder ^ me] * owned + (entry - holder * owned)
    for copy in copies:
        copy.wait()

    @pl.loop(0, len(ks))
    def _(n):
        places = []
        for m in range(UNIQ):
            where = lax.div(spots_ref[n, m], owned)
            places.append(where * part + (spots_ref[n, m] - where * owned) * width)
        held = gather_rows(pool, places, rows, width, chunks)
        at = 0
        for value in sum(packed_gram(held, width), []):
            acc_ref[n, at : at + value.shape[0], :] = value
            at += value.shape[0]


def late_kernel(slots, owned, width, spots_hbm, core_ref, acc_ref, *rest):
    refs, rest = rest[:-8], rest[-8:]
    keep_ref, near_ref, even_ref, odd_ref, pool, spots_ref, spots_sem, sems = rest
    rows = owned * width
    part = refs[0].shape[0]
    chunks = part // rows
    owners = acc_ref.shape[0]
    half = acc_ref.shape[1] // 2
    core = core_ref[0]
    targets = [jnp.where(core % 2 == 0, *pair) for pair in zip(*slots)]
    copies = pool_copies(refs, targets, part, pool, sems)
    copies.append(pltpu.make_async_copy(spots_hbm, spots_ref, spots_sem))
    for copy in reversed(copies):
        copy.start()
    for copy in copies:
        copy.wait()
    for n in range(owners):
        places = []
        for m in range(UNIQ):
            where = lax.div(spots_ref[n, m], owned)
            places.append(where * part + (spots_ref[n, m] - where * owned) * width)
        halves = packed_gram(gather_rows(pool, places, rows, width, chunks), width)
        at = 0
        for first, second in zip(*halves):
            height = first.shape[0]
            first += acc_ref[n, at : at + height, :]
            second += acc_ref[n, half + at : half + at + height, :]
            keep = jnp.where(core == 0, first, second)
            send = jnp.where(core == 0, second, first)
            keep_ref[n, at : at + height, :] = keep.astype(jnp.bfloat16)
            if n < owners // 2:
                even_ref[n, at : at + height, :] = send.astype(jnp.bfloat16)
            elif at < FIRST:
                near_ref[n - owners // 2, at : at + height, :] = send.astype(jnp.bfloat16)
            else:
                row = at - FIRST
                odd_ref[n - owners // 2, row : row + height, :] = send.astype(jnp.bfloat16)
            at += height


def half_rows(width):
    return SIDE * TILE + width


def early_grams(ks, owned, width, wanted, place, slot, parts):
    holders = len(parts)
    rows = owned * width
    chunks = parts[0].shape[0] // rows
    return pl.pallas_call(
        functools.partial(early_kernel, ks, owned, width),
        in_specs=[SMEM_SPEC] * 3 + [HBM_SPEC] * holders,
        out_specs=[VMEM_SPEC, SMEM_SPEC],
        out_shape=[
            jax.ShapeDtypeStruct((len(ks), 2 * half_rows(width), TILE), jnp.float32),
            jax.ShapeDtypeStruct((len(ks), UNIQ), jnp.int32),
        ],
        scratch_shapes=[
            pltpu.VMEM((holders * rows * chunks, TILE), jnp.bfloat16),
            pltpu.VMEM((holders, LIST_ROWS, TILE), jnp.bfloat16),
            pltpu.VMEM((len(ks), TILE), jnp.int32),
            pltpu.SMEM((len(ks), TILE), jnp.int32),
            pltpu.SemaphoreType.DMA((holders,)),
            pltpu.SemaphoreType.DMA((holders,)),
        ],
        compiler_params=pltpu.CompilerParams(vmem_limit_bytes=24 * 1024 * 1024),
        cost_estimate=pl.CostEstimate(
            flops=2 * len(ks) * (SIDE * TILE) ** 2 * chunks * TILE,
            bytes_accessed=2 * holders * rows * chunks * TILE,
            transcendentals=0,
        ),
    )(wanted, place, slot, *parts)


def late_grams(slots, owned, width, spots, core, acc, parts):
    holders = len(parts)
    rows = owned * width
    chunks = parts[0].shape[0] // rows
    half = half_rows(width)
    owners = acc.shape[0]
    return pl.pallas_call(
        functools.partial(late_kernel, slots, owned, width),
        in_specs=[HBM_SPEC, SMEM_SPEC, VMEM_SPEC] + [HBM_SPEC] * holders,
        out_specs=[VMEM_SPEC] * 4,
        out_shape=[
            jax.ShapeDtypeStruct((count, height, TILE), jnp.bfloat16)
            for count, height in (
                (owners, half),
                (owners // 2, FIRST),
                (owners // 2, half),
                (owners // 2, half - FIRST),
            )
        ],
        scratch_shapes=[
            pltpu.VMEM((holders * rows * chunks, TILE), jnp.bfloat16),
            pltpu.SMEM(spots.shape, spots.dtype),
            pltpu.SemaphoreType.DMA,
            pltpu.SemaphoreType.DMA((holders,)),
        ],
        compiler_params=pltpu.CompilerParams(vmem_limit_bytes=16 * 1024 * 1024),
        cost_estimate=pl.CostEstimate(
            flops=2 * owners * (SIDE * TILE) ** 2 * chunks * TILE,
            bytes_accessed=2 * holders * rows * chunks * TILE,
            transcendentals=0,
        ),
    )(spots, core, acc, *parts)


def finish_kernel(slots_hbm, core_ref, mine_ref, other_ref, choose_ref, terms_ref, out_ref, *rest):
    slots_ref, slots_sem, gram, stage, sems = rest
    fetch = pltpu.make_async_copy(slots_hbm, slots_ref, slots_sem)
    fetch.start()
    core = core_ref[0]
    width = gram.shape[0] // UNIQ
    pairs = out_ref.shape[0]

    def put(i, j, value):
        gram[i * TILE : (i + 1) * TILE, j * TILE : (j + 1) * TILE] = value.astype(jnp.bfloat16)

    mine, other = mine_ref[...], other_ref[...]
    first = jnp.where(core == 0, mine, other).astype(jnp.float32)
    second = jnp.where(core == 0, other, mine).astype(jnp.float32)
    pieces = [
        v[width + t * TILE : width + (t + 1) * TILE]
        for v in (first, second)
        for t in range(SIDE)
    ]
    places = [(0, 1), (0, 2), (0, 3), (1, 2), (1, 3), (2, 3)]
    for (i, j), value in zip(places, pieces):
        put(i, j, value)
        put(j, i, value.T)
    row, col = block_order(width)
    for i, value, diagonal in zip((0, 2), pieces[6:], (first, second)):
        flipped = value.T
        squares = jnp.concatenate([diagonal[:width]] * (TILE // width), axis=0)
        put(i, i, jnp.where(row <= col, value, flipped))
        lower = jnp.where(row > col, value, flipped)
        put(i + 1, i + 1, jnp.where(row == col, squares, lower))

    fetch.wait()

    def result(pair):
        return pltpu.make_async_copy(stage.at[pair], out_ref.at[pair], sems.at[pair])

    for pair in range(pairs):
        left = jnp.concatenate(
            [gram[pl.ds(slots_ref[pair, m] * width, width), :] for m in range(DOM)], axis=0
        )
        integrals = jnp.dot(left, choose_ref[pair], preferred_element_type=jnp.float32)
        stage[pair] = (integrals + terms_ref[pair]).astype(jnp.bfloat16)
        result(pair).start()
    for pair in range(pairs):
        result(pair).wait()


def finish(slots, core, mine, other, choose, terms):
    pairs, rows, cols = terms.shape
    gram_side = UNIQ * rows // DOM
    return pl.pallas_call(
        finish_kernel,
        in_specs=[HBM_SPEC, SMEM_SPEC] + [VMEM_SPEC] * 4,
        out_specs=HBM_SPEC,
        out_shape=jax.ShapeDtypeStruct(terms.shape, jnp.bfloat16),
        scratch_shapes=[
            pltpu.SMEM(slots.shape, slots.dtype),
            pltpu.SemaphoreType.DMA,
            pltpu.VMEM((gram_side, gram_side), jnp.bfloat16),
            pltpu.VMEM(terms.shape, jnp.bfloat16),
            pltpu.SemaphoreType.DMA((pairs,)),
        ],
        compiler_params=pltpu.CompilerParams(vmem_limit_bytes=LAST_VMEM),
        cost_estimate=pl.CostEstimate(
            flops=2 * pairs * rows * cols * gram_side,
            bytes_accessed=10 * pairs * rows * cols,
            transcendentals=0,
        ),
    )(slots, core, mine, other, choose, terms)


def swap(value, axis, bit):
    size = lax.axis_size(axis)
    return lax.ppermute(value, axis, [(i, i ^ bit) for i in range(size)])


def add(*values):
    return sum(value.astype(jnp.float32) for value in values)


def to_owner(keep, came_near, came_even, came_odd):
    half = keep.shape[0] // 2
    keep = keep.reshape(2, half, *keep.shape[1:])
    top, rest = slice(0, FIRST), slice(FIRST, None)
    top_near = swap(add(keep[1, :, top], came_near).astype(jnp.bfloat16), "pairs", 1)

    def rest_sum(j):
        even = add(keep[0, j, rest], came_even[j, rest])
        return jnp.stack([even, add(keep[1, j, rest], came_odd[j])])

    far_first = range(half - 1, 0, -1)
    rest_far = [swap(rest_sum(j).astype(jnp.bfloat16), "pairs", 2 * j) for j in far_first]
    top_sums = [
        add(keep[0, j, top], came_even[j, top], top_near[j]).astype(jnp.bfloat16)
        for j in range(half)
    ]
    top_far = [swap(top_sums[j], "pairs", 2 * j) for j in far_first]
    rest_sums = [
        add(rest_sum(0)[b], *(v[b] for v in rest_far)).astype(jnp.bfloat16)
        for b in range(2)
    ]
    rest_near = swap(rest_sums[1], "pairs", 1)
    top_total = add(top_sums[0], *top_far).astype(jnp.bfloat16)
    rest_total = add(rest_sums[0], rest_near).astype(jnp.bfloat16)
    return jnp.concatenate([top_total, rest_total], axis=0)


def exchange_orders(holders):
    light, heavy = [*range(1, holders // 2)], [*range(holders // 2, holders)]
    first = heavy[:1]
    for pair in zip(heavy[1:], light):
        first += pair
    second = [k for pair in zip(light, heavy) for k in pair] + heavy[-1:]
    return [first, second]


def split_by_columns(blocks, wanted, pair_slots, fock, correlation, amplitudes):
    holders = lax.axis_size("pairs")
    core = lax.axis_index("aux")
    owned, width, depth = blocks.shape
    stacked = blocks.reshape(owned * width, depth)
    place = lax.axis_index("pairs").reshape(1).astype(jnp.int32)
    core_id = core.reshape(1).astype(jnp.int32)
    orders = exchange_orders(holders)
    slot_tables = [[0] * holders for _ in orders]
    for table, ks in zip(slot_tables, orders):
        for n, k in enumerate(ks, 1):
            table[k] = n
    slot = jnp.asarray(slot_tables, jnp.int32)[core % 2]
    chunks = depth // holders // TILE
    cores = lax.axis_size("aux")

    def exchange(parts, orders):
        arrived = []
        for n, part in enumerate(parts):
            moves = [
                (p * cores + c, (p ^ orders[c % 2][n]) * cores + c)
                for p in range(holders)
                for c in range(cores)
            ]
            arrived.append(lax.ppermute(part, ("pairs", "aux"), moves))
        return arrived

    cut = max(1, chunks - LATE)
    first, second = (0, cut), (cut, chunks)
    early = exchange(column_parts(orders, first, False, wanted, place, core_id, stacked), orders)
    tied = max(0, len(early) - 2)
    early[tied], later = lax.optimization_barrier((early[tied], stacked))
    late_orders = orders[::-1]
    late_slots = [[0] + [t[k] for k in ks] for t, ks in zip(slot_tables, late_orders)]
    *late, own_early, own_late = column_parts(late_orders, second, True, wanted, place, core_id, later)
    late = exchange(late, late_orders)
    pairs_here = fock.shape[0]
    slots = lax.dynamic_slice_in_dim(pair_slots, core * pairs_here, pairs_here, axis=0)
    offsets = jnp.arange(width, dtype=jnp.int32)
    right_rows = (slots[:, DOM:, None] * width + offsets).reshape(pairs_here, 1, DOM * width)
    terms, choose = pair_terms(right_rows, fock, correlation, amplitudes)
    early, terms, choose, slots = lax.optimization_barrier((early, terms, choose, slots))
    order = (*range(0, holders, 2), *range(1, holders, 2))
    acc, spots = early_grams(order, owned, width, wanted, place, slot, [own_early, *early])
    keep, *sent = late_grams(late_slots, owned, width, spots, core_id, acc, [own_late, *late])
    mine = to_owner(keep, *(swap(value, "aux", 1) for value in sent))
    other = swap(mine, "aux", 1)
    return finish(slots, core_id, mine, other, choose, terms)


def pick_tiles(gram, left_ids, right_ids):
    count = left_ids.shape[0]
    sides = left_ids.shape[1]
    width = gram.shape[2]
    tiles = gram[left_ids[:, :, None], right_ids[:, None, :]]
    return tiles.transpose(0, 1, 3, 2, 4).reshape(count, sides * width, sides * width)


def pair_integrals(held, left_ids, right_ids):
    units, width, depth = held.shape
    stacked = held.reshape(units * width, depth)
    gram = lax.dot_general(
        stacked, stacked, (((1,), (1,)), ((), ())), preferred_element_type=jnp.float32
    )
    gram = gram.reshape(units, width, units, width).transpose(0, 2, 1, 3)
    return pick_tiles(gram, left_ids, right_ids)


def by_request(blocks, wanted, pair_slots, fock, correlation, amplitudes):
    holders = lax.axis_size("pairs")
    owned, width, depth = blocks.shape
    capacity = max(2, (2 * UNIQ + holders - 1) // holders)
    holder = wanted // owned
    local_ids = wanted - holder * owned
    order_ids = jnp.arange(wanted.shape[0])
    earlier = (holder[None, :] == holder[:, None]) & (order_ids[None, :] < order_ids[:, None])
    rank = jnp.sum(earlier.astype(jnp.int32), axis=1)
    slot = holder * capacity + rank
    places = jnp.arange(holders * capacity)
    table = jnp.sum(jnp.where(places[:, None] == slot[None, :], local_ids[None, :], 0), axis=1)
    table = table.reshape(holders, capacity)
    asked = lax.all_to_all(table, "pairs", split_axis=0, concat_axis=0, tiled=True)
    outgoing = jnp.take(blocks, asked.reshape(-1), axis=0).reshape(holders, capacity, width, depth)
    arrived = lax.all_to_all(outgoing, "pairs", split_axis=0, concat_axis=0, tiled=True)
    held = jnp.take(arrived.reshape(holders * capacity, width, depth), slot, axis=0)
    partial_value = pair_integrals(held, pair_slots[:, :DOM], pair_slots[:, DOM:])
    integrals = lax.psum_scatter(
        partial_value.astype(jnp.bfloat16), "aux", scatter_dimension=0, tiled=True
    ).astype(jnp.float32)
    products = functools.partial(
        jnp.einsum, "pab,pbc->pac", preferred_element_type=jnp.float32
    )
    fock_amp = products(fock, amplitudes).astype(jnp.bfloat16)
    over_amp = products(correlation, amplitudes).astype(jnp.bfloat16)
    terms = products(fock_amp, correlation) + products(over_amp, fock)
    return (integrals + terms).astype(jnp.bfloat16)


def on_device(blocks, *others):
    holders = lax.axis_size("pairs")
    owned, width, depth = blocks.shape
    fits = holders > 1 and holders & (holders - 1) == 0 and width & (width - 1) == 0
    fits = fits and depth % (TILE * holders) == 0 and depth // holders >= 2 * TILE
    fits = fits and holders * owned <= 256 and UNIQ * width == SIDE * TILE
    return (split_by_columns if fits else by_request)(blocks, *others)


def solution(mesh):
    return jax.shard_map(
        on_device,
        mesh=mesh,
        in_specs=(
            P(("groups", "pairs"), None, "aux"),
            P(("groups", "pairs")),
            P(("groups", "pairs"), None),
            P(("groups", "pairs", "aux"), None, None),
            P(("groups", "pairs", "aux"), None, None),
            P(("groups", "pairs", "aux"), None, None),
        ),
        out_specs=P(("groups", "pairs", "aux"), None, None),
        check_vma=False,
    )
```

```python
import functools

import jax
import jax.numpy as jnp
from jax import lax
from jax.experimental import pallas as pl
from jax.experimental.pallas import tpu as pltpu
from jax.sharding import PartitionSpec as P

DOM = 8
UNIQ = 16
TILE = 128
SIDE = 4
LATE = 2

STRIP = 256
LIST_ROWS = 16
VMEM_BYTES = 60 * 1024 * 1024
LAST_VMEM = 24 * 1024 * 1024
FIRST = 416
SMEM_SPEC = pl.BlockSpec(memory_space=pltpu.SMEM)
VMEM_SPEC = pl.BlockSpec(memory_space=pltpu.VMEM)
HBM_SPEC = pl.BlockSpec(memory_space=pltpu.HBM)


def terms_kernel(right_ref, fock_ref, corr_ref, amp_ref, out_ref, choose_ref):
    fock, corr, amp = fock_ref[0], corr_ref[0], amp_ref[0]
    fock_amp = jnp.dot(fock, amp, preferred_element_type=jnp.float32).astype(jnp.bfloat16)
    over_amp = jnp.dot(corr, amp, preferred_element_type=jnp.float32).astype(jnp.bfloat16)
    first = jnp.dot(fock_amp, corr, preferred_element_type=jnp.float32)
    out_ref[0] = first + jnp.dot(over_amp, fock, preferred_element_type=jnp.float32)
    rows = lax.broadcasted_iota(jnp.int32, choose_ref.shape[1:], 0)
    choose_ref[0] = (rows == right_ref[0]).astype(jnp.float32).astype(jnp.bfloat16)


def pair_terms(right_rows, fock, correlation, amplitudes):
    pairs, rows, cols = fock.shape
    spec = pl.BlockSpec((1, rows, cols), lambda p: (p, 0, 0))
    side = UNIQ * rows // DOM
    return pl.pallas_call(
        terms_kernel,
        grid=(pairs,),
        in_specs=[pl.BlockSpec((1, 1, cols), lambda p: (p, 0, 0))] + [spec] * 3,
        out_specs=[spec, pl.BlockSpec((1, side, cols), lambda p: (p, 0, 0))],
        out_shape=[
            jax.ShapeDtypeStruct(fock.shape, jnp.float32),
            jax.ShapeDtypeStruct((pairs, side, cols), jnp.bfloat16),
        ],
        compiler_params=pltpu.CompilerParams(vmem_limit_bytes=VMEM_BYTES),
        cost_estimate=pl.CostEstimate(
            flops=8 * pairs * rows * rows * cols,
            bytes_accessed=14 * pairs * rows * cols,
            transcendentals=0,
        ),
    )(right_rows, fock, correlation, amplitudes)


def split_kernel(orders, span, own, wanted_ref, place_ref, core_ref, blocks_ref, *rest):
    outs, (bufs, own_buf, tail, ids_smem, in_sems, out_sems) = rest[:-6], rest[-6:]
    rows, depth = blocks_ref.shape
    columns = own_buf.shape[1]
    chunks = span[1] - span[0]
    count = len(orders[0])
    fetches, stores = [], []

    def fetch(n, offset, first, buf):
        start = pl.multiple_of((place_ref[0] ^ offset) * columns + first * TILE, TILE)
        source = blocks_ref.at[:, pl.ds(start, buf.shape[1])]
        fetches.append(pltpu.make_async_copy(source, buf, in_sems.at[n]))
        fetches[-1].start()

    def store(n, c, source, out, row):
        target = out.at[pl.ds(row, source.shape[0])]
        stores.append(pltpu.make_async_copy(source, target, out_sems.at[n, c]))
        stores[-1].start()

    lists = pltpu.make_async_copy(wanted_ref, ids_smem, in_sems.at[count])
    if not own:
        lists.start()
    for n, ks in enumerate(zip(*orders)):
        offset = jnp.where(core_ref[0] % 2 == 0, *ks)
        fetch(n, offset, span[0], bufs.at[n])
    if own:
        fetch(count, 0, 0, own_buf)
    else:
        lists.wait()
        lane = lax.broadcasted_iota(jnp.int32, tail.shape, 1)
        ids = jnp.zeros(tail.shape, jnp.int32)
        for m in range(UNIQ):
            ids = jnp.where(lane == m, ids_smem[m], ids)
        tail[...] = ids.astype(jnp.float32).astype(jnp.bfloat16)
        for n in range(count):
            store(n, chunks, tail, outs[n], chunks * rows)
    for n in range(count):
        fetches[n].wait()
        for c in range(chunks):
            store(n, c, bufs.at[n, :, pl.ds(c * TILE, TILE)], outs[n], c * rows)
    if own:
        fetches[count].wait()
        for c in range(columns // TILE):
            early = c < span[0]
            out = outs[count] if early else outs[count + 1]
            row = (c if early else c - span[0]) * rows
            store(count, c, own_buf.at[:, pl.ds(c * TILE, TILE)], out, row)
    for copy in stores:
        copy.wait()


def column_parts(orders, span, own, wanted, place, core, blocks):
    rows, depth = blocks.shape
    count = len(orders[0])
    columns = depth // (count + 1)
    chunks = span[1] - span[0]
    heights = [chunks * rows + LIST_ROWS * (not own)] * count
    if own:
        heights += [span[0] * rows, chunks * rows]
    return pl.pallas_call(
        functools.partial(split_kernel, orders, span, own),
        in_specs=[HBM_SPEC, SMEM_SPEC, SMEM_SPEC, HBM_SPEC],
        out_specs=[HBM_SPEC] * len(heights),
        out_shape=[jax.ShapeDtypeStruct((height, TILE), blocks.dtype) for height in heights],
        scratch_shapes=[
            pltpu.VMEM((count, rows, chunks * TILE), blocks.dtype),
            pltpu.VMEM((rows, columns), blocks.dtype),
            pltpu.VMEM((LIST_ROWS, TILE), blocks.dtype),
            pltpu.SMEM(wanted.shape, wanted.dtype),
            pltpu.SemaphoreType.DMA((count + 1,)),
            pltpu.SemaphoreType.DMA((count + 1, columns // TILE + 1)),
        ],
        compiler_params=pltpu.CompilerParams(vmem_limit_bytes=VMEM_BYTES),
    )(wanted, place, core, blocks)


def block_order(width):
    bits = width.bit_length() - 1
    row = lax.broadcasted_iota(jnp.int32, (TILE, TILE), 0) >> bits
    col = lax.broadcasted_iota(jnp.int32, (TILE, TILE), 1) >> bits
    return row, col


def packed_gram(held, width):
    tile = {}
    for top in range(0, SIDE * TILE, STRIP):
        strip = lax.dot_general(
            held[top : top + STRIP],
            held[top:],
            (((1,), (1,)), ((), ())),
            preferred_element_type=jnp.float32,
        )
        for i in range(top // TILE, (top + STRIP) // TILE):
            for j in range(i, SIDE):
                r, c = i * TILE - top, j * TILE - top
                tile[i, j] = strip[r : r + TILE, c : c + TILE]
    row, col = block_order(width)

    def diagonal(value):
        found = value[:width]
        for r in range(1, TILE // width):
            here = col[:width] == r
            found = jnp.where(here, value[r * width : (r + 1) * width], found)
        return found

    both = [jnp.where(row <= col, tile[i, i], tile[i + 1, i + 1]) for i in (0, 2)]
    first = [diagonal(tile[1, 1]), tile[0, 1], tile[0, 2], tile[0, 3], tile[1, 2]]
    second = [diagonal(tile[3, 3]), tile[1, 3], tile[2, 3], *both]
    return first, second


def gather_rows(pool, places, rows, width, chunks):
    return jnp.concatenate(
        [
            jnp.concatenate(
                [
                    pool[pl.ds(pl.multiple_of(place + c * rows, width), width), :]
                    for place in places
                ],
                axis=0,
            )
            for c in range(chunks)
        ],
        axis=1,
    )


def pool_copies(refs, slots, part, pool, sems):
    return [
        pltpu.make_async_copy(
            ref.at[pl.ds(0, part)],
            pool.at[pl.ds(pl.multiple_of(slot * part, part), part)],
            sems.at[k],
        )
        for k, (ref, slot) in enumerate(zip(refs, slots))
    ]


def early_kernel(ks, owned, width, wanted_ref, place_ref, slot_ref, *rest):
    refs, rest = rest[:-8], rest[-8:]
    acc_ref, spots_ref, pool, lists, ids_vmem, ids, sems, list_sems = rest
    rows = owned * width
    part = refs[0].shape[0]
    chunks = part // rows
    me = place_ref[0]
    tails = [
        pltpu.make_async_copy(ref.at[pl.ds(part, LIST_ROWS)], lists.at[k], list_sems.at[k])
        for k, ref in enumerate(refs[1:], 1)
    ]
    copies = pool_copies(refs, range(len(refs)), part, pool, sems)
    for copy in tails + copies:
        copy.start()
    for copy in tails:
        copy.wait()
    ids_vmem[...] = jnp.zeros_like(ids_vmem)
    for n, k in enumerate(ks):
        if k > 0:
            ids_vmem[n, :] = lists[slot_ref[k]].astype(jnp.float32).astype(jnp.int32)[0]
    to_scalars = pltpu.make_async_copy(ids_vmem, ids, list_sems.at[0])
    to_scalars.start()
    to_scalars.wait()
    for n, k in enumerate(ks):
        for m in range(UNIQ):
            entry = wanted_ref[m] if k == 0 else ids[n, m]
            holder = lax.div(entry, owned)
            spots_ref[n, m] = slot_ref[holder ^ me] * owned + (entry - holder * owned)
    for copy in copies:
        copy.wait()

    @pl.loop(0, len(ks))
    def _(n):
        places = []
        for m in range(UNIQ):
            where = lax.div(spots_ref[n, m], owned)
            places.append(where * part + (spots_ref[n, m] - where * owned) * width)
        held = gather_rows(pool, places, rows, width, chunks)
        at = 0
        for value in sum(packed_gram(held, width), []):
            acc_ref[n, at : at + value.shape[0], :] = value
            at += value.shape[0]


def late_kernel(slots, owned, width, spots_hbm, core_ref, acc_ref, *rest):
    refs, rest = rest[:-8], rest[-8:]
    keep_ref, near_ref, even_ref, odd_ref, pool, spots_ref, spots_sem, sems = rest
    rows = owned * width
    part = refs[0].shape[0]
    chunks = part // rows
    owners = acc_ref.shape[0]
    half = acc_ref.shape[1] // 2
    core = core_ref[0]
    targets = [jnp.where(core % 2 == 0, *pair) for pair in zip(*slots)]
    copies = pool_copies(refs, targets, part, pool, sems)
    copies.append(pltpu.make_async_copy(spots_hbm, spots_ref, spots_sem))
    for copy in reversed(copies):
        copy.start()
    for copy in copies:
        copy.wait()
    for n in range(owners):
        places = []
        for m in range(UNIQ):
            where = lax.div(spots_ref[n, m], owned)
            places.append(where * part + (spots_ref[n, m] - where * owned) * width)
        halves = packed_gram(gather_rows(pool, places, rows, width, chunks), width)
        at = 0
        for first, second in zip(*halves):
            height = first.shape[0]
            first += acc_ref[n, at : at + height, :]
            second += acc_ref[n, half + at : half + at + height, :]
            keep = jnp.where(core == 0, first, second)
            send = jnp.where(core == 0, second, first)
            keep_ref[n, at : at + height, :] = keep.astype(jnp.bfloat16)
            if n < owners // 2:
                even_ref[n, at : at + height, :] = send.astype(jnp.bfloat16)
            elif at < FIRST:
                near_ref[n - owners // 2, at : at + height, :] = send.astype(jnp.bfloat16)
            else:
                row = at - FIRST
                odd_ref[n - owners // 2, row : row + height, :] = send.astype(jnp.bfloat16)
            at += height


def half_rows(width):
    return SIDE * TILE + width


def early_grams(ks, owned, width, wanted, place, slot, parts):
    holders = len(parts)
    rows = owned * width
    chunks = parts[0].shape[0] // rows
    return pl.pallas_call(
        functools.partial(early_kernel, ks, owned, width),
        in_specs=[SMEM_SPEC] * 3 + [HBM_SPEC] * holders,
        out_specs=[VMEM_SPEC, SMEM_SPEC],
        out_shape=[
            jax.ShapeDtypeStruct((len(ks), 2 * half_rows(width), TILE), jnp.float32),
            jax.ShapeDtypeStruct((len(ks), UNIQ), jnp.int32),
        ],
        scratch_shapes=[
            pltpu.VMEM((holders * rows * chunks, TILE), jnp.bfloat16),
            pltpu.VMEM((holders, LIST_ROWS, TILE), jnp.bfloat16),
            pltpu.VMEM((len(ks), TILE), jnp.int32),
            pltpu.SMEM((len(ks), TILE), jnp.int32),
            pltpu.SemaphoreType.DMA((holders,)),
            pltpu.SemaphoreType.DMA((holders,)),
        ],
        compiler_params=pltpu.CompilerParams(vmem_limit_bytes=24 * 1024 * 1024),
        cost_estimate=pl.CostEstimate(
            flops=2 * len(ks) * (SIDE * TILE) ** 2 * chunks * TILE,
            bytes_accessed=2 * holders * rows * chunks * TILE,
            transcendentals=0,
        ),
    )(wanted, place, slot, *parts)


def late_grams(slots, owned, width, spots, core, acc, parts):
    holders = len(parts)
    rows = owned * width
    chunks = parts[0].shape[0] // rows
    half = half_rows(width)
    owners = acc.shape[0]
    return pl.pallas_call(
        functools.partial(late_kernel, slots, owned, width),
        in_specs=[HBM_SPEC, SMEM_SPEC, VMEM_SPEC] + [HBM_SPEC] * holders,
        out_specs=[VMEM_SPEC] * 4,
        out_shape=[
            jax.ShapeDtypeStruct((count, height, TILE), jnp.bfloat16)
            for count, height in (
                (owners, half),
                (owners // 2, FIRST),
                (owners // 2, half),
                (owners // 2, half - FIRST),
            )
        ],
        scratch_shapes=[
            pltpu.VMEM((holders * rows * chunks, TILE), jnp.bfloat16),
            pltpu.SMEM(spots.shape, spots.dtype),
            pltpu.SemaphoreType.DMA,
            pltpu.SemaphoreType.DMA((holders,)),
        ],
        compiler_params=pltpu.CompilerParams(vmem_limit_bytes=16 * 1024 * 1024),
        cost_estimate=pl.CostEstimate(
            flops=2 * owners * (SIDE * TILE) ** 2 * chunks * TILE,
            bytes_accessed=2 * holders * rows * chunks * TILE,
            transcendentals=0,
        ),
    )(spots, core, acc, *parts)


def finish_kernel(slots_hbm, core_ref, mine_top, mine_rest, other_top, other_rest, choose_ref, terms_ref, out_ref, *rest):
    slots_ref, slots_sem, gram, stage, sems = rest
    fetch = pltpu.make_async_copy(slots_hbm, slots_ref, slots_sem)
    fetch.start()
    core = core_ref[0]
    width = gram.shape[0] // UNIQ
    pairs = out_ref.shape[0]

    def put(i, j, value):
        gram[i * TILE : (i + 1) * TILE, j * TILE : (j + 1) * TILE] = value.astype(jnp.bfloat16)

    mine = jnp.concatenate([mine_top[...], mine_rest[...]], axis=0)
    other = jnp.concatenate([other_top[...], other_rest[...]], axis=0)
    first = jnp.where(core == 0, mine, other).astype(jnp.float32)
    second = jnp.where(core == 0, other, mine).astype(jnp.float32)
    pieces = [
        v[width + t * TILE : width + (t + 1) * TILE]
        for v in (first, second)
        for t in range(SIDE)
    ]
    places = [(0, 1), (0, 2), (0, 3), (1, 2), (1, 3), (2, 3)]
    for (i, j), value in zip(places, pieces):
        put(i, j, value)
        put(j, i, value.T)
    row, col = block_order(width)
    for i, value, diagonal in zip((0, 2), pieces[6:], (first, second)):
        flipped = value.T
        squares = jnp.concatenate([diagonal[:width]] * (TILE // width), axis=0)
        put(i, i, jnp.where(row <= col, value, flipped))
        lower = jnp.where(row > col, value, flipped)
        put(i + 1, i + 1, jnp.where(row == col, squares, lower))

    fetch.wait()

    def result(pair):
        return pltpu.make_async_copy(stage.at[pair], out_ref.at[pair], sems.at[pair])

    for pair in range(pairs):
        left = jnp.concatenate(
            [gram[pl.ds(slots_ref[pair, m] * width, width), :] for m in range(DOM)], axis=0
        )
        integrals = jnp.dot(left, choose_ref[pair], preferred_element_type=jnp.float32)
        stage[pair] = (integrals + terms_ref[pair]).astype(jnp.bfloat16)
        result(pair).start()
    for pair in range(pairs):
        result(pair).wait()


def finish(slots, core, mine, other, choose, terms):
    pairs, rows, cols = terms.shape
    gram_side = UNIQ * rows // DOM
    return pl.pallas_call(
        finish_kernel,
        in_specs=[HBM_SPEC, SMEM_SPEC] + [VMEM_SPEC] * 6,
        out_specs=HBM_SPEC,
        out_shape=jax.ShapeDtypeStruct(terms.shape, jnp.bfloat16),
        scratch_shapes=[
            pltpu.SMEM(slots.shape, slots.dtype),
            pltpu.SemaphoreType.DMA,
            pltpu.VMEM((gram_side, gram_side), jnp.bfloat16),
            pltpu.VMEM(terms.shape, jnp.bfloat16),
            pltpu.SemaphoreType.DMA((pairs,)),
        ],
        compiler_params=pltpu.CompilerParams(vmem_limit_bytes=LAST_VMEM),
        cost_estimate=pl.CostEstimate(
            flops=2 * pairs * rows * cols * gram_side,
            bytes_accessed=10 * pairs * rows * cols,
            transcendentals=0,
        ),
    )(slots, core, *mine, *other, choose, terms)


def swap(value, axis, bit):
    size = lax.axis_size(axis)
    return lax.ppermute(value, axis, [(i, i ^ bit) for i in range(size)])


def add(*values):
    return sum(value.astype(jnp.float32) for value in values)


def to_owner(keep, came_near, came_even, came_odd):
    half = keep.shape[0] // 2
    keep = keep.reshape(2, half, *keep.shape[1:])
    top, rest = slice(0, FIRST), slice(FIRST, None)
    top_near = swap(add(keep[1, :, top], came_near).astype(jnp.bfloat16), "pairs", 1)

    def rest_sum(j):
        even = add(keep[0, j, rest], came_even[j, rest])
        return jnp.stack([even, add(keep[1, j, rest], came_odd[j])])

    far_first = range(half - 1, 0, -1)
    rest_far = [swap(rest_sum(j).astype(jnp.bfloat16), "pairs", 2 * j) for j in far_first]
    top_sums = [
        add(keep[0, j, top], came_even[j, top], top_near[j]).astype(jnp.bfloat16)
        for j in range(half)
    ]
    top_far = [swap(top_sums[j], "pairs", 2 * j) for j in far_first]
    rest_sums = [
        add(rest_sum(0)[b], *(v[b] for v in rest_far)).astype(jnp.bfloat16)
        for b in range(2)
    ]
    rest_near = swap(rest_sums[1], "pairs", 1)
    top_total = add(top_sums[0], *top_far).astype(jnp.bfloat16)
    rest_total = add(rest_sums[0], rest_near).astype(jnp.bfloat16)
    return top_total, rest_total


def exchange_orders(holders):
    light, heavy = [*range(1, holders // 2)], [*range(holders // 2, holders)]
    first = heavy[:1]
    for pair in zip(heavy[1:], light):
        first += pair
    second = [k for pair in zip(light, heavy) for k in pair] + heavy[-1:]
    return [first, second]


def split_by_columns(blocks, wanted, pair_slots, fock, correlation, amplitudes):
    holders = lax.axis_size("pairs")
    core = lax.axis_index("aux")
    owned, width, depth = blocks.shape
    stacked = blocks.reshape(owned * width, depth)
    place = lax.axis_index("pairs").reshape(1).astype(jnp.int32)
    core_id = core.reshape(1).astype(jnp.int32)
    orders = exchange_orders(holders)
    slot_tables = [[0] * holders for _ in orders]
    for table, ks in zip(slot_tables, orders):
        for n, k in enumerate(ks, 1):
            table[k] = n
    slot = jnp.asarray(slot_tables, jnp.int32)[core % 2]
    chunks = depth // holders // TILE
    cores = lax.axis_size("aux")

    def exchange(parts, orders):
        arrived = []
        for n, part in enumerate(parts):
            moves = [
                (p * cores + c, (p ^ orders[c % 2][n]) * cores + c)
                for p in range(holders)
                for c in range(cores)
            ]
            arrived.append(lax.ppermute(part, ("pairs", "aux"), moves))
        return arrived

    cut = max(1, chunks - LATE)
    first, second = (0, cut), (cut, chunks)
    early = exchange(column_parts(orders, first, False, wanted, place, core_id, stacked), orders)
    tied = max(0, len(early) - 2)
    early[tied], later = lax.optimization_barrier((early[tied], stacked))
    late_orders = orders[::-1]
    late_slots = [[0] + [t[k] for k in ks] for t, ks in zip(slot_tables, late_orders)]
    *late, own_early, own_late = column_parts(late_orders, second, True, wanted, place, core_id, later)
    late = exchange(late, late_orders)
    pairs_here = fock.shape[0]
    slots = lax.dynamic_slice_in_dim(pair_slots, core * pairs_here, pairs_here, axis=0)
    offsets = jnp.arange(width, dtype=jnp.int32)
    right_rows = (slots[:, DOM:, None] * width + offsets).reshape(pairs_here, 1, DOM * width)
    terms, choose = pair_terms(right_rows, fock, correlation, amplitudes)
    early, terms, choose, slots = lax.optimization_barrier((early, terms, choose, slots))
    order = (*range(0, holders, 2), *range(1, holders, 2))
    acc, spots = early_grams(order, owned, width, wanted, place, slot, [own_early, *early])
    keep, *sent = late_grams(late_slots, owned, width, spots, core_id, acc, [own_late, *late])
    mine = to_owner(keep, *(swap(value, "aux", 1) for value in sent))
    other = [swap(value, "aux", 1) for value in mine]
    return finish(slots, core_id, mine, other, choose, terms)


def pick_tiles(gram, left_ids, right_ids):
    count = left_ids.shape[0]
    sides = left_ids.shape[1]
    width = gram.shape[2]
    tiles = gram[left_ids[:, :, None], right_ids[:, None, :]]
    return tiles.transpose(0, 1, 3, 2, 4).reshape(count, sides * width, sides * width)


def pair_integrals(held, left_ids, right_ids):
    units, width, depth = held.shape
    stacked = held.reshape(units * width, depth)
    gram = lax.dot_general(
        stacked, stacked, (((1,), (1,)), ((), ())), preferred_element_type=jnp.float32
    )
    gram = gram.reshape(units, width, units, width).transpose(0, 2, 1, 3)
    return pick_tiles(gram, left_ids, right_ids)


def by_request(blocks, wanted, pair_slots, fock, correlation, amplitudes):
    holders = lax.axis_size("pairs")
    owned, width, depth = blocks.shape
    capacity = max(2, (2 * UNIQ + holders - 1) // holders)
    holder = wanted // owned
    local_ids = wanted - holder * owned
    order_ids = jnp.arange(wanted.shape[0])
    earlier = (holder[None, :] == holder[:, None]) & (order_ids[None, :] < order_ids[:, None])
    rank = jnp.sum(earlier.astype(jnp.int32), axis=1)
    slot = holder * capacity + rank
    places = jnp.arange(holders * capacity)
    table = jnp.sum(jnp.where(places[:, None] == slot[None, :], local_ids[None, :], 0), axis=1)
    table = table.reshape(holders, capacity)
    asked = lax.all_to_all(table, "pairs", split_axis=0, concat_axis=0, tiled=True)
    outgoing = jnp.take(blocks, asked.reshape(-1), axis=0).reshape(holders, capacity, width, depth)
    arrived = lax.all_to_all(outgoing, "pairs", split_axis=0, concat_axis=0, tiled=True)
    held = jnp.take(arrived.reshape(holders * capacity, width, depth), slot, axis=0)
    partial_value = pair_integrals(held, pair_slots[:, :DOM], pair_slots[:, DOM:])
    integrals = lax.psum_scatter(
        partial_value.astype(jnp.bfloat16), "aux", scatter_dimension=0, tiled=True
    ).astype(jnp.float32)
    products = functools.partial(
        jnp.einsum, "pab,pbc->pac", preferred_element_type=jnp.float32
    )
    fock_amp = products(fock, amplitudes).astype(jnp.bfloat16)
    over_amp = products(correlation, amplitudes).astype(jnp.bfloat16)
    terms = products(fock_amp, correlation) + products(over_amp, fock)
    return (integrals + terms).astype(jnp.bfloat16)


def on_device(blocks, *others):
    holders = lax.axis_size("pairs")
    owned, width, depth = blocks.shape
    fits = holders > 1 and holders & (holders - 1) == 0 and width & (width - 1) == 0
    fits = fits and depth % (TILE * holders) == 0 and depth // holders >= 2 * TILE
    fits = fits and holders * owned <= 256 and UNIQ * width == SIDE * TILE
    return (split_by_columns if fits else by_request)(blocks, *others)


def solution(mesh):
    return jax.shard_map(
        on_device,
        mesh=mesh,
        in_specs=(
            P(("groups", "pairs"), None, "aux"),
            P(("groups", "pairs")),
            P(("groups", "pairs"), None),
            P(("groups", "pairs", "aux"), None, None),
            P(("groups", "pairs", "aux"), None, None),
            P(("groups", "pairs", "aux"), None, None),
        ),
        out_specs=P(("groups", "pairs", "aux"), None, None),
        check_vma=False,
    )
```

```python
import functools

import jax
import jax.numpy as jnp
from jax import lax
from jax.experimental import pallas as pl
from jax.experimental.pallas import tpu as pltpu
from jax.sharding import PartitionSpec as P

DOM = 8
UNIQ = 16
TILE = 128
SIDE = 4
LATE = 2

STRIP = 256
LIST_ROWS = 16
VMEM_BYTES = 60 * 1024 * 1024
LAST_VMEM = 24 * 1024 * 1024
FIRST = 416
SMEM_SPEC = pl.BlockSpec(memory_space=pltpu.SMEM)
VMEM_SPEC = pl.BlockSpec(memory_space=pltpu.VMEM)
HBM_SPEC = pl.BlockSpec(memory_space=pltpu.HBM)


def terms_kernel(right_ref, fock_ref, corr_ref, amp_ref, out_ref, choose_ref):
    fock, corr, amp = fock_ref[0], corr_ref[0], amp_ref[0]
    fock_amp = jnp.dot(fock, amp, preferred_element_type=jnp.float32).astype(jnp.bfloat16)
    over_amp = jnp.dot(corr, amp, preferred_element_type=jnp.float32).astype(jnp.bfloat16)
    first = jnp.dot(fock_amp, corr, preferred_element_type=jnp.float32)
    out_ref[0] = first + jnp.dot(over_amp, fock, preferred_element_type=jnp.float32)
    rows = lax.broadcasted_iota(jnp.int32, choose_ref.shape[1:], 0)
    choose_ref[0] = (rows == right_ref[0]).astype(jnp.float32).astype(jnp.bfloat16)


def pair_terms(right_rows, fock, correlation, amplitudes):
    pairs, rows, cols = fock.shape
    spec = pl.BlockSpec((1, rows, cols), lambda p: (p, 0, 0))
    side = UNIQ * rows // DOM
    return pl.pallas_call(
        terms_kernel,
        grid=(pairs,),
        in_specs=[pl.BlockSpec((1, 1, cols), lambda p: (p, 0, 0))] + [spec] * 3,
        out_specs=[spec, pl.BlockSpec((1, side, cols), lambda p: (p, 0, 0))],
        out_shape=[
            jax.ShapeDtypeStruct(fock.shape, jnp.float32),
            jax.ShapeDtypeStruct((pairs, side, cols), jnp.bfloat16),
        ],
        compiler_params=pltpu.CompilerParams(vmem_limit_bytes=VMEM_BYTES),
        cost_estimate=pl.CostEstimate(
            flops=8 * pairs * rows * rows * cols,
            bytes_accessed=14 * pairs * rows * cols,
            transcendentals=0,
        ),
    )(right_rows, fock, correlation, amplitudes)


def split_kernel(orders, span, own, wanted_ref, place_ref, core_ref, blocks_ref, *rest):
    outs, (bufs, own_buf, tail, ids_smem, in_sems, out_sems) = rest[:-6], rest[-6:]
    rows, depth = blocks_ref.shape
    columns = own_buf.shape[1]
    chunks = span[1] - span[0]
    count = len(orders[0])
    fetches, stores = [], []

    def fetch(n, offset, first, buf):
        start = pl.multiple_of((place_ref[0] ^ offset) * columns + first * TILE, TILE)
        source = blocks_ref.at[:, pl.ds(start, buf.shape[1])]
        fetches.append(pltpu.make_async_copy(source, buf, in_sems.at[n]))
        fetches[-1].start()

    def store(n, c, source, out, row):
        target = out.at[pl.ds(row, source.shape[0])]
        stores.append(pltpu.make_async_copy(source, target, out_sems.at[n, c]))
        stores[-1].start()

    lists = pltpu.make_async_copy(wanted_ref, ids_smem, in_sems.at[count])
    if not own:
        lists.start()
    for n, ks in enumerate(zip(*orders)):
        offset = jnp.where(core_ref[0] % 2 == 0, *ks)
        fetch(n, offset, span[0], bufs.at[n])
    if own:
        fetch(count, 0, 0, own_buf)
    else:
        lists.wait()
        lane = lax.broadcasted_iota(jnp.int32, tail.shape, 1)
        ids = jnp.zeros(tail.shape, jnp.int32)
        for m in range(UNIQ):
            ids = jnp.where(lane == m, ids_smem[m], ids)
        tail[...] = ids.astype(jnp.float32).astype(jnp.bfloat16)
        for n in range(count):
            store(n, chunks, tail, outs[n], chunks * rows)
    for n in range(count):
        fetches[n].wait()
        for c in range(chunks):
            store(n, c, bufs.at[n, :, pl.ds(c * TILE, TILE)], outs[n], c * rows)
    if own:
        fetches[count].wait()
        for c in range(columns // TILE):
            early = c < span[0]
            out = outs[count] if early else outs[count + 1]
            row = (c if early else c - span[0]) * rows
            store(count, c, own_buf.at[:, pl.ds(c * TILE, TILE)], out, row)
    for copy in stores:
        copy.wait()


def column_parts(orders, span, own, wanted, place, core, blocks):
    rows, depth = blocks.shape
    count = len(orders[0])
    columns = depth // (count + 1)
    chunks = span[1] - span[0]
    heights = [chunks * rows + LIST_ROWS * (not own)] * count
    if own:
        heights += [span[0] * rows, chunks * rows]
    return pl.pallas_call(
        functools.partial(split_kernel, orders, span, own),
        in_specs=[HBM_SPEC, SMEM_SPEC, SMEM_SPEC, HBM_SPEC],
        out_specs=[HBM_SPEC] * len(heights),
        out_shape=[jax.ShapeDtypeStruct((height, TILE), blocks.dtype) for height in heights],
        scratch_shapes=[
            pltpu.VMEM((count, rows, chunks * TILE), blocks.dtype),
            pltpu.VMEM((rows, columns), blocks.dtype),
            pltpu.VMEM((LIST_ROWS, TILE), blocks.dtype),
            pltpu.SMEM(wanted.shape, wanted.dtype),
            pltpu.SemaphoreType.DMA((count + 1,)),
            pltpu.SemaphoreType.DMA((count + 1, columns // TILE + 1)),
        ],
        compiler_params=pltpu.CompilerParams(vmem_limit_bytes=VMEM_BYTES),
    )(wanted, place, core, blocks)


def block_order(width):
    bits = width.bit_length() - 1
    row = lax.broadcasted_iota(jnp.int32, (TILE, TILE), 0) >> bits
    col = lax.broadcasted_iota(jnp.int32, (TILE, TILE), 1) >> bits
    return row, col


def packed_gram(held, width):
    tile = {}
    for top in range(0, SIDE * TILE, STRIP):
        strip = lax.dot_general(
            held[top : top + STRIP],
            held[top:],
            (((1,), (1,)), ((), ())),
            preferred_element_type=jnp.float32,
        )
        for i in range(top // TILE, (top + STRIP) // TILE):
            for j in range(i, SIDE):
                r, c = i * TILE - top, j * TILE - top
                tile[i, j] = strip[r : r + TILE, c : c + TILE]
    row, col = block_order(width)

    def diagonal(value):
        found = value[:width]
        for r in range(1, TILE // width):
            here = col[:width] == r
            found = jnp.where(here, value[r * width : (r + 1) * width], found)
        return found

    both = [jnp.where(row <= col, tile[i, i], tile[i + 1, i + 1]) for i in (0, 2)]
    first = [diagonal(tile[1, 1]), tile[0, 1], tile[0, 2], tile[0, 3], tile[1, 2]]
    second = [diagonal(tile[3, 3]), tile[1, 3], tile[2, 3], *both]
    return first, second


def gather_rows(pool, places, rows, width, chunks):
    return jnp.concatenate(
        [
            jnp.concatenate(
                [
                    pool[pl.ds(pl.multiple_of(place + c * rows, width), width), :]
                    for place in places
                ],
                axis=0,
            )
            for c in range(chunks)
        ],
        axis=1,
    )


def pool_copies(refs, slots, part, pool, sems):
    return [
        pltpu.make_async_copy(
            ref.at[pl.ds(0, part)],
            pool.at[pl.ds(pl.multiple_of(slot * part, part), part)],
            sems.at[k],
        )
        for k, (ref, slot) in enumerate(zip(refs, slots))
    ]


def early_kernel(ks, owned, width, wanted_ref, place_ref, slot_ref, *rest):
    refs, rest = rest[:-8], rest[-8:]
    acc_ref, spots_ref, pool, lists, ids_vmem, ids, sems, list_sems = rest
    rows = owned * width
    part = refs[0].shape[0]
    chunks = part // rows
    me = place_ref[0]
    tails = [
        pltpu.make_async_copy(ref.at[pl.ds(part, LIST_ROWS)], lists.at[k], list_sems.at[k])
        for k, ref in enumerate(refs[1:], 1)
    ]
    copies = pool_copies(refs, range(len(refs)), part, pool, sems)
    for copy in tails + copies:
        copy.start()
    for copy in tails:
        copy.wait()
    ids_vmem[...] = jnp.zeros_like(ids_vmem)
    for n, k in enumerate(ks):
        if k > 0:
            ids_vmem[n, :] = lists[slot_ref[k]].astype(jnp.float32).astype(jnp.int32)[0]
    to_scalars = pltpu.make_async_copy(ids_vmem, ids, list_sems.at[0])
    to_scalars.start()
    to_scalars.wait()
    for n, k in enumerate(ks):
        for m in range(UNIQ):
            entry = wanted_ref[m] if k == 0 else ids[n, m]
            holder = lax.div(entry, owned)
            spots_ref[n, m] = slot_ref[holder ^ me] * owned + (entry - holder * owned)
    for copy in copies:
        copy.wait()

    @pl.loop(0, len(ks))
    def _(n):
        places = []
        for m in range(UNIQ):
            where = lax.div(spots_ref[n, m], owned)
            places.append(where * part + (spots_ref[n, m] - where * owned) * width)
        held = gather_rows(pool, places, rows, width, chunks)
        at = 0
        for value in sum(packed_gram(held, width), []):
            acc_ref[n, at : at + value.shape[0], :] = value
            at += value.shape[0]


def late_kernel(slots, owned, width, spots_hbm, core_ref, acc_ref, *rest):
    refs, rest = rest[:-8], rest[-8:]
    keep_ref, near_ref, even_ref, odd_ref, pool, spots_ref, spots_sem, sems = rest
    rows = owned * width
    part = refs[0].shape[0]
    chunks = part // rows
    owners = acc_ref.shape[0]
    half = acc_ref.shape[1] // 2
    core = core_ref[0]
    targets = [jnp.where(core % 2 == 0, *pair) for pair in zip(*slots)]
    copies = pool_copies(refs, targets, part, pool, sems)
    copies.append(pltpu.make_async_copy(spots_hbm, spots_ref, spots_sem))
    for copy in reversed(copies):
        copy.start()
    for copy in copies:
        copy.wait()
    for n in range(owners):
        places = []
        for m in range(UNIQ):
            where = lax.div(spots_ref[n, m], owned)
            places.append(where * part + (spots_ref[n, m] - where * owned) * width)
        halves = packed_gram(gather_rows(pool, places, rows, width, chunks), width)
        at = 0
        for first, second in zip(*halves):
            height = first.shape[0]
            first += acc_ref[n, at : at + height, :]
            second += acc_ref[n, half + at : half + at + height, :]
            keep = jnp.where(core == 0, first, second)
            send = jnp.where(core == 0, second, first)
            keep_ref[n, at : at + height, :] = keep.astype(jnp.bfloat16)
            if n < owners // 2:
                even_ref[n, at : at + height, :] = send.astype(jnp.bfloat16)
            elif at < FIRST:
                near_ref[n - owners // 2, at : at + height, :] = send.astype(jnp.bfloat16)
            else:
                row = at - FIRST
                odd_ref[n - owners // 2, row : row + height, :] = send.astype(jnp.bfloat16)
            at += height


def half_rows(width):
    return SIDE * TILE + width


def early_grams(ks, owned, width, wanted, place, slot, parts):
    holders = len(parts)
    rows = owned * width
    chunks = parts[0].shape[0] // rows
    return pl.pallas_call(
        functools.partial(early_kernel, ks, owned, width),
        in_specs=[SMEM_SPEC] * 3 + [HBM_SPEC] * holders,
        out_specs=[VMEM_SPEC, SMEM_SPEC],
        out_shape=[
            jax.ShapeDtypeStruct((len(ks), 2 * half_rows(width), TILE), jnp.float32),
            jax.ShapeDtypeStruct((len(ks), UNIQ), jnp.int32),
        ],
        scratch_shapes=[
            pltpu.VMEM((holders * rows * chunks, TILE), jnp.bfloat16),
            pltpu.VMEM((holders, LIST_ROWS, TILE), jnp.bfloat16),
            pltpu.VMEM((len(ks), TILE), jnp.int32),
            pltpu.SMEM((len(ks), TILE), jnp.int32),
            pltpu.SemaphoreType.DMA((holders,)),
            pltpu.SemaphoreType.DMA((holders,)),
        ],
        compiler_params=pltpu.CompilerParams(vmem_limit_bytes=24 * 1024 * 1024),
        cost_estimate=pl.CostEstimate(
            flops=2 * len(ks) * (SIDE * TILE) ** 2 * chunks * TILE,
            bytes_accessed=2 * holders * rows * chunks * TILE,
            transcendentals=0,
        ),
    )(wanted, place, slot, *parts)


def late_grams(slots, owned, width, spots, core, acc, parts):
    holders = len(parts)
    rows = owned * width
    chunks = parts[0].shape[0] // rows
    half = half_rows(width)
    owners = acc.shape[0]
    return pl.pallas_call(
        functools.partial(late_kernel, slots, owned, width),
        in_specs=[HBM_SPEC, SMEM_SPEC, VMEM_SPEC] + [HBM_SPEC] * holders,
        out_specs=[VMEM_SPEC] * 4,
        out_shape=[
            jax.ShapeDtypeStruct((count, height, TILE), jnp.bfloat16)
            for count, height in (
                (owners, half),
                (owners // 2, FIRST),
                (owners // 2, half),
                (owners // 2, half - FIRST),
            )
        ],
        scratch_shapes=[
            pltpu.VMEM((holders * rows * chunks, TILE), jnp.bfloat16),
            pltpu.SMEM(spots.shape, spots.dtype),
            pltpu.SemaphoreType.DMA,
            pltpu.SemaphoreType.DMA((holders,)),
        ],
        compiler_params=pltpu.CompilerParams(vmem_limit_bytes=16 * 1024 * 1024),
        cost_estimate=pl.CostEstimate(
            flops=2 * owners * (SIDE * TILE) ** 2 * chunks * TILE,
            bytes_accessed=2 * holders * rows * chunks * TILE,
            transcendentals=0,
        ),
    )(spots, core, acc, *parts)


def finish_kernel(slots_hbm, core_ref, mine_top, mine_rest, other_top, other_rest, choose_ref, terms_ref, out_ref, *rest):
    slots_ref, slots_sem, gram, stage, sems = rest
    fetch = pltpu.make_async_copy(slots_hbm, slots_ref, slots_sem)
    fetch.start()
    core = core_ref[0]
    width = gram.shape[0] // UNIQ
    pairs = out_ref.shape[0]

    def put(i, j, value):
        gram[i * TILE : (i + 1) * TILE, j * TILE : (j + 1) * TILE] = value.astype(jnp.bfloat16)

    mine = jnp.concatenate([mine_top[...], mine_rest[...]], axis=0)
    other = jnp.concatenate([other_top[...], other_rest[...]], axis=0)
    first = jnp.where(core == 0, mine, other).astype(jnp.float32)
    second = jnp.where(core == 0, other, mine).astype(jnp.float32)
    pieces = [
        v[width + t * TILE : width + (t + 1) * TILE]
        for v in (first, second)
        for t in range(SIDE)
    ]
    places = [(0, 1), (0, 2), (0, 3), (1, 2), (1, 3), (2, 3)]
    for (i, j), value in zip(places, pieces):
        put(i, j, value)
        put(j, i, value.T)
    row, col = block_order(width)
    for i, value, diagonal in zip((0, 2), pieces[6:], (first, second)):
        flipped = value.T
        squares = jnp.concatenate([diagonal[:width]] * (TILE // width), axis=0)
        put(i, i, jnp.where(row <= col, value, flipped))
        lower = jnp.where(row > col, value, flipped)
        put(i + 1, i + 1, jnp.where(row == col, squares, lower))

    fetch.wait()

    def result(pair):
        return pltpu.make_async_copy(stage.at[pair], out_ref.at[pair], sems.at[pair])

    for pair in range(pairs):
        left = jnp.concatenate(
            [gram[pl.ds(slots_ref[pair, m] * width, width), :] for m in range(DOM)], axis=0
        )
        integrals = jnp.dot(left, choose_ref[pair], preferred_element_type=jnp.float32)
        stage[pair] = (integrals + terms_ref[pair]).astype(jnp.bfloat16)
        result(pair).start()
    for pair in range(pairs):
        result(pair).wait()


def finish(slots, core, mine, other, choose, terms):
    pairs, rows, cols = terms.shape
    gram_side = UNIQ * rows // DOM
    return pl.pallas_call(
        finish_kernel,
        in_specs=[HBM_SPEC, SMEM_SPEC] + [VMEM_SPEC] * 6,
        out_specs=HBM_SPEC,
        out_shape=jax.ShapeDtypeStruct(terms.shape, jnp.bfloat16),
        scratch_shapes=[
            pltpu.SMEM(slots.shape, slots.dtype),
            pltpu.SemaphoreType.DMA,
            pltpu.VMEM((gram_side, gram_side), jnp.bfloat16),
            pltpu.VMEM(terms.shape, jnp.bfloat16),
            pltpu.SemaphoreType.DMA((pairs,)),
        ],
        compiler_params=pltpu.CompilerParams(vmem_limit_bytes=LAST_VMEM),
        cost_estimate=pl.CostEstimate(
            flops=2 * pairs * rows * cols * gram_side,
            bytes_accessed=10 * pairs * rows * cols,
            transcendentals=0,
        ),
    )(slots, core, *mine, *other, choose, terms)


def swap(value, axis, bit):
    size = lax.axis_size(axis)
    return lax.ppermute(value, axis, [(i, i ^ bit) for i in range(size)])


def add(*values):
    return sum(value.astype(jnp.float32) for value in values)


def to_owner(keep, came_near, came_even, came_odd):
    half = keep.shape[0] // 2
    keep = keep.reshape(2, half, *keep.shape[1:])
    top, rest = slice(0, FIRST), slice(FIRST, None)
    top_near = swap(add(keep[1, :, top], came_near).astype(jnp.bfloat16), "pairs", 1)

    def rest_sum(j):
        even = add(keep[0, j, rest], came_even[j, rest])
        return jnp.stack([even, add(keep[1, j, rest], came_odd[j])])

    far_first = range(half - 1, 0, -1)
    rest_far = [swap(rest_sum(j).astype(jnp.bfloat16), "pairs", 2 * j) for j in far_first]
    top_sums = [
        add(keep[0, j, top], came_even[j, top], top_near[j]).astype(jnp.bfloat16)
        for j in range(half)
    ]
    top_far = [swap(top_sums[j], "pairs", 2 * j) for j in far_first]
    rest_sums = [
        add(rest_sum(0)[b], *(v[b] for v in rest_far)).astype(jnp.bfloat16)
        for b in range(2)
    ]
    rest_near = swap(rest_sums[1], "pairs", 1)
    top_total = add(top_sums[0], *top_far).astype(jnp.bfloat16)
    rest_total = add(rest_sums[0], rest_near).astype(jnp.bfloat16)
    return top_total, rest_total


def exchange_orders(holders):
    light, heavy = [*range(1, holders // 2)], [*range(holders // 2, holders)]
    first = []
    for pair in zip(heavy, light):
        first += pair
    first += heavy[-1:]
    second = [k for pair in zip(light, heavy) for k in pair] + heavy[-1:]
    return [first, second]


def split_by_columns(blocks, wanted, pair_slots, fock, correlation, amplitudes):
    holders = lax.axis_size("pairs")
    core = lax.axis_index("aux")
    owned, width, depth = blocks.shape
    stacked = blocks.reshape(owned * width, depth)
    place = lax.axis_index("pairs").reshape(1).astype(jnp.int32)
    core_id = core.reshape(1).astype(jnp.int32)
    orders = exchange_orders(holders)
    slot_tables = [[0] * holders for _ in orders]
    for table, ks in zip(slot_tables, orders):
        for n, k in enumerate(ks, 1):
            table[k] = n
    slot = jnp.asarray(slot_tables, jnp.int32)[core % 2]
    chunks = depth // holders // TILE
    cores = lax.axis_size("aux")

    def exchange(parts, orders):
        arrived = []
        for n, part in enumerate(parts):
            moves = [
                (p * cores + c, (p ^ orders[c % 2][n]) * cores + c)
                for p in range(holders)
                for c in range(cores)
            ]
            arrived.append(lax.ppermute(part, ("pairs", "aux"), moves))
        return arrived

    cut = max(1, chunks - LATE)
    first, second = (0, cut), (cut, chunks)
    early = exchange(column_parts(orders, first, False, wanted, place, core_id, stacked), orders)
    tied = max(0, len(early) - 2)
    early[tied], later = lax.optimization_barrier((early[tied], stacked))
    late_orders = orders[::-1]
    late_slots = [[0] + [t[k] for k in ks] for t, ks in zip(slot_tables, late_orders)]
    *late, own_early, own_late = column_parts(late_orders, second, True, wanted, place, core_id, later)
    late = exchange(late, late_orders)
    pairs_here = fock.shape[0]
    slots = lax.dynamic_slice_in_dim(pair_slots, core * pairs_here, pairs_here, axis=0)
    offsets = jnp.arange(width, dtype=jnp.int32)
    right_rows = (slots[:, DOM:, None] * width + offsets).reshape(pairs_here, 1, DOM * width)
    terms, choose = pair_terms(right_rows, fock, correlation, amplitudes)
    early, terms, choose, slots = lax.optimization_barrier((early, terms, choose, slots))
    order = (*range(0, holders, 2), *range(1, holders, 2))
    acc, spots = early_grams(order, owned, width, wanted, place, slot, [own_early, *early])
    keep, *sent = late_grams(late_slots, owned, width, spots, core_id, acc, [own_late, *late])
    mine = to_owner(keep, *(swap(value, "aux", 1) for value in sent))
    other = [swap(value, "aux", 1) for value in mine]
    return finish(slots, core_id, mine, other, choose, terms)


def pick_tiles(gram, left_ids, right_ids):
    count = left_ids.shape[0]
    sides = left_ids.shape[1]
    width = gram.shape[2]
    tiles = gram[left_ids[:, :, None], right_ids[:, None, :]]
    return tiles.transpose(0, 1, 3, 2, 4).reshape(count, sides * width, sides * width)


def pair_integrals(held, left_ids, right_ids):
    units, width, depth = held.shape
    stacked = held.reshape(units * width, depth)
    gram = lax.dot_general(
        stacked, stacked, (((1,), (1,)), ((), ())), preferred_element_type=jnp.float32
    )
    gram = gram.reshape(units, width, units, width).transpose(0, 2, 1, 3)
    return pick_tiles(gram, left_ids, right_ids)


def by_request(blocks, wanted, pair_slots, fock, correlation, amplitudes):
    holders = lax.axis_size("pairs")
    owned, width, depth = blocks.shape
    capacity = max(2, (2 * UNIQ + holders - 1) // holders)
    holder = wanted // owned
    local_ids = wanted - holder * owned
    order_ids = jnp.arange(wanted.shape[0])
    earlier = (holder[None, :] == holder[:, None]) & (order_ids[None, :] < order_ids[:, None])
    rank = jnp.sum(earlier.astype(jnp.int32), axis=1)
    slot = holder * capacity + rank
    places = jnp.arange(holders * capacity)
    table = jnp.sum(jnp.where(places[:, None] == slot[None, :], local_ids[None, :], 0), axis=1)
    table = table.reshape(holders, capacity)
    asked = lax.all_to_all(table, "pairs", split_axis=0, concat_axis=0, tiled=True)
    outgoing = jnp.take(blocks, asked.reshape(-1), axis=0).reshape(holders, capacity, width, depth)
    arrived = lax.all_to_all(outgoing, "pairs", split_axis=0, concat_axis=0, tiled=True)
    held = jnp.take(arrived.reshape(holders * capacity, width, depth), slot, axis=0)
    partial_value = pair_integrals(held, pair_slots[:, :DOM], pair_slots[:, DOM:])
    integrals = lax.psum_scatter(
        partial_value.astype(jnp.bfloat16), "aux", scatter_dimension=0, tiled=True
    ).astype(jnp.float32)
    products = functools.partial(
        jnp.einsum, "pab,pbc->pac", preferred_element_type=jnp.float32
    )
    fock_amp = products(fock, amplitudes).astype(jnp.bfloat16)
    over_amp = products(correlation, amplitudes).astype(jnp.bfloat16)
    terms = products(fock_amp, correlation) + products(over_amp, fock)
    return (integrals + terms).astype(jnp.bfloat16)


def on_device(blocks, *others):
    holders = lax.axis_size("pairs")
    owned, width, depth = blocks.shape
    fits = holders > 1 and holders & (holders - 1) == 0 and width & (width - 1) == 0
    fits = fits and depth % (TILE * holders) == 0 and depth // holders >= 2 * TILE
    fits = fits and holders * owned <= 256 and UNIQ * width == SIDE * TILE
    return (split_by_columns if fits else by_request)(blocks, *others)


def solution(mesh):
    return jax.shard_map(
        on_device,
        mesh=mesh,
        in_specs=(
            P(("groups", "pairs"), None, "aux"),
            P(("groups", "pairs")),
            P(("groups", "pairs"), None),
            P(("groups", "pairs", "aux"), None, None),
            P(("groups", "pairs", "aux"), None, None),
            P(("groups", "pairs", "aux"), None, None),
        ),
        out_specs=P(("groups", "pairs", "aux"), None, None),
        check_vma=False,
    )
```
